32 devices in a mesh: dp: 8 (over y, x, core), ctx: 4 (over z).
Axes of the slice: x: 2, y: 2, z: 4, core: 2. Of those that a mesh axis runs over, the one named last changes fastest.
Arguments:
- tokens: bfloat16 [8, 1024, 1536], P('dp', 'ctx'), may hold values from -6 to 6
- cotangent: bfloat16 [8, 1024, 1536], P('dp', 'ctx'), may hold values from -6 to 6
- gain_attn: bfloat16 [1536], P(('dp', 'ctx')), may hold values from 0.5 to 1.5
- w_query: bfloat16 [1536, 1536], P(('dp', 'ctx')), may hold values from -0.21875 to 0.21875
- w_key: bfloat16 [1536, 768], P(('dp', 'ctx')), may hold values from -0.21875 to 0.21875
- w_value: bfloat16 [1536, 768], P(('dp', 'ctx')), may hold values from -0.15625 to 0.15625
- w_out: bfloat16 [1536, 1536], P(('dp', 'ctx')), may hold values from -0.625 to 0.625
- gain_ffn: bfloat16 [1536], P(('dp', 'ctx')), may hold values from 0.5 to 1.5
- w_gate: bfloat16 [1536, 4096], P(('dp', 'ctx')), may hold values from -0.15625 to 0.15625
- w_up: bfloat16 [1536, 4096], P(('dp', 'ctx')), may hold values from -0.15625 to 0.15625
- w_down: bfloat16 [4096, 1536], P(('dp', 'ctx')), may hold values from -0.09375 to 0.09375
- order: int32 [8], replicated, may hold values from 0 to 7, each once
Outputs:
- mixed: bfloat16 [8, 1024, 1536], P('dp', 'ctx')
- token_input_gradient: float32 [8, 1024, 1536], P('dp', 'ctx')
- attention_gain_gradient: float32 [1536], P(('dp', 'ctx'))
- grad_query: float32 [1536, 1536], P(('dp', 'ctx'))
- grad_key: float32 [1536, 768], P(('dp', 'ctx'))
- grad_value: float32 [1536, 768], P(('dp', 'ctx'))
- grad_out: float32 [1536, 1536], P(('dp', 'ctx'))
- feedforward_gain_gradient: float32 [1536], P(('dp', 'ctx'))
- grad_gate: float32 [1536, 4096], P(('dp', 'ctx'))
- grad_up: float32 [1536, 4096], P(('dp', 'ctx'))
- grad_down: float32 [4096, 1536], P(('dp', 'ctx'))
The draws below stay inside these ranges and needn't reach their ends.
Inputs may be any that keep to these rules, and one draw needn't show every extreme that they name: Device c of ctx holds in its rows the half-blocks order[2 c] and order[2 c + 1] of every sequence, each of 128 positions.
All inputs are finite; a program needn't handle non-finite values.
Results may differ from the reference program's by a relative error of at most 0.024.
Values may be sent and summed in bfloat16 or wider, within the bound.
No kernel may reach another device: no remote copies, remote signals or barrier semaphores. Data moves between devices by JAX's collectives and lax.ppermute only.
A program may use at most 320 MiB of HBM per device.

```python
import math
import jax
import jax.numpy as jnp
from jax import lax

D = 1536
HEADS = 16
KV_HEADS = 8
HEAD_DIM = 96
FF = 4096
LEN = 1024
SEQS = 8
N_CTX = 4


def shard_levels(stream_key, dims, split, low, largest):
    gain = 1.0
    for dim, shards_of in split:
        steps = jax.random.uniform(jax.random.fold_in(jax.random.fold_in(stream_key, 6), dim), (shards_of,), jnp.float32, low / len(split), largest / len(split))
        gain = gain * jnp.repeat(jnp.exp(steps), dims[dim] // shards_of).reshape((-1,) + (1,) * (len(dims) - 1 - dim))
    return gain


def centred(key, extent, scale, bound, shards=(), kind=jnp.bfloat16):
    drawn = jax.random.normal(key, extent, jnp.float32) * scale
    if len(shards) > 0:
        drawn = shard_levels(key, extent, shards, -0.22, 0.18) * drawn
    return jnp.clip(drawn, min=-bound, max=bound).astype(kind)


def setup_inputs(seed: int = 0) -> dict:
    seeds = jax.random.split(jax.random.key(seed), 13)
    tokens = centred(seeds[0], (SEQS, LEN, D), 1.0, 6.0, ((0, 8), (1, 4)))
    cotangent = centred(seeds[1], (SEQS, LEN, D), 1.0, 6.0, ((0, 8), (1, 4)))
    gain_attn = jnp.clip(1.0 + 0.1 * jax.random.normal(seeds[2], (D,), jnp.float32), 0.5, 1.5).astype(jnp.bfloat16)
    w_query = centred(seeds[3], (D, HEADS * HEAD_DIM), (D // 2) ** -0.5, 0.21875, ((0, 32),))
    w_key = centred(seeds[4], (D, KV_HEADS * HEAD_DIM), (D // 2) ** -0.5, 0.21875, ((0, 32),))
    w_value = centred(seeds[5], (D, KV_HEADS * HEAD_DIM), D ** -0.5, 0.15625, ((0, 32),))
    w_out = centred(seeds[6], (HEADS * HEAD_DIM, D), (HEADS * HEAD_DIM // 16) ** -0.5, 0.625, ((0, 32),))
    gain_ffn = jnp.clip(1.0 + 0.1 * jax.random.normal(seeds[7], (D,), jnp.float32), 0.5, 1.5).astype(jnp.bfloat16)
    w_gate = centred(seeds[8], (D, FF), D ** -0.5, 0.15625, ((0, 32),))
    w_up = centred(seeds[9], (D, FF), D ** -0.5, 0.15625, ((0, 32),))
    w_down = centred(seeds[10], (FF, D), FF ** -0.5, 0.09375, ((0, 32),))
    order = jax.random.permutation(seeds[11], 2 * N_CTX).astype(jnp.int32)
    return {"tokens": tokens, "cotangent": cotangent, "gain_attn": gain_attn, "w_query": w_query, "w_key": w_key, "w_value": w_value, "w_out": w_out, "gain_ffn": gain_ffn, "w_gate": w_gate, "w_up": w_up, "w_down": w_down, "order": order}


PRECISION_TOP = lax.Precision.HIGHEST
eps = 1e-05
theta = 100000.0

@jax.custom_vjp
def low(v):
    return lax.optimization_barrier(v.astype(jnp.bfloat16)).astype(jnp.float32)

@jax.custom_vjp
def low_back(v):
    return v

def low_keep(v):
    return (low(v), None)

def low_pass(kept, grad):
    return (grad,)

def back_keep(v):
    return (v, None)

def back_low(kept, grad):
    return (low(grad),)
low.defvjp(low_keep, low_pass)
low_back.defvjp(back_keep, back_low)

def positions(order):
    half_rows = LEN // (2 * N_CTX)
    seq_rows = jnp.arange(LEN, dtype=jnp.int32)
    return order[seq_rows // half_rows] * half_rows + seq_rows % half_rows

def angle_tables(places):
    freqs = theta ** (-(jnp.arange(HEAD_DIM // 2).astype(jnp.float32) * 2.0 / HEAD_DIM))
    angles = places.astype(jnp.float32)[:, None] * freqs[None, :]
    return (jnp.cos(angles), jnp.sin(angles))

def rotate(values, cosine, sine):
    half_dim = values.shape[-1] // 2
    first = values[..., :half_dim]
    second = values[..., half_dim:]
    cos_b = cosine[:, None, :]
    sin_b = sine[:, None, :]
    return jnp.concatenate([first * cos_b - second * sin_b, second * cos_b + first * sin_b], axis=-1)

def rms_norm(values, norm_gain):
    return values * lax.rsqrt(lax.optimization_barrier(jnp.mean(values * values, axis=-1, keepdims=True)) + eps) * norm_gain

def project(left_operand, right_operand):
    return jnp.einsum('auo,or->aur', left_operand, right_operand, precision=PRECISION_TOP)

def attend(queries, keys, values, allowed):
    groups = HEADS // KV_HEADS
    grouped = queries.reshape(LEN, KV_HEADS, groups, HEAD_DIM)
    scores = jnp.einsum('qkgd,tkd->kgqt', grouped, keys, precision=PRECISION_TOP) * HEAD_DIM ** (-0.5)
    scores = jnp.where(allowed, low_back(scores), -1e+30)
    probs = jax.nn.softmax(scores, axis=-1)
    result = jnp.einsum('kgqt,tkd->qkgd', low(probs), values, precision=PRECISION_TOP)
    return result.reshape(LEN, HEADS * HEAD_DIM)

def block_forward(layer_inputs, gain_attn, w_query, w_key, w_value, w_out, gain_ffn, w_gate, w_up, w_down, cosine, sine, allowed):
    group_count = layer_inputs.shape[0]
    normalized_rows = low(rms_norm(layer_inputs, gain_attn))
    queries = low_back(project(normalized_rows, w_query)).reshape(group_count, LEN, HEADS, HEAD_DIM)
    queries = low(rotate(queries, cosine, sine))
    keys = low_back(project(normalized_rows, w_key)).reshape(group_count, LEN, KV_HEADS, HEAD_DIM)
    keys = low(rotate(keys, cosine, sine))
    values = low_back(low(project(normalized_rows, w_value))).reshape(group_count, LEN, KV_HEADS, HEAD_DIM)
    attend_one = jax.checkpoint(lambda items: attend(items[0], items[1], items[2], allowed))
    heads_out = lax.map(attend_one, (queries, keys, values))
    heads_out = low_back(low(heads_out))
    middle_activation = layer_inputs + low_back(project(heads_out, w_out))
    gated_input = low(rms_norm(middle_activation, gain_ffn))
    gate = low_back(project(gated_input, w_gate))
    upper = low_back(project(gated_input, w_up))
    hidden = low(jax.nn.silu(gate) * upper)
    return middle_activation + project(hidden, w_down)

def reference(tokens, cotangent, gain_attn, w_query, w_key, w_value, w_out, gain_ffn, w_gate, w_up, w_down, order):
    weights = tuple((item.astype(jnp.float32) for item in (gain_attn, w_query, w_key, w_value, w_out, gain_ffn, w_gate, w_up, w_down)))
    places = positions(order)
    cosine, sine = angle_tables(places)
    allowed = places[None, :] <= places[:, None]
    group = math.gcd(SEQS, max(1, 4096 // LEN))
    layer_inputs = tokens.astype(jnp.float32).reshape(SEQS // group, group, LEN, D)
    cotan = cotangent.astype(jnp.float32).reshape(SEQS // group, group, LEN, D)

    def step(totals, item):
        block_in, block_cot = item
        outputs, pull = jax.vjp(lambda xin, *wts: block_forward(xin, *wts, cosine, sine, allowed), block_in, *weights)
        grads = pull(block_cot)
        new_totals = tuple((total + extra for total, extra in zip(totals, grads[1:])))
        return (new_totals, (outputs.astype(jnp.bfloat16), grads[0]))
    zeros = tuple((jnp.zeros_like(item) for item in weights))
    totals, (results, in_grads) = lax.scan(step, zeros, (layer_inputs, cotan))
    return (results.reshape(SEQS, LEN, D), in_grads.reshape(SEQS, LEN, D), totals[0], totals[1], totals[2], totals[3], totals[4], totals[5], totals[6], totals[7], totals[8])
```

```python
import jax
import jax.numpy as jnp
from jax import lax
from jax.sharding import PartitionSpec as P

HEADS = 16
KV_HEADS = 8
HEAD_DIM = 96
GROUPS = HEADS // KV_HEADS
HALF = HEAD_DIM // 2
QW = GROUPS * HEAD_DIM
QKV = QW + 2 * HEAD_DIM

EPS = 1e-05
THETA = 100000.0
F32 = jnp.float32
BF16 = jnp.bfloat16

TEAM = KV_HEADS


def dot(a, b, dims):
    return lax.dot_general(a, b, (dims, ((), ())), preferred_element_type=F32)


def mm(a, b):
    return dot(a, b, ((1,), (0,)))


def mm_nt(a, b):
    return dot(a, b, ((1,), (1,)))


def mm_tn(a, b):
    return dot(a, b, ((0,), (0,)))


def swap(value, bit):
    n = lax.axis_size("dp")
    return lax.ppermute(value, "dp", [(i, i ^ bit) for i in range(n)])


def team_gather(own):
    half = own.shape[0] // 2
    p2 = swap(own, 2)
    p4 = swap(own, 4)
    p6 = jnp.concatenate([swap(p4[:half], 2), swap(p2[half:], 4)], axis=0)
    pieces = []
    for even in (own, p2, p4, p6):
        pieces += [even, swap(even, 1)]
    return pieces


def team_sum(parts):
    half = parts[0].shape[0] // 2
    sums = []
    for k in range(0, TEAM, 2):
        sums.append(parts[k] + swap(parts[k + 1].astype(BF16), 1).astype(F32))
    r0, r2, r4, r6 = sums
    r6 = r6.astype(BF16)
    via_x = swap(r6[:half], 2).astype(F32)
    via_y = swap(r6[half:], 4).astype(F32)
    r4 = jnp.concatenate([r4[:half] + via_x, r4[half:]], axis=0).astype(BF16)
    r2 = jnp.concatenate([r2[:half], r2[half:] + via_y], axis=0).astype(BF16)
    return r0 + swap(r2, 2).astype(F32) + swap(r4, 4).astype(F32)


def place_rows(seq_rows, order, half_rows):
    slots = seq_rows // half_rows
    hit = slots[:, None] == jnp.arange(order.shape[0], dtype=jnp.int32)[None, :]
    return jnp.sum(jnp.where(hit, order[None, :], 0), axis=1) * half_rows + seq_rows % half_rows


def angle_tables(places):
    freqs = THETA ** (-(jnp.arange(HALF).astype(F32) * 2.0 / HEAD_DIM))
    angles = places.astype(F32)[:, None] * freqs[None, :]
    return jnp.cos(angles), jnp.sin(angles)


def rotate(t, cosine, sine):
    a, b = t[..., :HALF], t[..., HALF:]
    return jnp.concatenate([a * cosine - b * sine, b * cosine + a * sine], axis=-1)


def columns_in(own, rows_all):
    n_dp, n_ctx = lax.axis_size("dp"), lax.axis_size("ctx")
    rows, _, width = own.shape
    if n_dp == TEAM:
        mine = lax.all_to_all(own, "dp", 1, 0, tiled=True).reshape(TEAM, rows, width)
        full = lax.all_gather(mine, "ctx", axis=1)
    else:
        whole = lax.all_gather(own, ("dp", "ctx"), axis=0, tiled=True)
        full = lax.dynamic_index_in_dim(whole, lax.axis_index("dp") % TEAM, 1, False)
    return full.reshape(rows_all, width)


def columns_out(grad):
    n_dp, n_ctx = lax.axis_size("dp"), lax.axis_size("ctx")
    rows_all, width = grad.shape
    rows = rows_all // (n_dp * n_ctx)
    grad = grad.astype(BF16)
    if n_dp == TEAM:
        part = lax.psum_scatter(grad.reshape(TEAM, n_ctx, rows, width), "ctx", scatter_dimension=1)
        out = lax.all_to_all(part, "dp", 0, 0, tiled=True)
        return jnp.transpose(out, (1, 0, 2)).astype(F32)
    member = lax.axis_index("dp") % TEAM
    hit = (jnp.arange(TEAM) == member)[None, :, None]
    whole = jnp.where(hit, grad[:, None, :], jnp.zeros((), BF16))
    return lax.psum_scatter(whole, ("dp", "ctx"), scatter_dimension=0, tiled=True).astype(F32)


def rows_in(own):
    n_dp, n_ctx = lax.axis_size("dp"), lax.axis_size("ctx")
    if n_dp == TEAM:
        return lax.all_gather(own, "ctx", axis=0, tiled=True)
    whole = lax.all_gather(own, ("dp", "ctx"), axis=0, tiled=True)
    count = whole.shape[0] // TEAM
    return lax.dynamic_slice_in_dim(whole, (lax.axis_index("dp") % TEAM) * count, count, 0)


def rows_out(grad):
    n_dp = lax.axis_size("dp")
    grad = grad.astype(BF16)
    if n_dp == TEAM:
        return lax.psum_scatter(grad, "ctx", scatter_dimension=0, tiled=True).astype(F32)
    member = lax.axis_index("dp") % TEAM
    hit = (jnp.arange(TEAM) == member)[:, None, None]
    whole = jnp.where(hit, grad[None], jnp.zeros((), BF16)).reshape(-1, grad.shape[1])
    return lax.psum_scatter(whole, ("dp", "ctx"), scatter_dimension=0, tiled=True).astype(F32)


def to_sequences(value):
    n_ctx = lax.axis_size("ctx")
    seqs, span, width = value.shape
    got = lax.all_to_all(value.reshape(n_ctx, seqs // n_ctx, span, width), "ctx", 0, 0, tiled=True)
    return jnp.transpose(got, (1, 0, 2, 3)).reshape(seqs // n_ctx, n_ctx * span, width)


def to_spans(value):
    n_ctx = lax.axis_size("ctx")
    seqs, rows, width = value.shape
    parts = jnp.transpose(value.reshape(seqs, n_ctx, rows // n_ctx, width), (1, 0, 2, 3))
    got = lax.all_to_all(parts, "ctx", 0, 0, tiled=True)
    return got.reshape(n_ctx * seqs, rows // n_ctx, width)


def split_qkv(value):
    shape = value.shape[:-1]
    return (
        value[..., :QW].reshape(*shape, GROUPS, HEAD_DIM),
        value[..., QW : QW + HEAD_DIM],
        value[..., QW + HEAD_DIM :],
    )


def norm_back(e, xhat, r):
    return r * (e - xhat * jnp.mean(e * xhat, axis=-1, keepdims=True))


def local(
    tokens, cotangent, gain_attn, w_query, w_key, w_value, w_out, gain_ffn, w_gate, w_up, w_down, order
):
    _, span, width = tokens.shape
    n_ctx = lax.axis_size("ctx")
    rows = w_query.shape[0]
    length = span * n_ctx
    half_rows = span // 2
    scale = HEAD_DIM**-0.5
    team = range(TEAM)

    def stacked(pieces):
        return jnp.concatenate(pieces, axis=0)

    def cut(value):
        return [value[k * span : (k + 1) * span] for k in team]

    gain_a = gain_attn.astype(F32)[:, None]
    gain_f = gain_ffn.astype(F32)[:, None]
    own_qkv = jnp.concatenate(
        [
            w_query.reshape(rows, TEAM, QW),
            w_key.reshape(rows, TEAM, HEAD_DIM),
            w_value.reshape(rows, TEAM, HEAD_DIM),
        ],
        axis=-1,
    ).astype(F32)
    own_gu = jnp.concatenate([w_gate.reshape(rows, TEAM, -1), w_up.reshape(rows, TEAM, -1)], axis=-1).astype(F32)
    ff = own_gu.shape[-1] // 2
    wqkv = columns_in((own_qkv * gain_a[..., None]).astype(BF16), width)
    wo = rows_in(w_out)
    wgu = columns_in((own_gu * gain_f[..., None]).astype(BF16), width)
    wd = rows_in(w_down)

    x = tokens[0].astype(F32)
    r1 = lax.rsqrt(jnp.mean(x * x, axis=-1, keepdims=True) + EPS)
    xhat1 = x * r1
    x1 = stacked(team_gather(xhat1.astype(BF16)))
    dy_own = cotangent[0]
    dy = stacked(team_gather(dy_own))

    span_rows = lax.axis_index("ctx") * span + jnp.arange(span, dtype=jnp.int32)
    cosine, sine = angle_tables(place_rows(span_rows, order, half_rows))
    place = place_rows(jnp.arange(length, dtype=jnp.int32), order, half_rows)
    allowed = place[None, :] <= place[:, None]

    q, k, v = split_qkv(mm(x1, wqkv).reshape(TEAM, span, QKV))
    q = rotate(q, cosine[:, None], sine[:, None]) * scale
    k = rotate(k, cosine, sine)
    qkv = jnp.concatenate([q.reshape(TEAM, span, QW), k, v], axis=-1).astype(BF16)
    q, k, v = split_qkv(to_sequences(qkv))
    s = jnp.einsum("sqgd,std->sgqt", q, k, preferred_element_type=F32)
    s = jnp.where(allowed, s, -1e30)
    top = jnp.max(s, axis=-1, keepdims=True)
    p = jnp.exp(s - top)
    total = jnp.sum(p, axis=-1, keepdims=True)
    probs = p / total
    heads = jnp.einsum("sgqt,std->sqgd", probs.astype(BF16), v, preferred_element_type=F32)
    heads_low = to_spans(heads.reshape(heads.shape[0], length, QW).astype(BF16)).reshape(TEAM * span, QW)

    middle = x + team_sum(cut(mm(heads_low, wo)))
    r2 = lax.rsqrt(jnp.mean(middle * middle, axis=-1, keepdims=True) + EPS)
    xhat2 = middle * r2
    x2 = stacked(team_gather(xhat2.astype(BF16)))
    gu = mm(x2, wgu)
    gate, upper = gu[:, :ff], gu[:, ff:]
    sigma = jax.nn.sigmoid(gate)
    act = gate * sigma
    hidden = (act * upper).astype(BF16)
    mixed = (middle + team_sum(cut(mm(hidden, wd)))).astype(BF16)[None]

    d_hidden = mm_nt(dy, wd)
    d_gate = d_hidden * upper * sigma * (1.0 + gate * (1.0 - sigma))
    d_up = d_hidden * act
    dgu = jnp.concatenate([d_gate, d_up], axis=-1).astype(BF16)
    e2 = team_sum(cut(mm_nt(dgu, wgu)))
    d_middle = dy_own.astype(F32) + norm_back(e2, xhat2, r2)
    g_gu = columns_out(mm_tn(x2, dgu))
    grad_down = rows_out(mm_tn(hidden, dy))

    dm = stacked(team_gather(d_middle.astype(BF16)))
    d_heads = mm_nt(dm, wo).astype(BF16).reshape(TEAM, span, QW)
    grad_out = rows_out(mm_tn(heads_low, dm))
    d_heads = to_sequences(d_heads).reshape(-1, length, GROUPS, HEAD_DIM)
    delta = jnp.sum(d_heads.astype(F32) * heads, axis=-1)
    dp = jnp.einsum("sqgd,std->sgqt", d_heads, v, preferred_element_type=F32)
    ds = (probs * (dp - jnp.transpose(delta, (0, 2, 1))[..., None])).astype(BF16)
    dq = jnp.einsum("sgqt,std->sqgd", ds, k, preferred_element_type=F32) * scale
    dk = jnp.einsum("sgqt,sqgd->std", ds, q, preferred_element_type=F32)
    dv = jnp.einsum("sgqt,sqgd->std", probs.astype(BF16), d_heads, preferred_element_type=F32)
    cos_all, sin_all = angle_tables(place)
    dq = rotate(dq, cos_all[:, None], -sin_all[:, None])
    dk = rotate(dk, cos_all, -sin_all)
    dqkv = jnp.concatenate([dq.reshape(dq.shape[0], length, QW), dk, dv], axis=-1).astype(BF16)
    dqkv = to_spans(dqkv).reshape(TEAM * span, QKV)
    e1 = team_sum(cut(mm_nt(dqkv, wqkv)))
    token_grad = (d_middle + norm_back(e1, xhat1, r1))[None]
    g_qkv = columns_out(mm_tn(x1, dqkv))

    gain_a_grad = jnp.sum(own_qkv * g_qkv, axis=(1, 2))
    gain_f_grad = jnp.sum(own_gu * g_gu, axis=(1, 2))
    g_qkv = g_qkv * gain_a[..., None]
    g_gu = g_gu * gain_f[..., None]
    return (
        mixed,
        token_grad,
        gain_a_grad,
        g_qkv[..., :QW].reshape(rows, -1),
        g_qkv[..., QW : QW + HEAD_DIM].reshape(rows, -1),
        g_qkv[..., QW + HEAD_DIM :].reshape(rows, -1),
        grad_out,
        gain_f_grad,
        g_gu[..., :ff].reshape(rows, -1),
        g_gu[..., ff:].reshape(rows, -1),
        grad_down,
    )


def solution(mesh):
    act = P("dp", "ctx", None)
    vec = P(("dp", "ctx"))
    mat = P(("dp", "ctx"), None)
    return jax.shard_map(
        local,
        mesh=mesh,
        in_specs=(act, act, vec, mat, mat, mat, mat, vec, mat, mat, mat, P()),
        out_specs=(act, act, vec, mat, mat, mat, mat, vec, mat, mat, mat),
        check_vma=False,
    )
```

```python
import functools

import jax
import jax.numpy as jnp
from jax import lax
from jax.experimental import pallas as pl
from jax.experimental.pallas import tpu as pltpu
from jax.sharding import PartitionSpec as P

HEADS = 16
KV_HEADS = 8
HEAD_DIM = 96
GROUPS = HEADS // KV_HEADS
HALF = HEAD_DIM // 2
QW = GROUPS * HEAD_DIM
QKV = QW + 2 * HEAD_DIM

EPS = 1e-05
THETA = 100000.0
F32 = jnp.float32
BF16 = jnp.bfloat16
CHUNKS = 4
VMEM_BYTES = 56 * 2**20

TEAM = KV_HEADS
PAIRS = TEAM // 2


def dot(a, b, dims):
    return lax.dot_general(a, b, (dims, ((), ())), preferred_element_type=F32)


def mm(a, b):
    return dot(a, b, ((1,), (0,)))


def mm_nt(a, b):
    return dot(a, b, ((1,), (1,)))


def mm_tn(a, b):
    return dot(a, b, ((0,), (0,)))


def swap(value, bit):
    n = lax.axis_size("dp")
    return lax.ppermute(value, "dp", [(i, i ^ bit) for i in range(n)])


def after(value, *others):
    return lax.optimization_barrier((value, *others))[0]


def params():
    return pltpu.CompilerParams(vmem_limit_bytes=VMEM_BYTES)


def cost(flops, nbytes, exps=0):
    return pl.CostEstimate(flops=int(flops), bytes_accessed=int(nbytes), transcendentals=int(exps))


def whole(shape):
    return pl.BlockSpec(shape, lambda *_: (0,) * len(shape))


def join(even_ref, odd_ref):
    return jnp.concatenate([even_ref[...], odd_ref[...]], axis=0)


def qkv_kernel(member_ref, *refs):
    x_refs = refs[:TEAM]
    w_ref, c_ref, s1_ref, s2_ref, out_ref, copy_ref = refs[TEAM:]
    block = x_refs[0].shape[0]
    y = mm(jnp.concatenate([ref[...] for ref in x_refs], axis=0), w_ref[...])
    ahead = pltpu.roll(y, QKV - HALF, 1)
    behind = pltpu.roll(y, HALF, 1)
    for k, x_ref in enumerate(x_refs):
        here = slice(k * block, (k + 1) * block)
        turned = y[here] * c_ref[...] + ahead[here] * s1_ref[...] + behind[here] * s2_ref[...]
        copy_ref[member_ref[k]] = x_ref[...]
        out_ref[member_ref[k]] = turned.astype(BF16)


def qkv_of(member, xs, w, tables):
    rows, width = xs[0].shape
    steps = 4
    block = rows // steps
    rowed = lambda n: pl.BlockSpec((block, n), lambda i, m: (i, 0))
    stacked = lambda n: pl.BlockSpec((TEAM, block, n), lambda i, m: (0, i, 0))
    return pl.pallas_call(
        qkv_kernel,
        grid_spec=pltpu.PrefetchScalarGridSpec(
            num_scalar_prefetch=1,
            grid=(steps,),
            in_specs=[rowed(width)] * TEAM + [whole(w.shape)] + [rowed(QKV)] * 3,
            out_specs=(stacked(QKV), stacked(width)),
        ),
        out_shape=(
            jax.ShapeDtypeStruct((TEAM, rows, QKV), BF16),
            jax.ShapeDtypeStruct((TEAM, rows, width), BF16),
        ),
        compiler_params=params(),
        cost_estimate=cost(2 * TEAM * rows * width * QKV, 4 * TEAM * rows * width + 2 * width * QKV),
        name="qkv",
    )(member, *xs, w, *tables)


def in_order(slots_ref, ref, scratch, half):
    for b in range(slots_ref.shape[0]):
        slot = slots_ref[b]
        at = pl.multiple_of((slot % 2) * half, half)
        scratch[pl.ds(b * half, half), :] = ref[slot // 2, 0, pl.ds(at, half), :]


def heads_in_order(slots_ref, ref, scratch, half):
    for b in range(slots_ref.shape[0]):
        slot = slots_ref[b]
        first, second = ref[slot // 2, 0, :, :QW], ref[slot // 2, 0, :, QW:]
        scratch[pl.ds(b * half, half), :] = jnp.where(slot % 2 == 0, first, second)


def heads_out_of_order(slots_ref, ref, first, value, half):
    for b in range(value.shape[0] // half):
        slot = slots_ref[first // half + b]
        block = value[b * half : (b + 1) * half]

        @pl.when(slot % 2 == 0)
        def _():
            ref[slot // 2, 0, :, :QW] = block

        @pl.when(slot % 2 == 1)
        def _():
            ref[slot // 2, 0, :, QW:] = block


def out_of_order(slots_ref, ref, first, value, half):
    for b in range(value.shape[0] // half):
        slot = slots_ref[first // half + b]
        at = pl.multiple_of((slot % 2) * half, half)
        ref[slot // 2, 0, pl.ds(at, half), :] = value[b * half : (b + 1) * half]


def flip(value):
    return value.astype(F32).T


def stacked_heads(ref, rows):
    return jnp.concatenate([ref[rows, g * HEAD_DIM : (g + 1) * HEAD_DIM] for g in range(GROUPS)], axis=0)


def causal(size):
    key = lax.broadcasted_iota(jnp.int32, (size, GROUPS * size), 0)
    query = lax.broadcasted_iota(jnp.int32, (size, GROUPS * size), 1) % size
    return key <= query


def attend_kernel(slots_ref, qkv_ref, out_ref, lse_ref, scratch):
    span = qkv_ref.shape[2]
    half = span // 2
    size = scratch.shape[0] // CHUNKS
    in_order(slots_ref, qkv_ref, scratch, half)
    v_t = flip(scratch[:, QW + HEAD_DIM :]).astype(BF16)
    allowed = causal(size)
    for i in range(CHUNKS):
        lo, hi = i * size, (i + 1) * size
        q = stacked_heads(scratch, slice(lo, hi))
        k_near = scratch[lo:hi, QW : QW + HEAD_DIM]
        near = jnp.where(allowed, mm_nt(k_near, q), -1e30)
        top = jnp.max(near, axis=0, keepdims=True)
        if i > 0:
            far = mm_nt(scratch[:lo, QW : QW + HEAD_DIM], q)
            top = jnp.maximum(top, jnp.max(far, axis=0, keepdims=True))
        near = jnp.exp(near - top)
        total = jnp.sum(near, axis=0, keepdims=True)
        acc = mm(v_t[:, lo:hi], near.astype(BF16))
        if i > 0:
            far = jnp.exp(far - top)
            total = total + jnp.sum(far, axis=0, keepdims=True)
            acc = acc + mm(v_t[:, :lo], far.astype(BF16))
        lse_ref[0, pl.ds(i, 1), :] = top + jnp.log(total)
        o = (acc / total).T.astype(BF16)
        o = jnp.concatenate([o[g * size : (g + 1) * size] for g in range(GROUPS)], axis=1)
        heads_out_of_order(slots_ref, out_ref, lo, o, half)


def attend_back_kernel(slots_ref, qkv_ref, do_ref, lse_ref, cos_ref, sin_ref, out_ref, scratch, do_scr, dk_scr, dv_scr):
    span = qkv_ref.shape[2]
    half = span // 2
    length = scratch.shape[0]
    size = length // CHUNKS
    scale = HEAD_DIM**-0.5
    in_order(slots_ref, qkv_ref, scratch, half)
    heads_in_order(slots_ref, do_ref, do_scr, half)
    k_t = flip(scratch[:, QW : QW + HEAD_DIM]).astype(BF16)
    allowed = causal(size)
    dk_scr[...] = jnp.zeros_like(dk_scr)
    dv_scr[...] = jnp.zeros_like(dv_scr)
    for i in range(CHUNKS):
        lo, hi = i * size, (i + 1) * size
        q = stacked_heads(scratch, slice(lo, hi))
        do = stacked_heads(do_scr, slice(lo, hi))
        lse = lse_ref[0, pl.ds(i, 1), :]
        spans = [(lo, hi)] + ([(0, lo)] if i > 0 else [])
        probs, prods = [], []
        delta = 0.0
        for at, (a, b) in enumerate(spans):
            p = jnp.exp(mm_nt(scratch[a:b, QW : QW + HEAD_DIM], q) - lse)
            if at == 0:
                p = jnp.where(allowed, p, 0.0)
            prod = p * mm_nt(scratch[a:b, QW + HEAD_DIM :], do)
            delta = delta + jnp.sum(prod, axis=0, keepdims=True)
            probs.append(p)
            prods.append(prod)
        dq_t = 0.0
        for (a, b), p, prod in zip(spans, probs, prods):
            ds = (prod - p * delta).astype(BF16)
            dk_scr[a:b, :] += mm(ds, q)
            dv_scr[a:b, :] += mm(p.astype(BF16), do)
            dq_t = dq_t + mm(k_t[:, a:b], ds)
        c = jnp.concatenate([cos_ref[:, lo:hi]] * GROUPS, axis=1) * scale
        s = jnp.concatenate([sin_ref[:, lo:hi]] * GROUPS, axis=1) * scale
        first, second = dq_t[:HALF], dq_t[HALF:]
        dq = jnp.concatenate([first * c + second * s, second * c - first * s], axis=0).T
        for g in range(GROUPS):
            do_scr[lo:hi, g * HEAD_DIM : (g + 1) * HEAD_DIM] = dq[g * size : (g + 1) * size].astype(BF16)
    for i in range(CHUNKS):
        lo, hi = i * size, (i + 1) * size
        dk_t = dk_scr[lo:hi, :].T
        first, second = dk_t[:HALF], dk_t[HALF:]
        c, s = cos_ref[:, lo:hi], sin_ref[:, lo:hi]
        dk = jnp.concatenate([first * c + second * s, second * c - first * s], axis=0).T
        value = jnp.concatenate([do_scr[lo:hi, :], dk.astype(BF16), dv_scr[lo:hi, :].astype(BF16)], axis=1)
        out_of_order(slots_ref, out_ref, lo, value, half)


def attend(slots, qkv):
    n_ctx, seqs, span, _ = qkv.shape
    length = n_ctx * span
    spec = lambda width: pl.BlockSpec((n_ctx, 1, span, width), lambda i, _: (0, i, 0, 0))
    lse_width = GROUPS * length // CHUNKS
    work = seqs * GROUPS * length * length
    return pl.pallas_call(
        attend_kernel,
        grid_spec=pltpu.PrefetchScalarGridSpec(
            num_scalar_prefetch=1,
            grid=(seqs,),
            in_specs=[spec(QKV)],
            out_specs=(
                pl.BlockSpec((n_ctx, 1, span // 2, 2 * QW), lambda i, _: (0, i, 0, 0)),
                pl.BlockSpec((1, CHUNKS, lse_width), lambda i, _: (i, 0, 0)),
            ),
            scratch_shapes=[pltpu.VMEM((length, QKV), BF16)],
        ),
        out_shape=(
            jax.ShapeDtypeStruct((n_ctx, seqs, span // 2, 2 * QW), BF16),
            jax.ShapeDtypeStruct((seqs, CHUNKS, lse_width), F32),
        ),
        compiler_params=params(),
        cost_estimate=cost(work * 2 * HEAD_DIM * 3, 2 * seqs * length * (QKV + QW), work // 2),
        name="attend",
    )(slots, qkv)


def attend_back(slots, qkv, d_heads, lse, cos_t, sin_t):
    n_ctx, seqs, span, _ = qkv.shape
    length = n_ctx * span
    spec = lambda width: pl.BlockSpec((n_ctx, 1, span, width), lambda i, _: (0, i, 0, 0))
    lse_width = GROUPS * length // CHUNKS
    work = seqs * GROUPS * length * length
    return pl.pallas_call(
        attend_back_kernel,
        grid_spec=pltpu.PrefetchScalarGridSpec(
            num_scalar_prefetch=1,
            grid=(seqs,),
            in_specs=[
                spec(QKV),
                pl.BlockSpec((n_ctx, 1, span // 2, 2 * QW), lambda i, _: (0, i, 0, 0)),
                pl.BlockSpec((1, CHUNKS, lse_width), lambda i, _: (i, 0, 0)),
                pl.BlockSpec((HALF, length), lambda i, _: (0, 0)),
                pl.BlockSpec((HALF, length), lambda i, _: (0, 0)),
            ],
            out_specs=spec(QKV),
            scratch_shapes=[
                pltpu.VMEM((length, QKV), BF16),
                pltpu.VMEM((length, QW), BF16),
                pltpu.VMEM((length, HEAD_DIM), F32),
                pltpu.VMEM((length, HEAD_DIM), F32),
            ],
        ),
        out_shape=jax.ShapeDtypeStruct((n_ctx, seqs, span, QKV), BF16),
        compiler_params=params(),
        cost_estimate=cost(work * 2 * HEAD_DIM * 8, 4 * seqs * length * QKV, work // 2),
        name="attend_back",
    )(slots, qkv, d_heads, lse, cos_t, sin_t)


def parts_kernel(transposed, order_ref, a_ref, w_ref, *out_refs):
    block = a_ref.shape[1]
    a = jnp.concatenate([a_ref[order_ref[k]] for k in range(TEAM)], axis=0)
    y = (mm_nt if transposed else mm)(a, w_ref[...]).astype(BF16)
    for k in range(TEAM):
        out_refs[k // 4 * 2 + k % 2][k // 2 % 2] = y[k * block : (k + 1) * block]


def parts_of(order, a, w, transposed):
    _, rows, depth = a.shape
    width = w.shape[0] if transposed else w.shape[1]
    steps = 4
    block = rows // steps
    return pl.pallas_call(
        functools.partial(parts_kernel, transposed),
        grid_spec=pltpu.PrefetchScalarGridSpec(
            num_scalar_prefetch=1,
            grid=(steps,),
            in_specs=[pl.BlockSpec((TEAM, block, depth), lambda i, m: (0, i, 0)), whole(w.shape)],
            out_specs=(pl.BlockSpec((2, block, width), lambda i, m: (0, i, 0)),) * 4,
        ),
        out_shape=(jax.ShapeDtypeStruct((2, rows, width), BF16),) * 4,
        compiler_params=params(),
        cost_estimate=cost(2 * TEAM * rows * depth * width, 2 * TEAM * rows * (width + depth) + 2 * depth * width),
        name="parts",
    )(order, a, w)


def grad_out_kernel(member_ref, heads_ref, *refs):
    dm_refs, out_ref = refs[:TEAM], refs[TEAM]
    acc = 0.0
    for k, dm in enumerate(dm_refs):
        acc = acc + mm_tn(unfold(heads_ref[member_ref[k]]), dm[...])
    out_ref[...] = acc.astype(BF16)


def grad_out_of(member, heads, dm):
    rows, width = dm[0].shape
    return pl.pallas_call(
        grad_out_kernel,
        grid_spec=pltpu.PrefetchScalarGridSpec(
            num_scalar_prefetch=1,
            grid=(1,),
            in_specs=[whole(t.shape) for t in (heads, *dm)],
            out_specs=whole((QW, width)),
        ),
        out_shape=jax.ShapeDtypeStruct((QW, width), BF16),
        compiler_params=params(),
        cost_estimate=cost(2 * TEAM * rows * QW * width, 2 * TEAM * rows * (width + QW)),
        name="grad_out",
    )(member, heads, *dm)


def unfold(block):
    return jnp.concatenate([block[:, :QW], block[:, QW:]], axis=0)


def middle_kernel(member_ref, heads_ref, x_ref, *refs):
    wo_refs, (middle_ref, xhat_ref) = refs[:TEAM], refs[TEAM:]
    acc = x_ref[...].astype(F32)
    for k, wo_ref in enumerate(wo_refs):
        acc = acc + mm(unfold(heads_ref[member_ref[k]]), wo_ref[...])
    middle_ref[...] = acc
    r = lax.rsqrt(jnp.mean(acc * acc, axis=-1, keepdims=True) + EPS)
    xhat_ref[...] = (acc * r).astype(BF16)


def middle_of(member, x, heads, wo):
    rows, width = x.shape
    return pl.pallas_call(
        middle_kernel,
        grid_spec=pltpu.PrefetchScalarGridSpec(
            num_scalar_prefetch=1,
            grid=(1,),
            in_specs=[whole(t.shape) for t in (heads, x, *wo)],
            out_specs=(whole(x.shape),) * 2,
        ),
        out_shape=(jax.ShapeDtypeStruct(x.shape, F32), jax.ShapeDtypeStruct(x.shape, BF16)),
        compiler_params=params(),
        cost_estimate=cost(2 * rows * width * TEAM * QW, 2 * width * TEAM * QW + 12 * rows * width),
        name="middle",
    )(member, heads, x, *wo)


def d_middle_kernel(member_ref, *refs):
    middle_ref, dy_ref = refs[6:8]
    wo_refs, (d_ref, low_ref, out_ref) = refs[8 : 8 + TEAM], refs[8 + TEAM :]
    middle = middle_ref[...]
    half = middle.shape[0] // 2
    r = lax.rsqrt(jnp.mean(middle * middle, axis=-1, keepdims=True) + EPS)
    d = dy_ref[...].astype(F32) + norm_back(team_total(refs[:6]), middle * r, r)
    d_ref[...] = d
    low = d.astype(BF16)
    low_ref[...] = low
    for k, wo_ref in enumerate(wo_refs):
        m = member_ref[k]
        y = mm_nt(low, wo_ref[...]).astype(BF16)
        out_ref[m, :, :QW] = y[:half]
        out_ref[m, :, QW:] = y[half:]


def d_middle_of(member, sums, middle, dy, wo):
    rows, width = dy.shape
    heads = (TEAM, rows // 2, 2 * QW)
    return pl.pallas_call(
        d_middle_kernel,
        grid_spec=pltpu.PrefetchScalarGridSpec(
            num_scalar_prefetch=1,
            grid=(1,),
            in_specs=summed(sums) + [whole(t.shape) for t in (middle, dy, *wo)],
            out_specs=(whole(dy.shape), whole(dy.shape), whole(heads)),
        ),
        out_shape=(
            jax.ShapeDtypeStruct(dy.shape, F32),
            jax.ShapeDtypeStruct(dy.shape, BF16),
            jax.ShapeDtypeStruct(heads, BF16),
        ),
        compiler_params=params(),
        cost_estimate=cost(2 * rows * width * TEAM * QW, 2 * width * TEAM * QW + 18 * rows * width),
        name="d_middle",
    )(member, *sums, middle, dy, *wo)


def mates_kernel(*refs):
    evens, odds, outs = refs[:2], refs[2:4], refs[4:]
    for j, k in enumerate((6, 2, 4)):
        r = evens[k // 4][k // 2 % 2].astype(F32) + odds[k // 4][k // 2 % 2].astype(F32)
        outs[j][...] = r.astype(BF16)


def mates_sum(evens, odds):
    _, rows, width = evens[0].shape
    half = rows // 2
    steps = 2
    block = half // steps

    def call(first):
        return pl.pallas_call(
            mates_kernel,
            grid=(steps,),
            in_specs=[pl.BlockSpec((2, block, width), lambda i: (0, first * steps + i, 0))] * 4,
            out_specs=(pl.BlockSpec((block, width), lambda i: (i, 0)),) * 3,
            out_shape=(jax.ShapeDtypeStruct((half, width), BF16),) * 3,
            compiler_params=params(),
            cost_estimate=cost(3 * half * width, 18 * half * width),
            name="mates_sum",
        )(*evens, *odds)

    (r6a, r2a, r4a), (r6b, r2b, r4b) = call(0), call(1)
    return r2a, r2b, r4a, r4b, r6a, r6b


def add_kernel(a_ref, b_ref, c_ref, d_ref, ab_ref, cd_ref):
    ab_ref[...] = (a_ref[...].astype(F32) + b_ref[...].astype(F32)).astype(BF16)
    cd_ref[...] = (c_ref[...].astype(F32) + d_ref[...].astype(F32)).astype(BF16)


def two_sums(a, b, c, d):
    return pl.pallas_call(
        add_kernel,
        grid=(1,),
        in_specs=[whole(a.shape)] * 4,
        out_specs=(whole(a.shape),) * 2,
        out_shape=(jax.ShapeDtypeStruct(a.shape, BF16),) * 2,
        compiler_params=params(),
        cost_estimate=cost(2 * a.size, 12 * a.size),
        name="two_sums",
    )(a, b, c, d)


def summed(sums):
    even = sums[0].shape
    return [pl.BlockSpec((1, *even[1:]), lambda *_: (0, 0, 0))] * 2 + [whole(t.shape) for t in sums[2:]]


def team_total(refs):
    even, odd, r2a, r2b, r4a, r4b = refs
    r0 = even[0].astype(F32) + odd[0].astype(F32)
    near = jnp.concatenate([r2a[...], r2b[...]], axis=0).astype(F32)
    far = jnp.concatenate([r4a[...], r4b[...]], axis=0).astype(F32)
    return r0 + near + far


def token_kernel(*refs):
    x_ref, d_ref, out_ref = refs[6:]
    x = x_ref[...].astype(F32)
    r = lax.rsqrt(jnp.mean(x * x, axis=-1, keepdims=True) + EPS)
    out_ref[...] = d_ref[...] + norm_back(team_total(refs[:6]), x * r, r)


def token_gradient(sums, x, d_middle):
    return pl.pallas_call(
        token_kernel,
        grid=(1,),
        in_specs=summed(sums) + [whole(t.shape) for t in (x, d_middle)],
        out_specs=whole(x.shape),
        out_shape=jax.ShapeDtypeStruct(x.shape, F32),
        compiler_params=params(),
        cost_estimate=cost(12 * x.size, 20 * x.size),
        name="token_gradient",
    )(*sums, x, d_middle)


def feed_kernel(*refs):
    x_refs, y_refs = refs[:TEAM], refs[TEAM : 2 * TEAM]
    wgu_any, wd_ref = refs[2 * TEAM : 2 * TEAM + 2]
    even0_ref, odd0_ref, even1_ref, odd1_ref, hidden_ref, dgu_ref, xc_ref, yc_ref, wgu_ref, sem = refs[2 * TEAM + 2 :]
    n_ctx, _, rows, _ = wgu_any.shape
    ff = wd_ref.shape[0]
    block = x_refs[0].shape[0]

    @pl.when(pl.program_id(0) == 0)
    def _():
        copies = [
            pltpu.make_async_copy(
                wgu_any.at[c, m], wgu_ref.at[pl.ds((m * n_ctx + c) * rows, rows)], sem.at[m * n_ctx + c]
            )
            for m in range(TEAM)
            for c in range(n_ctx)
        ]
        for copy in copies:
            copy.start()
        for copy in copies:
            copy.wait()

    for j in range(TEAM):
        xc_ref[j] = x_refs[j][...]
        yc_ref[j] = y_refs[j][...]
    x = jnp.concatenate([ref[...] for ref in x_refs], axis=0)
    y = jnp.concatenate([ref[...] for ref in y_refs], axis=0)
    gate = mm(x, wgu_ref[:, :ff])
    upper = mm(x, wgu_ref[:, ff:])
    d_hidden = mm_nt(y, wd_ref[...])
    sigma = jax.nn.sigmoid(gate)
    act = gate * sigma
    hidden = (act * upper).astype(BF16)
    d_gate = (d_hidden * upper * sigma * (1.0 + gate * (1.0 - sigma))).astype(BF16)
    dgu = jnp.concatenate([d_gate, (d_hidden * act).astype(BF16)], axis=1)
    e = mm_nt(dgu, wgu_ref[...]).astype(BF16)
    outs = (even0_ref, odd0_ref, even1_ref, odd1_ref)
    for j in range(TEAM):
        part = slice(j * block, (j + 1) * block)
        hidden_ref[j] = hidden[part]
        dgu_ref[j] = dgu[part]
        outs[j // 4 * 2 + j % 2][j // 2 % 2] = e[part]


def feed(xs, ys, wgu, wd):
    rows, width = xs[0].shape
    n_ctx, _, own_rows, _ = wgu.shape
    ff = wd.shape[0]
    steps = 4
    block = rows // steps
    widths = (ff, 2 * ff, width, width)
    rowed = pl.BlockSpec((block, width), lambda i: (i, 0))
    return pl.pallas_call(
        feed_kernel,
        grid=(steps,),
        in_specs=[rowed] * (2 * TEAM) + [pl.BlockSpec(memory_space=pl.ANY), whole(wd.shape)],
        out_specs=(pl.BlockSpec((2, block, width), lambda i: (0, i, 0)),) * 4
        + tuple(pl.BlockSpec((TEAM, block, n), lambda i: (0, i, 0)) for n in widths),
        out_shape=(jax.ShapeDtypeStruct((2, rows, width), BF16),) * 4
        + tuple(jax.ShapeDtypeStruct((TEAM, rows, n), BF16) for n in widths),
        scratch_shapes=[
            pltpu.VMEM((TEAM * n_ctx * own_rows, 2 * ff), BF16),
            pltpu.SemaphoreType.DMA((TEAM * n_ctx,)),
        ],
        compiler_params=params(),
        cost_estimate=cost(2 * TEAM * rows * width * 5 * ff, 6 * width * ff + 20 * TEAM * rows * width, TEAM * rows * ff),
        name="feed",
    )(*xs, *ys, wgu, wd)


def fold_kernel(widths, gain_ref, *refs):
    out_ref = refs[-1]
    gain = gain_ref[...]
    for m in range(TEAM):
        at = 0
        for n, ref in zip(widths, refs):
            out_ref[m, :, at : at + n] = (ref[:, m * n : (m + 1) * n].astype(F32) * gain).astype(BF16)
            at += n


def fold(gain, weights):
    widths = tuple(w.shape[1] // TEAM for w in weights)
    out = (TEAM, weights[0].shape[0], sum(widths))
    return pl.pallas_call(
        functools.partial(fold_kernel, widths),
        grid=(1,),
        in_specs=[whole(gain.shape)] + [whole(w.shape) for w in weights],
        out_specs=whole(out),
        out_shape=jax.ShapeDtypeStruct(out, BF16),
        compiler_params=params(),
        cost_estimate=cost(out[0] * out[1] * out[2], 4 * out[0] * out[1] * out[2]),
        name="fold",
    )(gain, *weights)


def unfold_kernel(widths, gain_ref, grad_ref, *refs):
    count = len(widths)
    weights, outs, gain_out = refs[:count], refs[count : 2 * count], refs[2 * count]
    gain = gain_ref[...]
    total = jnp.zeros(gain.shape, F32)
    for m in range(TEAM):
        at = 0
        for n, w_ref, out_ref in zip(widths, weights, outs):
            g = grad_ref[m, :, at : at + n].astype(F32)
            here = slice(m * n, (m + 1) * n)
            total = total + jnp.sum(w_ref[:, here].astype(F32) * g, axis=1, keepdims=True)
            out_ref[:, here] = g * gain
            at += n
    gain_out[...] = total


def gradients(gain, grad, weights):
    widths = tuple(w.shape[1] // TEAM for w in weights)
    return pl.pallas_call(
        functools.partial(unfold_kernel, widths),
        grid=(1,),
        in_specs=[whole(gain.shape), whole(grad.shape)] + [whole(w.shape) for w in weights],
        out_specs=tuple(whole(w.shape) for w in weights) + (whole(gain.shape),),
        out_shape=tuple(jax.ShapeDtypeStruct(w.shape, F32) for w in weights)
        + (jax.ShapeDtypeStruct(gain.shape, F32),),
        compiler_params=params(),
        cost_estimate=cost(4 * grad.size, 8 * grad.size),
        name="gradients",
    )(gain, grad, *weights)


def gathered(own, p1, p2, p4):
    half = own.shape[0] // 2
    p6 = jnp.concatenate([swap(p4[:half], 2), swap(p2[half:], 4)], axis=0)
    return [own, p1, p2, swap(p2, 1), p4, swap(p4, 1), p6, swap(p6, 1)]


def chip_mates(evens):
    pieces = []
    for even in evens:
        pieces += [even, swap(even, 1)]
    return pieces


def tie(*values):
    leaves, tree = jax.tree.flatten(values)
    return jax.tree.unflatten(tree, lax.optimization_barrier(leaves))


def teams():
    n = lax.axis_size("dp")
    return None if n == TEAM else [list(range(i, i + TEAM)) for i in range(0, n, TEAM)]


def team_trade(blocks):
    return lax.all_to_all(blocks, "dp", 0, 0, axis_index_groups=teams(), tiled=True)


def mates_trade(parts):
    evens, odds = (parts[0], parts[2]), (swap(parts[1], 1), swap(parts[3], 1))
    return (evens[0], odds[0]), mates_sum(evens, odds)


def team_sum(own, sums):
    r2a, r2b, r4a, r4b, r6a, r6b = sums
    via_x, via_y = swap(r6a, 2), swap(r6b, 4)
    r2a, r4b = swap(r2a, 2), swap(r4b, 4)
    r4a, r2b = two_sums(r4a, via_x, r2b, via_y)
    return *own, r2a, swap(r2b, 2), swap(r4a, 4), r4b


def direct_sum(own, sums):
    got = [swap(r, bit).astype(F32) for r, bit in zip(sums, (2, 2, 4, 4, 6, 6))]
    r0 = own[0][0].astype(F32) + own[1][0].astype(F32)
    return r0 + jnp.concatenate([got[0] + got[2] + got[4], got[1] + got[3] + got[5]], axis=0)


def place_rows(seq_rows, order, half_rows):
    slots = seq_rows // half_rows
    hit = slots[:, None] == jnp.arange(order.shape[0], dtype=jnp.int32)[None, :]
    return jnp.sum(jnp.where(hit, order[None, :], 0), axis=1) * half_rows + seq_rows % half_rows


def angles(places):
    freqs = THETA ** (-(jnp.arange(HALF).astype(F32) * 2.0 / HEAD_DIM))
    return places.astype(F32)[:, None] * freqs[None, :]


def member_columns(own):
    return lax.all_to_all(own, "dp", 0, 0, tiled=True)


def any_columns(own):
    n_dp, n_ctx = lax.axis_size("dp"), lax.axis_size("ctx")
    gathered = lax.all_gather(own, ("dp", "ctx"), axis=0)
    mine = lax.dynamic_index_in_dim(gathered, lax.axis_index("dp") % TEAM, 1, False)
    per = n_dp // TEAM
    mine = mine.reshape(TEAM, n_ctx, per * own.shape[1], own.shape[2])
    return jnp.transpose(mine, (1, 0, 2, 3))


def by_rows(columns):
    return jnp.transpose(columns, (1, 0, 2, 3)).reshape(-1, columns.shape[-1])


def any_rows(own):
    gathered = lax.all_gather(own, ("dp", "ctx"), axis=0, tiled=True)
    count = gathered.shape[0] // TEAM
    return lax.dynamic_slice_in_dim(gathered, (lax.axis_index("dp") % TEAM) * count, count, 0)


def column_blocks(grad):
    n_dp, n_ctx = lax.axis_size("dp"), lax.axis_size("ctx")
    rows_all, width = grad.shape
    blocks = grad.astype(BF16).reshape(TEAM, n_ctx, rows_all // (n_dp * n_ctx), width)
    return jnp.transpose(blocks, (1, 0, 2, 3))


def columns_home(part):
    return lax.all_to_all(part.astype(BF16), "dp", 0, 0, tiled=True)


def columns_out(grad):
    member = lax.axis_index("dp") % TEAM
    hit = (jnp.arange(TEAM) == member)[None, :, None]
    spread = jnp.where(hit, grad.astype(BF16)[:, None, :], jnp.zeros((), BF16))
    out = lax.psum_scatter(spread, ("dp", "ctx"), scatter_dimension=0, tiled=True)
    return jnp.transpose(out, (1, 0, 2))


def rows_out(grad):
    grad = grad.astype(BF16)
    if lax.axis_size("dp") == TEAM:
        return lax.psum_scatter(grad, "ctx", scatter_dimension=0, tiled=True).astype(F32)
    member = lax.axis_index("dp") % TEAM
    hit = (jnp.arange(TEAM) == member)[:, None, None]
    spread = jnp.where(hit, grad[None], jnp.zeros((), BF16)).reshape(-1, grad.shape[1])
    return lax.psum_scatter(spread, ("dp", "ctx"), scatter_dimension=0, tiled=True).astype(F32)


def exchange(value):
    n_ctx = lax.axis_size("ctx")
    parts = value.reshape(n_ctx, TEAM // n_ctx, *value.shape[-2:])
    return lax.all_to_all(parts, "ctx", 0, 0, tiled=True)


def ctx_gather(own):
    n_ctx = lax.axis_size("ctx")
    return lax.all_to_all(jnp.broadcast_to(own, (n_ctx, *own.shape)), "ctx", 0, 0, tiled=True)


def by_member(value):
    return value.reshape(TEAM, *value.shape[-2:])


def flat(value):
    return value.reshape(-1, value.shape[-1])


def norm_back(e, xhat, r):
    return r * (e - xhat * jnp.mean(e * xhat, axis=-1, keepdims=True))


def local(
    tokens, cotangent, gain_attn, w_query, w_key, w_value, w_out, gain_ffn, w_gate, w_up, w_down, order
):
    _, span, width = tokens.shape
    n_ctx = lax.axis_size("ctx")
    rows = w_query.shape[0]
    length = span * n_ctx
    half_rows = span // 2
    scale = HEAD_DIM**-0.5

    gain_a = gain_attn.astype(F32)[:, None]
    gain_f = gain_ffn.astype(F32)[:, None]
    span_rows = lax.axis_index("ctx") * span + jnp.arange(span, dtype=jnp.int32)
    places = place_rows(span_rows, order, half_rows).astype(F32)
    lane = jnp.arange(QKV, dtype=jnp.int32)
    turned = lane < QW + HEAD_DIM
    freq = jnp.where(turned, THETA ** (-((lane % HALF).astype(F32) * 2.0 / HEAD_DIM)), 0.0)
    size = jnp.where(lane < QW, scale, 1.0)
    turn = places[:, None] * freq[None, :]
    sine = jnp.sin(turn) * size
    first = lane % HEAD_DIM < HALF
    tables = (jnp.cos(turn) * size, jnp.where(first, -sine, 0.0), jnp.where(first, 0.0, sine))
    turn_t = angles(jnp.arange(length, dtype=jnp.int32)).T
    cos_t, sin_t = jnp.cos(turn_t), jnp.sin(turn_t)
    index = jnp.arange(order.shape[0], dtype=jnp.int32)
    slots = jnp.sum(jnp.where(order[None, :] == index[:, None], index[None, :], 0), axis=1)

    member = lax.axis_index("dp") % TEAM ^ jnp.arange(TEAM, dtype=jnp.int32)


    tok = tokens[0]
    x = tok.astype(F32)
    r1 = lax.rsqrt(jnp.mean(x * x, axis=-1, keepdims=True) + EPS)
    xhat1 = x * r1
    low_x1 = xhat1.astype(BF16)
    low_qkv = fold(gain_a, (w_query, w_key, w_value))
    low_gu = fold(gain_f, (w_gate, w_up))
    one_team = lax.axis_size("dp") == TEAM
    if one_team:
        wd = lax.all_gather(w_down, "ctx", axis=0, tiled=True)
        mine = member_columns(low_qkv)
        low_x1, mine = tie(low_x1, mine)
        got = ctx_gather(jnp.concatenate([mine.reshape(-1, QKV), w_out.reshape(-1, QKV)], axis=0))
        cut = TEAM * rows
        wqkv = by_rows(got[:, :cut].reshape(n_ctx, TEAM, rows, QKV))
        wo = got[:, cut:].reshape(QW, width)
    else:
        wqkv, wo = by_rows(any_columns(low_qkv)), any_rows(w_out)
    p2, p4, p1 = swap(low_x1, 2), swap(low_x1, 4), swap(low_x1, 1)
    p2, p4, tables = tie(p2, p4, tables)
    x1 = gathered(low_x1, p1, p2, p4)

    if one_team:
        x1[6], low_gu = tie(x1[6], low_gu)
        mine_gu = member_columns(low_gu)
    qkv, x1_all = qkv_of(member, x1, wqkv, tables)
    if one_team:
        qkv, mine_gu = tie(qkv, mine_gu)
    else:
        wd, wgu = any_rows(w_down), by_rows(any_columns(low_gu)).reshape(1, TEAM, width // TEAM, -1)

    dy_own, wo, qkv = tie(cotangent[0], wo, qkv)
    dy_even = [dy_own, swap(dy_own, 2), swap(dy_own, 4)]
    wo_even = [wo, swap(wo, 2), swap(wo, 4), swap(wo, 6)]
    qkv = exchange(qkv)
    qkv, dy_even, wo_even = tie(qkv, dy_even, wo_even)

    if one_team:
        wgu = lax.all_gather(after(mine_gu, qkv), "ctx", axis=0)
    dy_even = [*dy_even, swap(dy_even[0], 6)]
    wo_all = chip_mates(wo_even)
    heads, lse = attend(slots, qkv)
    heads = by_member(exchange(heads))
    heads, dy_even, wo_all = tie(heads, dy_even, wo_all)

    traded = team_trade(heads)
    middle, xhat2 = middle_of(member, tok, traded, wo_all)
    p2, p4, p1 = swap(xhat2, 2), swap(xhat2, 4), swap(xhat2, 1)
    dy = chip_mates(dy_even)
    p2, p4, p1, dy = tie(p2, p4, p1, dy)
    x2 = gathered(xhat2, p1, p2, p4)
    *parts, hidden, dgu, x2_all, dy_all = feed(x2, dy, wgu, wd)
    own, (r2a, r2b, r4a, r4b, r6a, r6b) = mates_trade(parts)

    r6a, r6b, dy_all = tie(r6a, r6b, dy_all)
    via_x, via_y = swap(r6a, 2), swap(r6b, 4)
    r2a, r4b = swap(r2a, 2), swap(r4b, 4)
    via_x, via_y, x2_all = tie(via_x, via_y, x2_all)
    r4a, r2b = two_sums(r4a, via_x, r2b, via_y)
    sums = (*own, r2a, swap(r2b, 2), swap(r4a, 4), r4b)
    g_gu = mm_tn(flat(x2_all), flat(dgu))
    if one_team:
        blocks_gu = column_blocks(g_gu)
        part_gu = lax.psum_scatter(blocks_gu.reshape(-1, blocks_gu.shape[-1]), "ctx", scatter_dimension=0, tiled=True)
        part_gu = part_gu.reshape(blocks_gu.shape[1:])
    g_down = mm_tn(flat(hidden), flat(dy_all)).astype(BF16)
    grad_down = rows_out(g_down)
    sums, g_down, g_gu = tie(sums, g_down, blocks_gu if one_team else g_gu)
    d_middle, d_low, d_heads = d_middle_of(member, sums, middle, dy_own, wo_all)
    d_heads = team_trade(d_heads)

    d_low, d_heads, hidden = tie(d_low, d_heads, hidden)
    dm_even = [d_low, swap(d_low, 2), swap(d_low, 4)]
    d_heads = exchange(d_heads)
    mixed_parts = parts_of(jnp.arange(TEAM, dtype=jnp.int32), hidden, wd, False)
    d_heads, dm_even, mixed_parts = tie(d_heads, dm_even, mixed_parts)

    dm_even = [*dm_even, swap(dm_even[0], 6)]
    mixed_sums = mates_trade(mixed_parts)
    dqkv = attend_back(slots, qkv, d_heads, lse, cos_t, sin_t)
    dqkv, dm_even, mixed_sums, grad_down = tie(dqkv, dm_even, mixed_sums, grad_down)

    g_out = grad_out_of(member, heads, chip_mates(dm_even))
    mixed_sum = direct_sum(*mixed_sums)
    g_gu = columns_home(part_gu) if one_team else columns_out(g_gu)
    dqkv = by_member(exchange(dqkv))
    dqkv, mixed_sum, g_out, g_gu = tie(dqkv, mixed_sum, g_out, g_gu)

    mixed = (middle + mixed_sum).astype(BF16)[None]
    *grads_gu, gain_f_grad = gradients(gain_f, g_gu, (w_gate, w_up))
    g_qkv = mm_tn(flat(x1_all), flat(dqkv))
    if one_team:
        blocks_qkv = column_blocks(g_qkv)
        moved = lax.all_to_all(blocks_qkv, "ctx", 0, 0, tiled=True)
        dqkv, blocks_qkv = tie(dqkv, blocks_qkv)
    sums = team_sum(*mates_trade(parts_of(member, dqkv, wqkv, True)))
    if one_team:
        sums, moved, g_out = tie(sums, moved, g_out)
        g_qkv = columns_home(jnp.sum(moved.astype(F32), axis=0))
    else:
        g_qkv = columns_out(g_qkv)
    grad_out = rows_out(g_out)
    token_grad = token_gradient(sums, tok, d_middle)[None]
    *grads_qkv, gain_a_grad = gradients(gain_a, g_qkv, (w_query, w_key, w_value))
    return (
        mixed,
        token_grad,
        gain_a_grad[:, 0],
        *grads_qkv,
        grad_out,
        gain_f_grad[:, 0],
        *grads_gu,
        grad_down,
    )


def solution(mesh):
    act = P("dp", "ctx", None)
    vec = P(("dp", "ctx"))
    mat = P(("dp", "ctx"), None)
    return jax.shard_map(
        local,
        mesh=mesh,
        in_specs=(act, act, vec, mat, mat, mat, mat, vec, mat, mat, mat, P()),
        out_specs=(act, act, vec, mat, mat, mat, mat, vec, mat, mat, mat),
        check_vma=False,
    )
```

```python
import functools

import jax
import jax.numpy as jnp
from jax import lax
from jax.experimental import pallas as pl
from jax.experimental.pallas import tpu as pltpu
from jax.sharding import PartitionSpec as P

HEADS = 16
KV_HEADS = 8
HEAD_DIM = 96
GROUPS = HEADS // KV_HEADS
HALF = HEAD_DIM // 2
QW = GROUPS * HEAD_DIM
QKV = QW + 2 * HEAD_DIM

EPS = 1e-05
THETA = 100000.0
F32 = jnp.float32
BF16 = jnp.bfloat16
CHUNKS = 4
VMEM_BYTES = 56 * 2**20
SMALL_BYTES = 20 * 2**20

TEAM = KV_HEADS
PAIRS = TEAM // 2


def dot(a, b, dims):
    return lax.dot_general(a, b, (dims, ((), ())), preferred_element_type=F32)


def mm(a, b):
    return dot(a, b, ((1,), (0,)))


def mm_nt(a, b):
    return dot(a, b, ((1,), (1,)))


def mm_tn(a, b):
    return dot(a, b, ((0,), (0,)))


def swap(value, bit):
    n = lax.axis_size("dp")
    return lax.ppermute(value, "dp", [(i, i ^ bit) for i in range(n)])


def after(value, *others):
    return lax.optimization_barrier((value, *others))[0]


def params(limit=VMEM_BYTES):
    return pltpu.CompilerParams(vmem_limit_bytes=limit)


def cost(flops, nbytes, exps=0):
    return pl.CostEstimate(flops=int(flops), bytes_accessed=int(nbytes), transcendentals=int(exps))


def whole(shape):
    return pl.BlockSpec(shape, lambda *_: (0,) * len(shape))


def join(even_ref, odd_ref):
    return jnp.concatenate([even_ref[...], odd_ref[...]], axis=0)


def qkv_kernel(seqs, *refs):
    x_refs = refs[:seqs]
    w_ref, c_ref, s1_ref, s2_ref, out_ref = refs[seqs:]
    block = c_ref.shape[0]
    y = mm(jnp.concatenate([ref[0] for ref in x_refs], axis=0), w_ref[...])
    ahead = pltpu.roll(y, QKV - HALF, 1)
    behind = pltpu.roll(y, HALF, 1)
    for k in range(seqs):
        here = slice(k * block, (k + 1) * block)
        turned = y[here] * c_ref[...] + ahead[here] * s1_ref[...] + behind[here] * s2_ref[...]
        out_ref[k, 0] = turned.astype(BF16)


def qkv_of(xs, w, tables):
    n_ctx, span, width = xs[0].shape
    seqs = len(xs)
    return pl.pallas_call(
        functools.partial(qkv_kernel, seqs),
        grid=(n_ctx,),
        in_specs=[pl.BlockSpec((1, span, width), lambda i: (i, 0, 0))] * seqs
        + [whole(w.shape)]
        + [pl.BlockSpec((span, QKV), lambda i: (i, 0))] * 3,
        out_specs=pl.BlockSpec((seqs, 1, span, QKV), lambda i: (0, i, 0, 0)),
        out_shape=jax.ShapeDtypeStruct((seqs, n_ctx, span, QKV), BF16),
        compiler_params=params(),
        cost_estimate=cost(2 * seqs * n_ctx * span * width * QKV, 2 * seqs * n_ctx * span * width + 2 * width * QKV),
        name="qkv",
    )(*xs, w, *tables)


def rows_kernel(member_ref, *refs):
    pieces, out_ref = refs[:-1], refs[-1]
    n_ctx, _, rows, _ = pieces[0].shape
    for p, piece in enumerate(pieces):
        for c in range(n_ctx):
            for j in range(2):
                at = pl.multiple_of((member_ref[2 * p + j] * n_ctx + c) * rows, 16)
                out_ref[pl.ds(at, rows), :] = piece[c, j]


def rows_of(member, pieces):
    n_ctx, two, rows, width = pieces[0].shape
    out = (len(pieces) * n_ctx * two * rows, width)
    return pl.pallas_call(
        rows_kernel,
        grid_spec=pltpu.PrefetchScalarGridSpec(
            num_scalar_prefetch=1,
            grid=(1,),
            in_specs=[whole(t.shape) for t in pieces],
            out_specs=whole(out),
        ),
        out_shape=jax.ShapeDtypeStruct(out, BF16),
        compiler_params=params(SMALL_BYTES),
        cost_estimate=cost(0, 4 * out[0] * out[1]),
        name="rows",
    )(member, *pieces)


def pieces_kernel(member_ref, grad_ref, *out_refs):
    for p, out_ref in enumerate(out_refs):
        for j in range(2):
            out_ref[j] = grad_ref[member_ref[2 * p + j]].astype(BF16)


def pieces_of(member, grad):
    rows, width = grad.shape[0] // TEAM, grad.shape[1]
    return pl.pallas_call(
        pieces_kernel,
        grid_spec=pltpu.PrefetchScalarGridSpec(
            num_scalar_prefetch=1,
            grid=(1,),
            in_specs=[whole((TEAM, rows, width))],
            out_specs=(whole((2, rows, width)),) * PAIRS,
        ),
        out_shape=(jax.ShapeDtypeStruct((2, rows, width), BF16),) * PAIRS,
        compiler_params=params(SMALL_BYTES),
        cost_estimate=cost(0, 6 * grad.size),
        name="pieces",
    )(member, grad.reshape(TEAM, rows, width))


def stack_kernel(order_ref, *refs):
    for k, ref in enumerate(refs[:-1]):
        refs[-1][order_ref[k]] = ref[...]


def stack(order, xs):
    rows, width = xs[0].shape
    steps = 4
    block = rows // steps
    return pl.pallas_call(
        stack_kernel,
        grid_spec=pltpu.PrefetchScalarGridSpec(
            num_scalar_prefetch=1,
            grid=(steps,),
            in_specs=[pl.BlockSpec((block, width), lambda i, m: (i, 0))] * len(xs),
            out_specs=pl.BlockSpec((len(xs), block, width), lambda i, m: (0, i, 0)),
        ),
        out_shape=jax.ShapeDtypeStruct((len(xs), rows, width), BF16),
        compiler_params=params(),
        cost_estimate=cost(0, 4 * len(xs) * rows * width),
        name="stack",
    )(order, *xs)


def in_order(slots_ref, ref, scratch, half):
    for b in range(slots_ref.shape[0]):
        slot = slots_ref[b]
        at = pl.multiple_of((slot % 2) * half, half)
        scratch[pl.ds(b * half, half), :] = ref[slot // 2, pl.ds(at, half), :]


def heads_in_order(slots_ref, ref, scratch, half):
    for b in range(slots_ref.shape[0]):
        slot = slots_ref[b]
        first, second = ref[slot // 2, :, :QW], ref[slot // 2, :, QW:]
        scratch[pl.ds(b * half, half), :] = jnp.where(slot % 2 == 0, first, second)


def heads_out_of_order(order_ref, ref, scratch, half):
    for c in range(ref.shape[0]):
        for j in range(2):
            at = pl.multiple_of(order_ref[2 * c + j] * half, half)
            ref[c, :, j * QW : (j + 1) * QW] = scratch[pl.ds(at, half), :]


def out_of_order(slots_ref, ref, first, value, half):
    for b in range(value.shape[0] // half):
        slot = slots_ref[first // half + b]
        at = pl.multiple_of((slot % 2) * half, half)
        ref[slot // 2, pl.ds(at, half), :] = value[b * half : (b + 1) * half]


def flip(value):
    return value.astype(F32).T


def stacked_heads(ref, rows):
    return jnp.concatenate([ref[rows, g * HEAD_DIM : (g + 1) * HEAD_DIM] for g in range(GROUPS)], axis=0)


def causal(size):
    key = lax.broadcasted_iota(jnp.int32, (size, GROUPS * size), 0)
    query = lax.broadcasted_iota(jnp.int32, (size, GROUPS * size), 1) % size
    return key <= query


def attend_kernel(slots_ref, order_ref, qkv_ref, out_ref, lse_ref, scratch, o_scr):
    half = qkv_ref.shape[2] // 2
    size = scratch.shape[0] // CHUNKS
    in_order(slots_ref, qkv_ref.at[0], scratch, half)
    v_t = flip(scratch[:, QW + HEAD_DIM :]).astype(BF16)
    allowed = causal(size)
    for i in range(CHUNKS):
        lo, hi = i * size, (i + 1) * size
        q = stacked_heads(scratch, slice(lo, hi))
        k_near = scratch[lo:hi, QW : QW + HEAD_DIM]
        near = jnp.where(allowed, mm_nt(k_near, q), -1e30)
        top = jnp.max(near, axis=0, keepdims=True)
        if i > 0:
            far = mm_nt(scratch[:lo, QW : QW + HEAD_DIM], q)
            top = jnp.maximum(top, jnp.max(far, axis=0, keepdims=True))
        near = jnp.exp(near - top)
        total = jnp.sum(near, axis=0, keepdims=True)
        acc = mm(v_t[:, lo:hi], near.astype(BF16))
        if i > 0:
            far = jnp.exp(far - top)
            total = total + jnp.sum(far, axis=0, keepdims=True)
            acc = acc + mm(v_t[:, :lo], far.astype(BF16))
        lse_ref[pl.ds(i, 1), :] = top + jnp.log(total)
        o = (acc / total).T.astype(BF16)
        for g in range(GROUPS):
            o_scr[lo:hi, g * HEAD_DIM : (g + 1) * HEAD_DIM] = o[g * size : (g + 1) * size]
    heads_out_of_order(order_ref, out_ref, o_scr, half)


def attend_back_kernel(slots_ref, qkv_ref, do_ref, lse_ref, cos_ref, sin_ref, out_ref, scratch, do_scr, dk_scr, dv_scr):
    half = qkv_ref.shape[2] // 2
    length = scratch.shape[0]
    size = length // CHUNKS
    scale = HEAD_DIM**-0.5
    in_order(slots_ref, qkv_ref.at[0], scratch, half)
    heads_in_order(slots_ref, do_ref, do_scr, half)
    k_t = flip(scratch[:, QW : QW + HEAD_DIM]).astype(BF16)
    allowed = causal(size)
    dk_scr[...] = jnp.zeros_like(dk_scr)
    dv_scr[...] = jnp.zeros_like(dv_scr)
    for i in range(CHUNKS):
        lo, hi = i * size, (i + 1) * size
        q = stacked_heads(scratch, slice(lo, hi))
        do = stacked_heads(do_scr, slice(lo, hi))
        lse = lse_ref[pl.ds(i, 1), :]
        spans = [(lo, hi)] + ([(0, lo)] if i > 0 else [])
        probs, prods = [], []
        delta = 0.0
        for at, (a, b) in enumerate(spans):
            p = jnp.exp(mm_nt(scratch[a:b, QW : QW + HEAD_DIM], q) - lse)
            if at == 0:
                p = jnp.where(allowed, p, 0.0)
            prod = p * mm_nt(scratch[a:b, QW + HEAD_DIM :], do)
            delta = delta + jnp.sum(prod, axis=0, keepdims=True)
            probs.append(p)
            prods.append(prod)
        dq_t = 0.0
        for (a, b), p, prod in zip(spans, probs, prods):
            ds = (prod - p * delta).astype(BF16)
            dk_scr[a:b, :] += mm(ds, q)
            dv_scr[a:b, :] += mm(p.astype(BF16), do)
            dq_t = dq_t + mm(k_t[:, a:b], ds)
        c = jnp.concatenate([cos_ref[:, lo:hi]] * GROUPS, axis=1) * scale
        s = jnp.concatenate([sin_ref[:, lo:hi]] * GROUPS, axis=1) * scale
        first, second = dq_t[:HALF], dq_t[HALF:]
        dq = jnp.concatenate([first * c + second * s, second * c - first * s], axis=0).T
        for g in range(GROUPS):
            do_scr[lo:hi, g * HEAD_DIM : (g + 1) * HEAD_DIM] = dq[g * size : (g + 1) * size].astype(BF16)
    for i in range(CHUNKS):
        lo, hi = i * size, (i + 1) * size
        dk_t = dk_scr[lo:hi, :].T
        first, second = dk_t[:HALF], dk_t[HALF:]
        c, s = cos_ref[:, lo:hi], sin_ref[:, lo:hi]
        dk = jnp.concatenate([first * c + second * s, second * c - first * s], axis=0).T
        value = jnp.concatenate([do_scr[lo:hi, :], dk.astype(BF16), dv_scr[lo:hi, :].astype(BF16)], axis=1)
        out_of_order(slots_ref, out_ref, lo, value, half)


def attend(slots, order, qkv, seq):
    _, n_ctx, span, _ = qkv.shape
    length = n_ctx * span
    heads = (n_ctx, span // 2, 2 * QW)
    lse = (CHUNKS, GROUPS * length // CHUNKS)
    work = GROUPS * length * length
    return pl.pallas_call(
        attend_kernel,
        grid_spec=pltpu.PrefetchScalarGridSpec(
            num_scalar_prefetch=2,
            grid=(1,),
            in_specs=[pl.BlockSpec((1, n_ctx, span, QKV), lambda *_: (seq, 0, 0, 0))],
            out_specs=(whole(heads), whole(lse)),
            scratch_shapes=[pltpu.VMEM((length, QKV), BF16), pltpu.VMEM((length, QW), BF16)],
        ),
        out_shape=(jax.ShapeDtypeStruct(heads, BF16), jax.ShapeDtypeStruct(lse, F32)),
        compiler_params=params(),
        cost_estimate=cost(work * 2 * HEAD_DIM * 3, 2 * length * (QKV + QW), work // 2),
        name="attend",
    )(slots, order, qkv)


def attend_back(slots, qkv, seq, d_heads, lse, cos_t, sin_t):
    _, n_ctx, span, _ = qkv.shape
    length = n_ctx * span
    work = GROUPS * length * length
    return pl.pallas_call(
        attend_back_kernel,
        grid_spec=pltpu.PrefetchScalarGridSpec(
            num_scalar_prefetch=1,
            grid=(1,),
            in_specs=[pl.BlockSpec((1, n_ctx, span, QKV), lambda *_: (seq, 0, 0, 0))]
            + [whole(t.shape) for t in (d_heads, lse, cos_t, sin_t)],
            out_specs=whole((n_ctx, span, QKV)),
            scratch_shapes=[
                pltpu.VMEM((length, QKV), BF16),
                pltpu.VMEM((length, QW), BF16),
                pltpu.VMEM((length, HEAD_DIM), F32),
                pltpu.VMEM((length, HEAD_DIM), F32),
            ],
        ),
        out_shape=jax.ShapeDtypeStruct((n_ctx, span, QKV), BF16),
        compiler_params=params(),
        cost_estimate=cost(work * 2 * HEAD_DIM * 8, 4 * length * QKV, work // 2),
        name="attend_back",
    )(slots, qkv, d_heads, lse, cos_t, sin_t)


def parts_kernel(a_ref, packed, *refs):
    out_refs, (wd_ref, sem) = refs[:4], refs[4:]

    @pl.when(pl.program_id(0) == 0)
    def _():
        copies = [pltpu.make_async_copy(src, dst, sem.at[i]) for i, (src, dst) in enumerate(down_ways(packed, wd_ref))]
        for copy in copies:
            copy.start()
        for copy in copies:
            copy.wait()

    block = a_ref.shape[1]
    y = mm(jnp.concatenate([a_ref[k] for k in range(TEAM)], axis=0), wd_ref[...]).astype(BF16)
    for k in range(TEAM):
        out_refs[k // 4 * 2 + k % 2][k // 2 % 2] = y[k * block : (k + 1) * block]


def parts_of(a, packed, width):
    _, rows, depth = a.shape
    steps = 4
    block = rows // steps
    return pl.pallas_call(
        parts_kernel,
        grid=(steps,),
        in_specs=[pl.BlockSpec((TEAM, block, depth), lambda i: (0, i, 0)), pl.BlockSpec(memory_space=pl.ANY)],
        out_specs=(pl.BlockSpec((2, block, width), lambda i: (0, i, 0)),) * 4,
        out_shape=(jax.ShapeDtypeStruct((2, rows, width), BF16),) * 4,
        scratch_shapes=[
            pltpu.VMEM((depth, width), BF16),
            pltpu.SemaphoreType.DMA((packed.shape[0] * (width // depth),)),
        ],
        compiler_params=params(SMALL_BYTES),
        cost_estimate=cost(2 * TEAM * rows * depth * width, 2 * TEAM * rows * (width + depth) + 2 * depth * width),
        name="parts",
    )(a, packed)


def input_own_kernel(a_ref, w_ref, *refs):
    y = mm_nt(a_ref[0], w_ref[...])
    for ref in refs[:-1]:
        y = y + ref[0].astype(F32)
    refs[-1][0] = y.astype(BF16)


def input_own(a, w, more):
    n_ctx, span, depth = a.shape
    width = w.shape[0]
    blocked = lambda n: pl.BlockSpec((1, span, n), lambda i: (i, 0, 0))
    return pl.pallas_call(
        input_own_kernel,
        grid=(n_ctx,),
        in_specs=[blocked(depth), whole(w.shape)] + [blocked(width)] * len(more),
        out_specs=blocked(width),
        out_shape=jax.ShapeDtypeStruct((n_ctx, span, width), BF16),
        compiler_params=params(),
        cost_estimate=cost(2 * n_ctx * span * depth * width, 4 * n_ctx * span * (width + depth) + 2 * depth * width),
        name="input_own",
    )(a, w, *more)


def input_all_kernel(a_ref, w_ref, out_ref):
    out_ref[0] = mm_nt(a_ref[0], w_ref[...]).astype(BF16)


def input_all(a, w):
    n_ctx, span, depth = a.shape
    width = w.shape[0]
    blocked = lambda n: pl.BlockSpec((1, span, n), lambda i: (i, 0, 0))
    return pl.pallas_call(
        input_all_kernel,
        grid=(n_ctx,),
        in_specs=[blocked(depth), whole(w.shape)],
        out_specs=blocked(width),
        out_shape=jax.ShapeDtypeStruct((n_ctx, span, width), BF16),
        compiler_params=params(),
        cost_estimate=cost(2 * n_ctx * span * depth * width, 4 * n_ctx * span * (width + depth) + 2 * depth * width),
        name="input_all",
    )(a, w)


def grad_out_kernel(at_ref, heads_ref, dm_ref, *out_refs):
    dm = dm_ref[...]
    for k in range(TEAM):
        y = mm_tn(unfold(heads_ref[at_ref[k]]), dm)
        out_refs[k // 4 * 2 + k % 2][k // 2 % 2] = y.astype(BF16)


def grad_out_parts(member_at, heads, dm):
    rows, width = dm.shape
    return pl.pallas_call(
        grad_out_kernel,
        grid_spec=pltpu.PrefetchScalarGridSpec(
            num_scalar_prefetch=1,
            grid=(1,),
            in_specs=[whole(t.shape) for t in (heads, dm)],
            out_specs=(whole((2, QW, width)),) * 4,
        ),
        out_shape=(jax.ShapeDtypeStruct((2, QW, width), BF16),) * 4,
        compiler_params=params(),
        cost_estimate=cost(2 * TEAM * rows * QW * width, 2 * TEAM * QW * width),
        name="grad_out",
    )(member_at, heads, dm)


def unfold(block):
    return jnp.concatenate([block[:, :QW], block[:, QW:]], axis=0)


def fetch(any_refs, ref, sem):
    copies = [pltpu.make_async_copy(a, ref.at[k], sem.at[k]) for k, a in enumerate(any_refs)]
    for copy in copies:
        copy.start()
    return copies


def fetched(arrays):
    specs = [pl.BlockSpec(memory_space=pl.ANY)] * len(arrays)
    scratch = [pltpu.VMEM((len(arrays), *arrays[0].shape), BF16), pltpu.SemaphoreType.DMA((len(arrays),))]
    return specs, scratch


def middle_kernel(at_ref, heads_ref, x_ref, *refs):
    wo_any, (middle_ref, xhat_ref, wo_ref, sem) = refs[:TEAM], refs[TEAM:]
    copies = fetch(wo_any, wo_ref, sem)
    heads = jnp.concatenate([unfold(heads_ref[at_ref[k]]) for k in range(TEAM)], axis=1)
    for copy in copies:
        copy.wait()
    acc = x_ref[...].astype(F32) + mm(heads, wo_ref[...].reshape(heads.shape[1], -1))
    middle_ref[...] = acc
    r = lax.rsqrt(jnp.mean(acc * acc, axis=-1, keepdims=True) + EPS)
    xhat_ref[...] = (acc * r).astype(BF16)


def middle_of(member_at, x, heads, wo):
    rows, width = x.shape
    specs, scratch = fetched(wo)
    return pl.pallas_call(
        middle_kernel,
        grid_spec=pltpu.PrefetchScalarGridSpec(
            num_scalar_prefetch=1,
            grid=(1,),
            in_specs=[whole(t.shape) for t in (heads, x)] + specs,
            out_specs=(whole(x.shape),) * 2,
            scratch_shapes=scratch,
        ),
        out_shape=(jax.ShapeDtypeStruct(x.shape, F32), jax.ShapeDtypeStruct(x.shape, BF16)),
        compiler_params=params(),
        cost_estimate=cost(2 * rows * width * TEAM * QW, 2 * width * TEAM * QW + 12 * rows * width),
        name="middle",
    )(member_at, heads, x, *wo)


def d_middle_kernel(at_ref, *refs):
    middle_ref, dy_ref = refs[5:7]
    wo_any, (d_ref, low_ref, out_ref, wo_ref, sem) = refs[7 : 7 + TEAM], refs[7 + TEAM :]
    copies = fetch(wo_any, wo_ref, sem)
    middle = middle_ref[...]
    half = middle.shape[0] // 2
    r = lax.rsqrt(jnp.mean(middle * middle, axis=-1, keepdims=True) + EPS)
    d = dy_ref[...].astype(F32) + norm_back(team_total(refs[:5]), middle * r, r)
    d_ref[...] = d
    low = d.astype(BF16)
    low_ref[...] = low
    for copy in copies:
        copy.wait()
    y = mm_nt(low, wo_ref[...].reshape(TEAM * QW, -1)).astype(BF16)
    for k in range(TEAM):
        part = slice(k * QW, (k + 1) * QW)
        out_ref[at_ref[k], :, :QW] = y[:half, part]
        out_ref[at_ref[k], :, QW:] = y[half:, part]


def d_middle_of(member_at, sums, middle, dy, wo):
    rows, width = dy.shape
    heads = (TEAM, rows // 2, 2 * QW)
    specs, scratch = fetched(wo)
    return pl.pallas_call(
        d_middle_kernel,
        grid_spec=pltpu.PrefetchScalarGridSpec(
            num_scalar_prefetch=1,
            grid=(1,),
            in_specs=summed(sums) + [whole(t.shape) for t in (middle, dy)] + specs,
            out_specs=(whole(dy.shape), whole(dy.shape), whole(heads)),
            scratch_shapes=scratch,
        ),
        out_shape=(
            jax.ShapeDtypeStruct(dy.shape, F32),
            jax.ShapeDtypeStruct(dy.shape, BF16),
            jax.ShapeDtypeStruct(heads, BF16),
        ),
        compiler_params=params(),
        cost_estimate=cost(2 * rows * width * TEAM * QW, 2 * width * TEAM * QW + 18 * rows * width),
        name="d_middle",
    )(member_at, *sums, middle, dy, *wo)


def mates_kernel(*refs):
    evens, odds, outs = refs[:2], refs[2:4], refs[4:]
    for j, k in enumerate((2, 4, 6)):
        r = evens[k // 4][k // 2 % 2].astype(F32) + odds[k // 4][k // 2 % 2].astype(F32)
        outs[j][...] = r.astype(BF16)


def mates_sum(evens, odds):
    _, rows, width = evens[0].shape
    steps = 2
    block = rows // steps
    return pl.pallas_call(
        mates_kernel,
        grid=(steps,),
        in_specs=[pl.BlockSpec((2, block, width), lambda i: (0, i, 0))] * 4,
        out_specs=(pl.BlockSpec((block, width), lambda i: (i, 0)),) * 3,
        out_shape=(jax.ShapeDtypeStruct((rows, width), BF16),) * 3,
        compiler_params=params(SMALL_BYTES),
        cost_estimate=cost(6 * rows * width, 36 * rows * width),
        name="mates_sum",
    )(*evens, *odds)


def summed(sums):
    even = sums[0].shape
    return [pl.BlockSpec((1, *even[1:]), lambda *_: (0, 0, 0))] * 2 + [whole(t.shape) for t in sums[2:]]


def team_total(refs):
    even, odd, *others = refs
    total = even[0].astype(F32) + odd[0].astype(F32)
    for ref in others:
        total = total + ref[...].astype(F32)
    return total


def token_kernel(e_ref, x_ref, d_ref, out_ref):
    x = x_ref[...].astype(F32)
    r = lax.rsqrt(jnp.mean(x * x, axis=-1, keepdims=True) + EPS)
    out_ref[...] = d_ref[...] + norm_back(e_ref[...].astype(F32), x * r, r)


def token_gradient(e, x, d_middle):
    rows, width = x.shape
    block = rows // 2
    return pl.pallas_call(
        token_kernel,
        grid=(2,),
        in_specs=[pl.BlockSpec((block, width), lambda i: (i, 0))] * 3,
        out_specs=pl.BlockSpec((block, width), lambda i: (i, 0)),
        out_shape=jax.ShapeDtypeStruct(x.shape, F32),
        compiler_params=params(),
        cost_estimate=cost(12 * x.size, 20 * x.size),
        name="token_gradient",
    )(e, x, d_middle)


def pack(gate_up, down):
    _, rows, twice = gate_up.shape
    ff = twice // 2
    blocks = [gate_up[..., :ff].reshape(-1, ff), gate_up[..., ff:].reshape(-1, ff)]
    return jnp.concatenate(blocks + [down[:, i : i + ff] for i in range(0, down.shape[1], ff)], axis=0)


def pack_back(gate, up, down):
    n = lax.axis_size("ctx")
    width, ff = gate.shape
    by_ctx = lambda g: jnp.transpose(g.reshape(TEAM, n, -1, ff), (1, 0, 2, 3)).reshape(n, -1, ff)
    blocks = [by_ctx(gate), by_ctx(up)]
    down = down.reshape(n, ff // n, width)
    return jnp.concatenate(blocks + [down[..., i : i + ff] for i in range(0, width, ff)], axis=1)


def down_ways(packed, wd_ref):
    n_ctx, count, ff = packed.shape
    width = wd_ref.shape[1]
    down = ff // n_ctx
    first = count - width // ff * down
    return [
        (packed.at[c, pl.ds(first + i * down, down)], wd_ref.at[pl.ds(c * down, down), pl.ds(i * ff, ff)])
        for c in range(n_ctx)
        for i in range(width // ff)
    ]


def unpack(packed, wgu_ref, wd_ref, sem):
    n_ctx, _, ff = packed.shape
    rows = wgu_ref.shape[0] // (TEAM * n_ctx)
    ways = down_ways(packed, wd_ref)
    for c in range(n_ctx):
        for part in range(2):
            for m in range(TEAM):
                out = wgu_ref.at[pl.ds((m * n_ctx + c) * rows, rows), pl.ds(part * ff, ff)]
                ways.append((packed.at[c, pl.ds((part * TEAM + m) * rows, rows)], out))
    copies = [pltpu.make_async_copy(src, dst, sem.at[i]) for i, (src, dst) in enumerate(ways)]
    for copy in copies:
        copy.start()
    for copy in copies:
        copy.wait()


def feed_kernel(*refs):
    x_refs = refs[:TEAM]
    y_ref, packed = refs[TEAM : TEAM + 2]
    even0_ref, odd0_ref, even1_ref, odd1_ref, hidden_ref, dgu_ref, xc_ref, wgu_ref, wd_ref, sem = refs[TEAM + 2 :]
    ff = wd_ref.shape[0]
    block = x_refs[0].shape[0]

    @pl.when(pl.program_id(0) == 0)
    def _():
        unpack(packed, wgu_ref, wd_ref, sem)

    for j in range(TEAM):
        xc_ref[j] = x_refs[j][...]
    x = jnp.concatenate([ref[...] for ref in x_refs], axis=0)
    y = y_ref[...].reshape(TEAM * block, y_ref.shape[2])
    gate = mm(x, wgu_ref[:, :ff])
    upper = mm(x, wgu_ref[:, ff:])
    d_hidden = mm_nt(y, wd_ref[...])
    sigma = jax.nn.sigmoid(gate)
    act = gate * sigma
    hidden = (act * upper).astype(BF16)
    d_gate = (d_hidden * upper * sigma * (1.0 + gate * (1.0 - sigma))).astype(BF16)
    dgu = jnp.concatenate([d_gate, (d_hidden * act).astype(BF16)], axis=1)
    e = mm_nt(dgu, wgu_ref[...]).astype(BF16)
    outs = (even0_ref, odd0_ref, even1_ref, odd1_ref)
    for j in range(TEAM):
        part = slice(j * block, (j + 1) * block)
        hidden_ref[j] = hidden[part]
        dgu_ref[j] = dgu[part]
        outs[j // 4 * 2 + j % 2][j // 2 % 2] = e[part]


def feed(xs, y, packed):
    rows, width = xs[0].shape
    n_ctx, packed_rows, ff = packed.shape
    steps = 4
    block = rows // steps
    widths = (ff, 2 * ff, width)
    rowed = pl.BlockSpec((block, width), lambda i: (i, 0))
    return pl.pallas_call(
        feed_kernel,
        grid=(steps,),
        in_specs=[rowed] * TEAM
        + [pl.BlockSpec((TEAM, block, width), lambda i: (0, i, 0)), pl.BlockSpec(memory_space=pl.ANY)],
        out_specs=(pl.BlockSpec((2, block, width), lambda i: (0, i, 0)),) * 4
        + tuple(pl.BlockSpec((TEAM, block, n), lambda i: (0, i, 0)) for n in widths),
        out_shape=(jax.ShapeDtypeStruct((2, rows, width), BF16),) * 4
        + tuple(jax.ShapeDtypeStruct((TEAM, rows, n), BF16) for n in widths),
        scratch_shapes=[
            pltpu.VMEM((width, 2 * ff), BF16),
            pltpu.VMEM((ff, width), BF16),
            pltpu.SemaphoreType.DMA((n_ctx * (2 * TEAM + width // ff),)),
        ],
        compiler_params=params(),
        cost_estimate=cost(2 * TEAM * rows * width * 5 * ff, 6 * width * ff + 20 * TEAM * rows * width, TEAM * rows * ff),
        name="feed",
    )(*xs, y, packed)


def fold_kernel(widths, at_ref, gain_ref, *refs):
    weights, out_ref = refs[:-1], refs[-1]
    gain = gain_ref[...]
    for m in range(TEAM):
        at = 0
        for n, ref in zip(widths, weights):
            out_ref[at_ref[m], :, at : at + n] = (ref[:, m * n : (m + 1) * n].astype(F32) * gain).astype(BF16)
            at += n


def fold(places, gain, weights):
    widths = tuple(w.shape[1] // TEAM for w in weights)
    out = (TEAM, weights[0].shape[0], sum(widths))
    return pl.pallas_call(
        functools.partial(fold_kernel, widths),
        grid_spec=pltpu.PrefetchScalarGridSpec(
            num_scalar_prefetch=1,
            grid=(1,),
            in_specs=[whole(t.shape) for t in (gain, *weights)],
            out_specs=whole(out),
        ),
        out_shape=jax.ShapeDtypeStruct(out, BF16),
        compiler_params=params(),
        cost_estimate=cost(out[0] * out[1] * out[2], 4 * out[0] * out[1] * out[2]),
        name="fold",
    )(places, gain, *weights)


def gradients_kernel(widths, at_ref, gain_ref, grad_ref, *refs):
    count = len(widths)
    weights, outs, gain_out = refs[:count], refs[count : 2 * count], refs[2 * count]
    gain = gain_ref[...]
    total = jnp.zeros(gain.shape, F32)
    for m in range(TEAM):
        at = 0
        for n, w_ref, out_ref in zip(widths, weights, outs):
            g = grad_ref[at_ref[m], :, at : at + n].astype(F32)
            here = slice(m * n, (m + 1) * n)
            total = total + jnp.sum(w_ref[:, here].astype(F32) * g, axis=1, keepdims=True)
            out_ref[:, here] = g * gain
            at += n
    gain_out[...] = jnp.broadcast_to(total, (total.shape[0], 128)).T[:1]


def gradients(places, gain, grad, weights):
    widths = tuple(w.shape[1] // TEAM for w in weights)
    outs = [w.shape for w in weights] + [(1, gain.shape[0])]
    return pl.pallas_call(
        functools.partial(gradients_kernel, widths),
        grid_spec=pltpu.PrefetchScalarGridSpec(
            num_scalar_prefetch=1,
            grid=(1,),
            in_specs=[whole(t.shape) for t in (gain, grad, *weights)],
            out_specs=tuple(whole(shape) for shape in outs),
        ),
        out_shape=tuple(jax.ShapeDtypeStruct(shape, F32) for shape in outs),
        compiler_params=params(SMALL_BYTES),
        cost_estimate=cost(4 * grad.size, 8 * grad.size),
        name="gradients",
    )(places, gain, grad, *weights)


def gathered(own, p1, p2, p4):
    half = own.shape[0] // 2
    p6 = jnp.concatenate([swap(p4[:half], 2), swap(p2[half:], 4)], axis=0)
    return [own, p1, p2, swap(p2, 1), p4, swap(p4, 1), p6, swap(p6, 1)]


def chip_mates(evens):
    pieces = []
    for even in evens:
        pieces += [even, swap(even, 1)]
    return pieces


def tie(*values):
    leaves, tree = jax.tree.flatten(values)
    return jax.tree.unflatten(tree, lax.optimization_barrier(leaves))


def mates_trade(parts):
    evens, odds = (parts[0], parts[2]), (swap(parts[1], 1), swap(parts[3], 1))
    return (evens[0], odds[0]), mates_sum(evens, odds)


def hop(sums):
    return [swap(r, bit) for r, bit in zip(sums, (2, 4, 6))]


def total_of(own, got):
    total = own[0][0].astype(F32) + own[1][0].astype(F32)
    for part in got:
        total = total + part.astype(F32)
    return total


def place_rows(seq_rows, order, half_rows):
    slots = seq_rows // half_rows
    hit = slots[:, None] == jnp.arange(order.shape[0], dtype=jnp.int32)[None, :]
    return jnp.sum(jnp.where(hit, order[None, :], 0), axis=1) * half_rows + seq_rows % half_rows


def angles(places):
    freqs = THETA ** (-(jnp.arange(HALF).astype(F32) * 2.0 / HEAD_DIM))
    return places.astype(F32)[:, None] * freqs[None, :]


def member_columns(own):
    return lax.all_to_all(own, "dp", 0, 0, tiled=True)


def any_columns(own, index):
    n_dp, n_ctx = lax.axis_size("dp"), lax.axis_size("ctx")
    gathered = lax.all_gather(own, ("dp", "ctx"), axis=0)
    mine = lax.dynamic_index_in_dim(gathered, index, 1, False)
    per = n_dp // TEAM
    mine = mine.reshape(TEAM, n_ctx, per * own.shape[1], own.shape[2])
    return jnp.transpose(mine, (1, 0, 2, 3))


def by_rows(columns):
    return jnp.transpose(columns, (1, 0, 2, 3)).reshape(-1, columns.shape[-1])


def any_rows(own):
    gathered = lax.all_gather(own, ("dp", "ctx"), axis=0, tiled=True)
    count = gathered.shape[0] // TEAM
    return lax.dynamic_slice_in_dim(gathered, (lax.axis_index("dp") % TEAM) * count, count, 0)


def column_blocks(grad):
    n_dp, n_ctx = lax.axis_size("dp"), lax.axis_size("ctx")
    rows_all, width = grad.shape
    blocks = grad.astype(BF16).reshape(TEAM, n_ctx, rows_all // (n_dp * n_ctx), width)
    return jnp.transpose(blocks, (1, 0, 2, 3))


def columns_home(part):
    return lax.all_to_all(part.astype(BF16), "dp", 0, 0, tiled=True)


def columns_out(grad, index):
    hit = (jnp.arange(TEAM) == index)[None, :, None]
    spread = jnp.where(hit, grad.astype(BF16)[:, None, :], jnp.zeros((), BF16))
    out = lax.psum_scatter(spread, ("dp", "ctx"), scatter_dimension=0, tiled=True)
    return jnp.transpose(out, (1, 0, 2))


def rows_out(grad):
    grad = grad.astype(BF16)
    if lax.axis_size("dp") == TEAM:
        return lax.psum_scatter(grad, "ctx", scatter_dimension=0, tiled=True).astype(F32)
    member = lax.axis_index("dp") % TEAM
    hit = (jnp.arange(TEAM) == member)[:, None, None]
    spread = jnp.where(hit, grad[None], jnp.zeros((), BF16)).reshape(-1, grad.shape[1])
    return lax.psum_scatter(spread, ("dp", "ctx"), scatter_dimension=0, tiled=True).astype(F32)


def across(value):
    return lax.all_to_all(value, "ctx", 0, 0, tiled=True)


def ctx_gather(own):
    return across(jnp.broadcast_to(own, (lax.axis_size("ctx"), *own.shape)))


def flat(value):
    return value.reshape(-1, value.shape[-1])


def norm_back(e, xhat, r):
    return r * (e - xhat * jnp.mean(e * xhat, axis=-1, keepdims=True))


def local(
    tokens, cotangent, gain_attn, w_query, w_key, w_value, w_out, gain_ffn, w_gate, w_up, w_down, order
):
    _, span, width = tokens.shape
    n_ctx = lax.axis_size("ctx")
    rows = w_query.shape[0]
    length = span * n_ctx
    half_rows = span // 2
    scale = HEAD_DIM**-0.5

    gain_a = gain_attn.astype(F32)[:, None]
    gain_f = gain_ffn.astype(F32)[:, None]
    mates = TEAM // n_ctx
    here = lax.axis_index("dp") % TEAM
    mate = here % mates
    ids = jnp.arange(TEAM, dtype=jnp.int32)
    place_of = lambda head: head // mates * mates + (head % mates ^ mate)
    member, head_at = here ^ ids, place_of(ids)
    member_at = place_of(member)
    head = lax.axis_index("ctx") * mates + mate
    one_team = lax.axis_size("dp") == TEAM and mates == 2

    storage = jnp.arange(length, dtype=jnp.int32)
    places = place_rows(storage, order, half_rows).astype(F32)
    lane = jnp.arange(QKV, dtype=jnp.int32)
    freq = jnp.where(lane < QW + HEAD_DIM, THETA ** (-((lane % HALF).astype(F32) * 2.0 / HEAD_DIM)), 0.0)
    size = jnp.where(lane < QW, scale, 1.0)
    turn = places[:, None] * freq[None, :]
    sine = jnp.sin(turn) * size
    first = lane % HEAD_DIM < HALF
    tables = (jnp.cos(turn) * size, jnp.where(first, -sine, 0.0), jnp.where(first, 0.0, sine))
    turn_t = angles(storage).T
    cos_t, sin_t = jnp.cos(turn_t), jnp.sin(turn_t)
    slots = jnp.sum(jnp.where(order[None, :] == jnp.arange(order.shape[0])[:, None], jnp.arange(order.shape[0]), 0), axis=1)
    slots = slots.astype(jnp.int32)

    tok, dy_own = tokens[0], cotangent[0]
    x = tok.astype(F32)
    low_x1 = (x * lax.rsqrt(jnp.mean(x * x, axis=-1, keepdims=True) + EPS)).astype(BF16)
    folded_qkv = fold(head_at if one_team else ids, gain_a, (w_query, w_key, w_value))
    folded_gu = fold(ids, gain_f, (w_gate, w_up))
    x1 = [lax.all_gather(low_x1, "ctx", axis=0)]
    if one_team:
        mine_gu = lax.all_to_all(folded_gu, "dp", 0, 0, tiled=True)
        blocks = folded_qkv.reshape(n_ctx, mates, rows, QKV)
        blocks = jnp.stack([blocks[:, 0], swap(blocks[:, 1], 1)], axis=1)
        blocks, mine_gu = tie(blocks, mine_gu)
        piece = across(blocks)
        piece, own_wo = tie(piece, w_out)
        pieces = [piece, swap(piece, 2), swap(piece, 4), swap(piece, 6)]
        wo = ctx_gather(own_wo).reshape(QW, width)
        pieces, wo = tie(pieces, wo)
        wqkv = rows_of(member, pieces)
        packed = lax.all_gather(pack(mine_gu, w_down), "ctx", axis=0)
    else:
        wqkv = by_rows(any_columns(folded_qkv, head))
        wgu = by_rows(any_columns(folded_gu, here)).reshape(TEAM, width // TEAM, -1)
        wo, wd = any_rows(w_out), any_rows(w_down)
        packed = pack(wgu, wd)[None]

    x1[0], wqkv, tables, dy_own = tie(x1[0], wqkv, tables, dy_own)
    wo_even = [wo, swap(wo, 2), swap(wo, 4), swap(wo, 6)]
    dy_even = [dy_own, swap(dy_own, 2), swap(dy_own, 4), swap(dy_own, 6)]
    if mates == 2:
        x1.append(swap(x1[0], 1))
    qkv = qkv_of(x1, wqkv, tables)
    other, lse_other = attend(slots, order, qkv, mates - 1)
    heads, lse = (other, lse_other) if mates == 1 else attend(slots, order, qkv, 0)
    heads = heads[:, None] if mates == 1 else jnp.stack([heads, swap(other, 1)], axis=1)
    heads, wo_even = tie(heads, wo_even)
    wo_all = chip_mates(wo_even)
    traded = across(heads)
    traded, wo_all, dy_even = tie(traded, wo_all, dy_even)

    traded = traded.reshape(TEAM, *traded.shape[2:])
    middle, xhat2 = middle_of(member_at, tok, traded, wo_all)
    p2, p4, p1 = swap(xhat2, 2), swap(xhat2, 4), swap(xhat2, 1)
    dy_all = stack(ids, chip_mates(dy_even))
    p2, p4, p1, dy_all = tie(p2, p4, p1, dy_all)
    x2 = gathered(xhat2, p1, p2, p4)
    *parts, hidden, dgu, x2_all = feed(x2, dy_all, packed)
    dgu = flat(dgu)
    odd0, odd1 = swap(parts[1], 1), swap(parts[3], 1)
    g_gate = mm_tn(flat(x2_all), dgu[:, : dgu.shape[1] // 2]).astype(BF16)
    odd0, odd1, g_gate = tie(odd0, odd1, g_gate)

    got = mates_sum((parts[0], parts[2]), (odd0, odd1))
    *got, x2_all, dy_all, hidden = tie(*got, x2_all, dy_all, hidden)
    got = hop(got)
    g_up = mm_tn(flat(x2_all), dgu[:, dgu.shape[1] // 2 :]).astype(BF16)
    g_down = mm_tn(flat(hidden), flat(dy_all)).astype(BF16)
    mixed_parts = parts_of(hidden, packed, width)
    if one_team:
        g_ff = pack_back(g_gate, g_up, g_down)
        got, packed_ff, mixed_parts = tie(got, g_ff, mixed_parts)
        g_ff = lax.psum_scatter(packed_ff.reshape(-1, g_ff.shape[-1]), "ctx", scatter_dimension=0, tiled=True)
    sums = (parts[0], odd0, *got)
    d_middle, d_low, d_heads = d_middle_of(member_at, sums, middle, dy_own, wo_all)

    hidden, d_low, d_heads = tie(hidden, d_low, d_heads)
    d_heads = across(d_heads.reshape(n_ctx, mates, *d_heads.shape[1:]))
    mixed_own, mixed_sums = mates_trade(mixed_parts)
    mixed_got = hop(mixed_sums)
    out_parts = grad_out_parts(member_at, traded, d_low)
    d_heads, mixed_got, out_parts = tie(d_heads, mixed_got, out_parts)

    d_other = d_heads[:, 0] if mates == 1 else swap(d_heads[:, 1], 1)
    d_qkv, more = [attend_back(slots, qkv, mates - 1, d_other, lse_other, cos_t, sin_t)], []
    if mates == 2:
        more = [swap(input_all(d_qkv[0], wqkv), 1)]
        d_qkv = [attend_back(slots, qkv, 0, d_heads[:, 0], lse, cos_t, sin_t), *d_qkv]
    d_qkv, more = tie(d_qkv, more)
    e1 = input_own(d_qkv[0], wqkv, more)
    e1, d_qkv, mixed_got, out_parts = tie(e1, d_qkv, mixed_got, out_parts)
    e1 = lax.psum_scatter(e1, "ctx", scatter_dimension=0)

    out_own, out_sums = mates_trade(out_parts)
    mixed = (middle + total_of(mixed_own, mixed_got)).astype(BF16)[None]
    g_qkv = mm_tn(flat(x1[0]), flat(d_qkv[0]))
    for a, b in zip(x1[1:], d_qkv[1:]):
        g_qkv = g_qkv + mm_tn(flat(a), flat(b))
    if one_team:
        ff = g_ff.shape[1]
        cut = TEAM * rows
        g_gu = jnp.concatenate([g_ff[:cut].reshape(TEAM, rows, ff), g_ff[cut : 2 * cut].reshape(TEAM, rows, ff)], axis=2)
        g_gu = lax.all_to_all(g_gu, "dp", 0, 0, tiled=True)
        ways = pieces_of(member, g_qkv)
        ways, out_sums, g_gu = tie(ways, out_sums, g_gu)
        home = ways[0].astype(F32)
        for bit, way in zip((2, 4, 6), ways[1:]):
            home = home + swap(way, bit).astype(F32)
        home = home.astype(BF16).reshape(mates, n_ctx, rows, QKV)
        home, out_sums = tie(jnp.stack([home[0], swap(home[1], 1)], axis=1), out_sums)
        home = across(home).reshape(TEAM, rows, QKV)
        g_out = total_of(out_own, hop(out_sums)).astype(BF16)
        home, g_out = tie(home, g_out)
        grad_out = jnp.sum(across(g_out.reshape(n_ctx, -1, width)).astype(F32), axis=0)
        down = g_ff[2 * cut :].reshape(width // ff, -1, ff)
        grad_down = jnp.concatenate([down[i] for i in range(width // ff)], axis=1).astype(F32)
    else:
        home = columns_out(g_qkv, head)
        g_gu = columns_out(jnp.concatenate([g_gate, g_up], axis=1), here)
        grad_down, grad_out = rows_out(g_down), rows_out(total_of(out_own, hop(out_sums)))
    *grads_qkv, gain_a_grad = gradients(head_at if one_team else ids, gain_a, home, (w_query, w_key, w_value))
    *grads_gu, gain_f_grad = gradients(ids, gain_f, g_gu, (w_gate, w_up))
    token_grad = token_gradient(e1, tok, d_middle)[None]
    return (
        mixed,
        token_grad,
        gain_a_grad[0],
        *grads_qkv,
        grad_out,
        gain_f_grad[0],
        *grads_gu,
        grad_down,
    )


def solution(mesh):
    act = P("dp", "ctx", None)
    vec = P(("dp", "ctx"))
    mat = P(("dp", "ctx"), None)
    return jax.shard_map(
        local,
        mesh=mesh,
        in_specs=(act, act, vec, mat, mat, mat, mat, vec, mat, mat, mat, P()),
        out_specs=(act, act, vec, mat, mat, mat, mat, vec, mat, mat, mat),
        check_vma=False,
    )
```

```python
import functools

import jax
import jax.numpy as jnp
from jax import lax
from jax.experimental import pallas as pl
from jax.experimental.pallas import tpu as pltpu
from jax.sharding import PartitionSpec as P

HEADS = 16
KV_HEADS = 8
HEAD_DIM = 96
GROUPS = HEADS // KV_HEADS
HALF = HEAD_DIM // 2
QW = GROUPS * HEAD_DIM
QKV = QW + 2 * HEAD_DIM

EPS = 1e-05
THETA = 100000.0
F32 = jnp.float32
BF16 = jnp.bfloat16
CHUNKS = 4
VMEM_BYTES = 56 * 2**20
SMALL_BYTES = 20 * 2**20

TEAM = KV_HEADS
PAIRS = TEAM // 2


def dot(a, b, dims):
    return lax.dot_general(a, b, (dims, ((), ())), preferred_element_type=F32)


def mm(a, b):
    return dot(a, b, ((1,), (0,)))


def mm_nt(a, b):
    return dot(a, b, ((1,), (1,)))


def mm_tn(a, b):
    return dot(a, b, ((0,), (0,)))


def swap(value, bit):
    n = lax.axis_size("dp")
    return lax.ppermute(value, "dp", [(i, i ^ bit) for i in range(n)])


def after(value, *others):
    return lax.optimization_barrier((value, *others))[0]


def params(limit=VMEM_BYTES):
    return pltpu.CompilerParams(vmem_limit_bytes=limit)


def cost(flops, nbytes, exps=0):
    return pl.CostEstimate(flops=int(flops), bytes_accessed=int(nbytes), transcendentals=int(exps))


def whole(shape):
    return pl.BlockSpec(shape, lambda *_: (0,) * len(shape))


def join(even_ref, odd_ref):
    return jnp.concatenate([even_ref[...], odd_ref[...]], axis=0)


def qkv_kernel(seqs, *refs):
    x_refs = refs[:seqs]
    w_ref, c_ref, s1_ref, s2_ref, out_ref = refs[seqs:]
    block = c_ref.shape[0]
    y = mm(jnp.concatenate([ref[0] for ref in x_refs], axis=0), w_ref[...])
    ahead = pltpu.roll(y, QKV - HALF, 1)
    behind = pltpu.roll(y, HALF, 1)
    for k in range(seqs):
        here = slice(k * block, (k + 1) * block)
        turned = y[here] * c_ref[...] + ahead[here] * s1_ref[...] + behind[here] * s2_ref[...]
        out_ref[k, 0] = turned.astype(BF16)


def qkv_of(xs, span, w, tables):
    n_ctx, _, width = xs[0].shape
    seqs = len(xs)
    return pl.pallas_call(
        functools.partial(qkv_kernel, seqs),
        grid=(n_ctx,),
        in_specs=[pl.BlockSpec((1, span, width), lambda i: (i, 0, 0))] * seqs
        + [whole(w.shape)]
        + [pl.BlockSpec((span, QKV), lambda i: (i, 0))] * 3,
        out_specs=pl.BlockSpec((seqs, 1, span, QKV), lambda i: (0, i, 0, 0)),
        out_shape=jax.ShapeDtypeStruct((seqs, n_ctx, span, QKV), BF16),
        compiler_params=params(),
        cost_estimate=cost(2 * seqs * n_ctx * span * width * QKV, 2 * seqs * n_ctx * span * width + 2 * width * QKV),
        name="qkv",
    )(*xs, w, *tables)


def rows_kernel(member_ref, *refs):
    pieces, out_ref = refs[:-1], refs[-1]
    n_ctx, _, rows, _ = pieces[0].shape
    for p, piece in enumerate(pieces):
        for c in range(n_ctx):
            for j in range(2):
                at = pl.multiple_of((member_ref[2 * p + j] * n_ctx + c) * rows, 16)
                out_ref[pl.ds(at, rows), :] = piece[c, j]


def rows_of(member, pieces):
    n_ctx, two, rows, width = pieces[0].shape
    out = (len(pieces) * n_ctx * two * rows, width)
    return pl.pallas_call(
        rows_kernel,
        grid_spec=pltpu.PrefetchScalarGridSpec(
            num_scalar_prefetch=1,
            grid=(1,),
            in_specs=[whole(t.shape) for t in pieces],
            out_specs=whole(out),
        ),
        out_shape=jax.ShapeDtypeStruct(out, BF16),
        compiler_params=params(SMALL_BYTES),
        cost_estimate=cost(0, 4 * out[0] * out[1]),
        name="rows",
    )(member, *pieces)


def pieces_kernel(member_ref, grad_ref, *out_refs):
    for p, out_ref in enumerate(out_refs):
        for j in range(2):
            out_ref[j] = grad_ref[member_ref[2 * p + j]].astype(BF16)


def pieces_of(member, grad):
    rows, width = grad.shape[0] // TEAM, grad.shape[1]
    return pl.pallas_call(
        pieces_kernel,
        grid_spec=pltpu.PrefetchScalarGridSpec(
            num_scalar_prefetch=1,
            grid=(1,),
            in_specs=[whole((TEAM, rows, width))],
            out_specs=(whole((2, rows, width)),) * PAIRS,
        ),
        out_shape=(jax.ShapeDtypeStruct((2, rows, width), BF16),) * PAIRS,
        compiler_params=params(SMALL_BYTES),
        cost_estimate=cost(0, 6 * grad.size),
        name="pieces",
    )(member, grad.reshape(TEAM, rows, width))


def stack_kernel(order_ref, *refs):
    for k, ref in enumerate(refs[:-1]):
        refs[-1][order_ref[k]] = ref[...]


def stack(order, xs):
    rows, width = xs[0].shape
    steps = 4
    block = rows // steps
    return pl.pallas_call(
        stack_kernel,
        grid_spec=pltpu.PrefetchScalarGridSpec(
            num_scalar_prefetch=1,
            grid=(steps,),
            in_specs=[pl.BlockSpec((block, width), lambda i, m: (i, 0))] * len(xs),
            out_specs=pl.BlockSpec((len(xs), block, width), lambda i, m: (0, i, 0)),
        ),
        out_shape=jax.ShapeDtypeStruct((len(xs), rows, width), BF16),
        compiler_params=params(),
        cost_estimate=cost(0, 4 * len(xs) * rows * width),
        name="stack",
    )(order, *xs)


def in_order(slots_ref, ref, scratch, half):
    for b in range(slots_ref.shape[0]):
        slot = slots_ref[b]
        at = pl.multiple_of((slot % 2) * half, half)
        scratch[pl.ds(b * half, half), :] = ref[slot // 2, pl.ds(at, half), :]


def heads_in_order(slots_ref, ref, scratch, half):
    for b in range(slots_ref.shape[0]):
        slot = slots_ref[b]
        first, second = ref[slot // 2, 0, :, :QW], ref[slot // 2, 0, :, QW:]
        scratch[pl.ds(b * half, half), :] = jnp.where(slot % 2 == 0, first, second)


def heads_out_of_order(order_ref, ref, scratch, half):
    for c in range(ref.shape[0]):
        for j in range(2):
            at = pl.multiple_of(order_ref[2 * c + j] * half, half)
            ref[c, 0, :, j * QW : (j + 1) * QW] = scratch[pl.ds(at, half), :]


def out_of_order(slots_ref, ref, first, value, half):
    for b in range(value.shape[0] // half):
        slot = slots_ref[first // half + b]
        at = pl.multiple_of((slot % 2) * half, half)
        ref[slot // 2, pl.ds(at, half), :] = value[b * half : (b + 1) * half]


def flip(value):
    return value.astype(F32).T


def stacked_heads(ref, rows):
    return jnp.concatenate([ref[rows, g * HEAD_DIM : (g + 1) * HEAD_DIM] for g in range(GROUPS)], axis=0)


def causal(size):
    key = lax.broadcasted_iota(jnp.int32, (size, GROUPS * size), 0)
    query = lax.broadcasted_iota(jnp.int32, (size, GROUPS * size), 1) % size
    return key <= query


def attend_kernel(slots_ref, order_ref, qkv_ref, *refs):
    more, (out_ref, lse_ref, scratch, o_scr) = refs[:-4], refs[-4:]
    half = qkv_ref.shape[2] // 2
    size = scratch.shape[0] // CHUNKS
    in_order(slots_ref, qkv_ref.at[0], scratch, half)
    v_t = flip(scratch[:, QW + HEAD_DIM :]).astype(BF16)
    allowed = causal(size)
    for i in range(CHUNKS):
        lo, hi = i * size, (i + 1) * size
        q = stacked_heads(scratch, slice(lo, hi))
        k_near = scratch[lo:hi, QW : QW + HEAD_DIM]
        near = jnp.where(allowed, mm_nt(k_near, q), -1e30)
        top = jnp.max(near, axis=0, keepdims=True)
        if i > 0:
            far = mm_nt(scratch[:lo, QW : QW + HEAD_DIM], q)
            top = jnp.maximum(top, jnp.max(far, axis=0, keepdims=True))
        near = jnp.exp(near - top)
        total = jnp.sum(near, axis=0, keepdims=True)
        acc = mm(v_t[:, lo:hi], near.astype(BF16))
        if i > 0:
            far = jnp.exp(far - top)
            total = total + jnp.sum(far, axis=0, keepdims=True)
            acc = acc + mm(v_t[:, :lo], far.astype(BF16))
        lse_ref[pl.ds(i, 1), :] = top + jnp.log(total)
        o = (acc / total).T.astype(BF16)
        for g in range(GROUPS):
            o_scr[lo:hi, g * HEAD_DIM : (g + 1) * HEAD_DIM] = o[g * size : (g + 1) * size]
    heads_out_of_order(order_ref, out_ref, o_scr, half)
    for ref in more:
        out_ref[:, 1] = ref[:, 0]


def attend_back_kernel(slots_ref, qkv_ref, do_ref, lse_ref, cos_ref, sin_ref, out_ref, scratch, do_scr, dk_scr, dv_scr):
    half = qkv_ref.shape[2] // 2
    length = scratch.shape[0]
    size = length // CHUNKS
    scale = HEAD_DIM**-0.5
    in_order(slots_ref, qkv_ref.at[0], scratch, half)
    heads_in_order(slots_ref, do_ref, do_scr, half)
    k_t = flip(scratch[:, QW : QW + HEAD_DIM]).astype(BF16)
    allowed = causal(size)
    dk_scr[...] = jnp.zeros_like(dk_scr)
    dv_scr[...] = jnp.zeros_like(dv_scr)
    for i in range(CHUNKS):
        lo, hi = i * size, (i + 1) * size
        q = stacked_heads(scratch, slice(lo, hi))
        do = stacked_heads(do_scr, slice(lo, hi))
        lse = lse_ref[pl.ds(i, 1), :]
        spans = [(lo, hi)] + ([(0, lo)] if i > 0 else [])
        probs, prods = [], []
        delta = 0.0
        for at, (a, b) in enumerate(spans):
            p = jnp.exp(mm_nt(scratch[a:b, QW : QW + HEAD_DIM], q) - lse)
            if at == 0:
                p = jnp.where(allowed, p, 0.0)
            prod = p * mm_nt(scratch[a:b, QW + HEAD_DIM :], do)
            delta = delta + jnp.sum(prod, axis=0, keepdims=True)
            probs.append(p)
            prods.append(prod)
        dq_t = 0.0
        for (a, b), p, prod in zip(spans, probs, prods):
            ds = (prod - p * delta).astype(BF16)
            dk_scr[a:b, :] += mm(ds, q)
            dv_scr[a:b, :] += mm(p.astype(BF16), do)
            dq_t = dq_t + mm(k_t[:, a:b], ds)
        c = jnp.concatenate([cos_ref[:, lo:hi]] * GROUPS, axis=1) * scale
        s = jnp.concatenate([sin_ref[:, lo:hi]] * GROUPS, axis=1) * scale
        first, second = dq_t[:HALF], dq_t[HALF:]
        dq = jnp.concatenate([first * c + second * s, second * c - first * s], axis=0).T
        for g in range(GROUPS):
            do_scr[lo:hi, g * HEAD_DIM : (g + 1) * HEAD_DIM] = dq[g * size : (g + 1) * size].astype(BF16)
    for i in range(CHUNKS):
        lo, hi = i * size, (i + 1) * size
        dk_t = dk_scr[lo:hi, :].T
        first, second = dk_t[:HALF], dk_t[HALF:]
        c, s = cos_ref[:, lo:hi], sin_ref[:, lo:hi]
        dk = jnp.concatenate([first * c + second * s, second * c - first * s], axis=0).T
        value = jnp.concatenate([do_scr[lo:hi, :], dk.astype(BF16), dv_scr[lo:hi, :].astype(BF16)], axis=1)
        out_of_order(slots_ref, out_ref, lo, value, half)


def attend(slots, order, qkv, seq, more):
    _, n_ctx, span, _ = qkv.shape
    length = n_ctx * span
    heads = (n_ctx, 1 + len(more), span // 2, 2 * QW)
    lse = (CHUNKS, GROUPS * length // CHUNKS)
    work = GROUPS * length * length
    return pl.pallas_call(
        attend_kernel,
        grid_spec=pltpu.PrefetchScalarGridSpec(
            num_scalar_prefetch=2,
            grid=(1,),
            in_specs=[pl.BlockSpec((1, n_ctx, span, QKV), lambda *_: (seq, 0, 0, 0))] + [whole(t.shape) for t in more],
            out_specs=(whole(heads), whole(lse)),
            scratch_shapes=[pltpu.VMEM((length, QKV), BF16), pltpu.VMEM((length, QW), BF16)],
        ),
        out_shape=(jax.ShapeDtypeStruct(heads, BF16), jax.ShapeDtypeStruct(lse, F32)),
        compiler_params=params(),
        cost_estimate=cost(work * 2 * HEAD_DIM * 3, 2 * length * (QKV + QW), work // 2),
        name="attend",
    )(slots, order, qkv, *more)


def attend_back(slots, qkv, seq, d_heads, lse, cos_t, sin_t):
    _, n_ctx, span, _ = qkv.shape
    length = n_ctx * span
    work = GROUPS * length * length
    return pl.pallas_call(
        attend_back_kernel,
        grid_spec=pltpu.PrefetchScalarGridSpec(
            num_scalar_prefetch=1,
            grid=(1,),
            in_specs=[
                pl.BlockSpec((1, n_ctx, span, QKV), lambda *_: (seq, 0, 0, 0)),
                whole((n_ctx, 1, *d_heads.shape[2:])),
            ]
            + [whole(t.shape) for t in (lse, cos_t, sin_t)],
            out_specs=whole((n_ctx, span, QKV)),
            scratch_shapes=[
                pltpu.VMEM((length, QKV), BF16),
                pltpu.VMEM((length, QW), BF16),
                pltpu.VMEM((length, HEAD_DIM), F32),
                pltpu.VMEM((length, HEAD_DIM), F32),
            ],
        ),
        out_shape=jax.ShapeDtypeStruct((n_ctx, span, QKV), BF16),
        compiler_params=params(),
        cost_estimate=cost(work * 2 * HEAD_DIM * 8, 4 * length * QKV, work // 2),
        name="attend_back",
    )(slots, qkv, d_heads, lse, cos_t, sin_t)


def parts_kernel(a_ref, packed, *refs):
    out_refs, (wd_ref, sem) = refs[:4], refs[4:]

    @pl.when(pl.program_id(0) == 0)
    def _():
        copies = [pltpu.make_async_copy(src, dst, sem.at[i]) for i, (src, dst) in enumerate(down_ways(packed, wd_ref))]
        for copy in copies:
            copy.start()
        for copy in copies:
            copy.wait()

    block = a_ref.shape[1]
    y = mm(jnp.concatenate([a_ref[k] for k in range(TEAM)], axis=0), wd_ref[...]).astype(BF16)
    for k in range(TEAM):
        out_refs[k // 4 * 2 + k % 2][k // 2 % 2] = y[k * block : (k + 1) * block]


def parts_of(a, packed, width):
    _, rows, depth = a.shape
    steps = 4
    block = rows // steps
    return pl.pallas_call(
        parts_kernel,
        grid=(steps,),
        in_specs=[pl.BlockSpec((TEAM, block, depth), lambda i: (0, i, 0)), pl.BlockSpec(memory_space=pl.ANY)],
        out_specs=(pl.BlockSpec((2, block, width), lambda i: (0, i, 0)),) * 4,
        out_shape=(jax.ShapeDtypeStruct((2, rows, width), BF16),) * 4,
        scratch_shapes=[
            pltpu.VMEM((depth, width), BF16),
            pltpu.SemaphoreType.DMA((packed.shape[0] * (width // depth),)),
        ],
        compiler_params=params(SMALL_BYTES),
        cost_estimate=cost(2 * TEAM * rows * depth * width, 2 * TEAM * rows * (width + depth) + 2 * depth * width),
        name="parts",
    )(a, packed)


def input_own_kernel(a_ref, w_ref, *refs):
    y = mm_nt(a_ref[0], w_ref[...])
    for ref in refs[:-1]:
        y = y + ref[0].astype(F32)
    refs[-1][0] = y.astype(BF16)


def input_own(a, w, more):
    n_ctx, span, depth = a.shape
    width = w.shape[0]
    blocked = lambda n: pl.BlockSpec((1, span, n), lambda i: (i, 0, 0))
    return pl.pallas_call(
        input_own_kernel,
        grid=(n_ctx,),
        in_specs=[blocked(depth), whole(w.shape)] + [blocked(width)] * len(more),
        out_specs=blocked(width),
        out_shape=jax.ShapeDtypeStruct((n_ctx, span, width), BF16),
        compiler_params=params(),
        cost_estimate=cost(2 * n_ctx * span * depth * width, 4 * n_ctx * span * (width + depth) + 2 * depth * width),
        name="input_own",
    )(a, w, *more)


def input_all_kernel(a_ref, w_ref, out_ref):
    out_ref[0] = mm_nt(a_ref[0], w_ref[...]).astype(BF16)


def input_all(a, w):
    n_ctx, span, depth = a.shape
    width = w.shape[0]
    blocked = lambda n: pl.BlockSpec((1, span, n), lambda i: (i, 0, 0))
    return pl.pallas_call(
        input_all_kernel,
        grid=(n_ctx,),
        in_specs=[blocked(depth), whole(w.shape)],
        out_specs=blocked(width),
        out_shape=jax.ShapeDtypeStruct((n_ctx, span, width), BF16),
        compiler_params=params(),
        cost_estimate=cost(2 * n_ctx * span * depth * width, 4 * n_ctx * span * (width + depth) + 2 * depth * width),
        name="input_all",
    )(a, w)


def grad_out_kernel(at_ref, heads_ref, dm_ref, *out_refs):
    dm = dm_ref[...]
    for k in range(TEAM):
        y = mm_tn(unfold(heads_ref[at_ref[k]]), dm)
        out_refs[k // 4 * 2 + k % 2][k // 2 % 2] = y.astype(BF16)


def grad_out_parts(member_at, heads, dm):
    rows, width = dm.shape
    return pl.pallas_call(
        grad_out_kernel,
        grid_spec=pltpu.PrefetchScalarGridSpec(
            num_scalar_prefetch=1,
            grid=(1,),
            in_specs=[whole(t.shape) for t in (heads, dm)],
            out_specs=(whole((2, QW, width)),) * 4,
        ),
        out_shape=(jax.ShapeDtypeStruct((2, QW, width), BF16),) * 4,
        compiler_params=params(),
        cost_estimate=cost(2 * TEAM * rows * QW * width, 2 * TEAM * QW * width),
        name="grad_out",
    )(member_at, heads, dm)


def unfold(block):
    return jnp.concatenate([block[:, :QW], block[:, QW:]], axis=0)


def fetch(any_refs, ref, sem):
    copies = [pltpu.make_async_copy(a, ref.at[k], sem.at[k]) for k, a in enumerate(any_refs)]
    for copy in copies:
        copy.start()
    return copies


def fetched(arrays):
    specs = [pl.BlockSpec(memory_space=pl.ANY)] * len(arrays)
    scratch = [pltpu.VMEM((len(arrays), *arrays[0].shape), BF16), pltpu.SemaphoreType.DMA((len(arrays),))]
    return specs, scratch


def middle_kernel(at_ref, heads_ref, x_ref, *refs):
    wo_any, (middle_ref, top_ref, low_ref, wo_ref, sem) = refs[:TEAM], refs[TEAM:]
    copies = fetch(wo_any, wo_ref, sem)
    heads = jnp.concatenate([unfold(heads_ref[at_ref[k]]) for k in range(TEAM)], axis=1)
    for copy in copies:
        copy.wait()
    acc = x_ref[...].astype(F32) + mm(heads, wo_ref[...].reshape(heads.shape[1], -1))
    middle_ref[...] = acc
    r = lax.rsqrt(jnp.mean(acc * acc, axis=-1, keepdims=True) + EPS)
    xhat = (acc * r).astype(BF16)
    half = top_ref.shape[0]
    top_ref[...] = xhat[:half]
    low_ref[...] = xhat[half:]


def middle_of(member_at, x, heads, wo):
    rows, width = x.shape
    specs, scratch = fetched(wo)
    return pl.pallas_call(
        middle_kernel,
        grid_spec=pltpu.PrefetchScalarGridSpec(
            num_scalar_prefetch=1,
            grid=(1,),
            in_specs=[whole(t.shape) for t in (heads, x)] + specs,
            out_specs=(whole(x.shape),) + (whole((rows // 2, width)),) * 2,
            scratch_shapes=scratch,
        ),
        out_shape=(jax.ShapeDtypeStruct(x.shape, F32),) + (jax.ShapeDtypeStruct((rows // 2, width), BF16),) * 2,
        compiler_params=params(),
        cost_estimate=cost(2 * rows * width * TEAM * QW, 2 * width * TEAM * QW + 12 * rows * width),
        name="middle",
    )(member_at, heads, x, *wo)


def d_middle_kernel(at_ref, *refs):
    middle_ref, dy_ref = refs[10:12]
    wo_any, (d_ref, low_ref, out_ref, wo_ref, sem) = refs[12 : 12 + TEAM], refs[12 + TEAM :]
    copies = fetch(wo_any, wo_ref, sem)
    middle = middle_ref[...]
    half = middle.shape[0] // 2
    r = lax.rsqrt(jnp.mean(middle * middle, axis=-1, keepdims=True) + EPS)
    d = dy_ref[...].astype(F32) + norm_back(team_total(refs[:10]), middle * r, r)
    d_ref[...] = d
    low = d.astype(BF16)
    low_ref[...] = low
    for copy in copies:
        copy.wait()
    y = mm_nt(low, wo_ref[...].reshape(TEAM * QW, -1)).astype(BF16)
    for k in range(TEAM):
        part = slice(k * QW, (k + 1) * QW)
        out_ref[at_ref[k], :, :QW] = y[:half, part]
        out_ref[at_ref[k], :, QW:] = y[half:, part]


def d_middle_of(member_at, sums, middle, dy, wo):
    rows, width = dy.shape
    heads = (TEAM, rows // 2, 2 * QW)
    specs, scratch = fetched(wo)
    return pl.pallas_call(
        d_middle_kernel,
        grid_spec=pltpu.PrefetchScalarGridSpec(
            num_scalar_prefetch=1,
            grid=(1,),
            in_specs=summed(sums) + [whole(t.shape) for t in (middle, dy)] + specs,
            out_specs=(whole(dy.shape), whole(dy.shape), whole(heads)),
            scratch_shapes=scratch,
        ),
        out_shape=(
            jax.ShapeDtypeStruct(dy.shape, F32),
            jax.ShapeDtypeStruct(dy.shape, BF16),
            jax.ShapeDtypeStruct(heads, BF16),
        ),
        compiler_params=params(),
        cost_estimate=cost(2 * rows * width * TEAM * QW, 2 * width * TEAM * QW + 18 * rows * width),
        name="d_middle",
    )(member_at, *sums, middle, dy, *wo)


def mates_kernel(*refs):
    evens, odds, outs = refs[:2], refs[2:4], refs[4:]
    for j, k in enumerate((2, 4, 6)):
        r = evens[k // 4][k // 2 % 2].astype(F32) + odds[k // 4][k // 2 % 2].astype(F32)
        outs[j][...] = r.astype(BF16)


def mates_sum(evens, odds):
    _, rows, width = evens[0].shape
    steps = 2
    block = rows // steps
    return pl.pallas_call(
        mates_kernel,
        grid=(steps,),
        in_specs=[pl.BlockSpec((2, block, width), lambda i: (0, i, 0))] * 4,
        out_specs=(pl.BlockSpec((block, width), lambda i: (i, 0)),) * 3,
        out_shape=(jax.ShapeDtypeStruct((rows, width), BF16),) * 3,
        compiler_params=params(SMALL_BYTES),
        cost_estimate=cost(6 * rows * width, 36 * rows * width),
        name="mates_sum",
    )(*evens, *odds)


def summed(sums):
    first = lambda t: pl.BlockSpec((1, *t.shape[1:]), lambda *_: (0, 0, 0))
    return [first(t) if t.ndim == 3 else whole(t.shape) for t in sums]


def team_total(refs):
    halves = []
    for even, odd, *others in (refs[:5], refs[5:]):
        total = even[0].astype(F32) + odd[0].astype(F32)
        for ref in others:
            total = total + ref[...].astype(F32)
        halves.append(total)
    return jnp.concatenate(halves, axis=0)


def token_kernel(e_ref, x_ref, d_ref, out_ref):
    x = x_ref[...].astype(F32)
    r = lax.rsqrt(jnp.mean(x * x, axis=-1, keepdims=True) + EPS)
    out_ref[...] = d_ref[...] + norm_back(e_ref[...].astype(F32), x * r, r)


def token_gradient(e, x, d_middle):
    rows, width = x.shape
    block = rows // 2
    return pl.pallas_call(
        token_kernel,
        grid=(2,),
        in_specs=[pl.BlockSpec((block, width), lambda i: (i, 0))] * 3,
        out_specs=pl.BlockSpec((block, width), lambda i: (i, 0)),
        out_shape=jax.ShapeDtypeStruct(x.shape, F32),
        compiler_params=params(),
        cost_estimate=cost(12 * x.size, 20 * x.size),
        name="token_gradient",
    )(e, x, d_middle)


def pack(gate_up, down):
    _, rows, twice = gate_up.shape
    ff = twice // 2
    blocks = [gate_up[..., :ff].reshape(-1, ff), gate_up[..., ff:].reshape(-1, ff)]
    return jnp.concatenate(blocks + [down[:, i : i + ff] for i in range(0, down.shape[1], ff)], axis=0)


def pack_back(gate, up, down):
    n = lax.axis_size("ctx")
    width, ff = gate.shape
    by_ctx = lambda g: jnp.transpose(g.reshape(TEAM, n, -1, ff), (1, 0, 2, 3)).reshape(n, -1, ff)
    blocks = [by_ctx(gate), by_ctx(up)]
    down = down.reshape(n, ff // n, width)
    return jnp.concatenate(blocks + [down[..., i : i + ff] for i in range(0, width, ff)], axis=1)


def down_ways(packed, wd_ref):
    n_ctx, count, ff = packed.shape
    width = wd_ref.shape[1]
    down = ff // n_ctx
    first = count - width // ff * down
    return [
        (packed.at[c, pl.ds(first + i * down, down)], wd_ref.at[pl.ds(c * down, down), pl.ds(i * ff, ff)])
        for c in range(n_ctx)
        for i in range(width // ff)
    ]


def unpack(packed, wgu_ref, wd_ref, sem):
    n_ctx, _, ff = packed.shape
    rows = wgu_ref.shape[0] // (TEAM * n_ctx)
    ways = []
    for part in range(2):
        for c in range(n_ctx):
            for m in range(TEAM):
                out = wgu_ref.at[pl.ds((m * n_ctx + c) * rows, rows), pl.ds(part * ff, ff)]
                ways.append((packed.at[c, pl.ds((part * TEAM + m) * rows, rows)], out))
    ways += down_ways(packed, wd_ref)
    copies = [pltpu.make_async_copy(src, dst, sem.at[i]) for i, (src, dst) in enumerate(ways)]
    for copy in copies:
        copy.start()
    return copies


def feed_kernel(*refs):
    x_refs = refs[:TEAM]
    y_ref, packed = refs[TEAM : TEAM + 2]
    even0_ref, odd0_ref, even1_ref, odd1_ref, hidden_ref, dgu_ref, xc_ref, wgu_ref, wd_ref, sem = refs[-10:]
    ff = wd_ref.shape[0]
    block = x_refs[0].shape[0]

    @pl.when(pl.program_id(0) == 0)
    def _():
        for copy in unpack(packed, wgu_ref, wd_ref, sem):
            copy.wait()

    for j in range(TEAM):
        xc_ref[j] = x_refs[j][...]
    x = jnp.concatenate([ref[...] for ref in x_refs], axis=0)
    y = y_ref[...].reshape(TEAM * block, y_ref.shape[2])
    gate = mm(x, wgu_ref[:, :ff])
    upper = mm(x, wgu_ref[:, ff:])
    d_hidden = mm_nt(y, wd_ref[...])
    sigma = jax.nn.sigmoid(gate)
    act = gate * sigma
    hidden = (act * upper).astype(BF16)
    d_gate = (d_hidden * upper * sigma * (1.0 + gate * (1.0 - sigma))).astype(BF16)
    dgu = jnp.concatenate([d_gate, (d_hidden * act).astype(BF16)], axis=1)
    e = mm_nt(dgu, wgu_ref[...]).astype(BF16)
    outs = (even0_ref, odd0_ref, even1_ref, odd1_ref)
    for j in range(TEAM):
        part = slice(j * block, (j + 1) * block)
        hidden_ref[j] = hidden[part]
        dgu_ref[j] = dgu[part]
        outs[j // 4 * 2 + j % 2][j // 2 % 2] = e[part]


def feed(part, xs, y, packed, held):
    rows, width = xs[0].shape
    n_ctx, packed_rows, ff = packed.shape
    steps = 4
    block = rows // steps
    widths = (ff, 2 * ff, width)
    extra = [] if held is None else list(held)
    at_part = lambda n: pl.BlockSpec((TEAM, block, n), lambda i: (0, part * steps + i, 0))
    return pl.pallas_call(
        feed_kernel,
        grid=(steps,),
        in_specs=[pl.BlockSpec((block, width), lambda i: (i, 0))] * TEAM
        + [at_part(width)]
        + [pl.BlockSpec(memory_space=pl.ANY)] * (1 + len(extra)),
        out_specs=(pl.BlockSpec((2, block, width), lambda i: (0, i, 0)),) * 4 + tuple(at_part(n) for n in widths),
        out_shape=(jax.ShapeDtypeStruct((2, rows, width), BF16),) * 4
        + tuple(jax.ShapeDtypeStruct((TEAM, 2 * rows, n), BF16) for n in widths),
        input_output_aliases={TEAM + 2 + i: 4 + i for i in range(len(extra))},
        scratch_shapes=[
            pltpu.VMEM((width, 2 * ff), BF16),
            pltpu.VMEM((ff, width), BF16),
            pltpu.SemaphoreType.DMA((n_ctx * (2 * TEAM + width // ff),)),
        ],
        compiler_params=params(),
        cost_estimate=cost(2 * TEAM * rows * width * 5 * ff, 6 * width * ff + 18 * TEAM * rows * width, TEAM * rows * ff),
        name="feed",
    )(*xs, y, packed, *extra)


def fold_kernel(widths, at_ref, gain_ref, *refs):
    weights, out_ref = refs[:-1], refs[-1]
    gain = gain_ref[...]
    for m in range(TEAM):
        at = 0
        for n, ref in zip(widths, weights):
            out_ref[at_ref[m], :, at : at + n] = (ref[:, m * n : (m + 1) * n].astype(F32) * gain).astype(BF16)
            at += n


def fold(places, gain, weights):
    widths = tuple(w.shape[1] // TEAM for w in weights)
    out = (TEAM, weights[0].shape[0], sum(widths))
    return pl.pallas_call(
        functools.partial(fold_kernel, widths),
        grid_spec=pltpu.PrefetchScalarGridSpec(
            num_scalar_prefetch=1,
            grid=(1,),
            in_specs=[whole(t.shape) for t in (gain, *weights)],
            out_specs=whole(out),
        ),
        out_shape=jax.ShapeDtypeStruct(out, BF16),
        compiler_params=params(),
        cost_estimate=cost(out[0] * out[1] * out[2], 4 * out[0] * out[1] * out[2]),
        name="fold",
    )(places, gain, *weights)


def gradients_kernel(widths, at_ref, gain_ref, grad_ref, *refs):
    count = len(widths)
    weights, outs, gain_out = refs[:count], refs[count : 2 * count], refs[2 * count]
    gain = gain_ref[...]
    total = jnp.zeros(gain.shape, F32)
    for m in range(TEAM):
        at = 0
        for n, w_ref, out_ref in zip(widths, weights, outs):
            g = grad_ref[at_ref[m], :, at : at + n].astype(F32)
            here = slice(m * n, (m + 1) * n)
            total = total + jnp.sum(w_ref[:, here].astype(F32) * g, axis=1, keepdims=True)
            out_ref[:, here] = g * gain
            at += n
    gain_out[...] = jnp.broadcast_to(total, (total.shape[0], 128)).T[:1]


def gradients(places, gain, grad, weights):
    widths = tuple(w.shape[1] // TEAM for w in weights)
    outs = [w.shape for w in weights] + [(1, gain.shape[0])]
    return pl.pallas_call(
        functools.partial(gradients_kernel, widths),
        grid_spec=pltpu.PrefetchScalarGridSpec(
            num_scalar_prefetch=1,
            grid=(1,),
            in_specs=[whole(t.shape) for t in (gain, grad, *weights)],
            out_specs=tuple(whole(shape) for shape in outs),
        ),
        out_shape=tuple(jax.ShapeDtypeStruct(shape, F32) for shape in outs),
        compiler_params=params(SMALL_BYTES),
        cost_estimate=cost(4 * grad.size, 8 * grad.size),
        name="gradients",
    )(places, gain, grad, *weights)


def chip_mates(evens):
    pieces = []
    for even in evens:
        pieces += [even, swap(even, 1)]
    return pieces


def tie(*values):
    leaves, tree = jax.tree.flatten(values)
    return jax.tree.unflatten(tree, lax.optimization_barrier(leaves))


def mates_trade(parts):
    evens, odds = (parts[0], parts[2]), (swap(parts[1], 1), swap(parts[3], 1))
    return (evens[0], odds[0]), mates_sum(evens, odds)


def hop(sums):
    return [swap(r, bit) for r, bit in zip(sums, (2, 4, 6))]


def total_of(own, got):
    total = own[0][0].astype(F32) + own[1][0].astype(F32)
    for part in got:
        total = total + part.astype(F32)
    return total


def place_rows(seq_rows, order, half_rows):
    slots = seq_rows // half_rows
    hit = slots[:, None] == jnp.arange(order.shape[0], dtype=jnp.int32)[None, :]
    return jnp.sum(jnp.where(hit, order[None, :], 0), axis=1) * half_rows + seq_rows % half_rows


def angles(places):
    freqs = THETA ** (-(jnp.arange(HALF).astype(F32) * 2.0 / HEAD_DIM))
    return places.astype(F32)[:, None] * freqs[None, :]


def member_columns(own):
    return lax.all_to_all(own, "dp", 0, 0, tiled=True)


def any_columns(own, index):
    n_dp, n_ctx = lax.axis_size("dp"), lax.axis_size("ctx")
    gathered = lax.all_gather(own, ("dp", "ctx"), axis=0)
    mine = lax.dynamic_index_in_dim(gathered, index, 1, False)
    per = n_dp // TEAM
    mine = mine.reshape(TEAM, n_ctx, per * own.shape[1], own.shape[2])
    return jnp.transpose(mine, (1, 0, 2, 3))


def by_rows(columns):
    return jnp.transpose(columns, (1, 0, 2, 3)).reshape(-1, columns.shape[-1])


def any_rows(own):
    gathered = lax.all_gather(own, ("dp", "ctx"), axis=0, tiled=True)
    count = gathered.shape[0] // TEAM
    return lax.dynamic_slice_in_dim(gathered, (lax.axis_index("dp") % TEAM) * count, count, 0)


def column_blocks(grad):
    n_dp, n_ctx = lax.axis_size("dp"), lax.axis_size("ctx")
    rows_all, width = grad.shape
    blocks = grad.astype(BF16).reshape(TEAM, n_ctx, rows_all // (n_dp * n_ctx), width)
    return jnp.transpose(blocks, (1, 0, 2, 3))


def columns_home(part):
    return lax.all_to_all(part.astype(BF16), "dp", 0, 0, tiled=True)


def columns_out(grad, index):
    hit = (jnp.arange(TEAM) == index)[None, :, None]
    spread = jnp.where(hit, grad.astype(BF16)[:, None, :], jnp.zeros((), BF16))
    out = lax.psum_scatter(spread, ("dp", "ctx"), scatter_dimension=0, tiled=True)
    return jnp.transpose(out, (1, 0, 2))


def rows_out(grad):
    grad = grad.astype(BF16)
    if lax.axis_size("dp") == TEAM:
        return lax.psum_scatter(grad, "ctx", scatter_dimension=0, tiled=True).astype(F32)
    member = lax.axis_index("dp") % TEAM
    hit = (jnp.arange(TEAM) == member)[:, None, None]
    spread = jnp.where(hit, grad[None], jnp.zeros((), BF16)).reshape(-1, grad.shape[1])
    return lax.psum_scatter(spread, ("dp", "ctx"), scatter_dimension=0, tiled=True).astype(F32)


def across(value):
    return lax.all_to_all(value, "ctx", 0, 0, tiled=True)


def ctx_gather(own):
    return across(jnp.broadcast_to(own, (lax.axis_size("ctx"), *own.shape)))


def flat(value):
    return value.reshape(-1, value.shape[-1])


def norm_back(e, xhat, r):
    return r * (e - xhat * jnp.mean(e * xhat, axis=-1, keepdims=True))


def local(
    tokens, cotangent, gain_attn, w_query, w_key, w_value, w_out, gain_ffn, w_gate, w_up, w_down, order
):
    _, span, width = tokens.shape
    n_ctx = lax.axis_size("ctx")
    rows = w_query.shape[0]
    length = span * n_ctx
    half_rows = span // 2
    scale = HEAD_DIM**-0.5

    gain_a = gain_attn.astype(F32)[:, None]
    gain_f = gain_ffn.astype(F32)[:, None]
    mates = TEAM // n_ctx
    here = lax.axis_index("dp") % TEAM
    mate = here % mates
    ids = jnp.arange(TEAM, dtype=jnp.int32)
    place_of = lambda head: head // mates * mates + (head % mates ^ mate)
    member, head_at = here ^ ids, place_of(ids)
    member_at = place_of(member)
    head = lax.axis_index("ctx") * mates + mate
    one_team = lax.axis_size("dp") == TEAM and mates == 2

    storage = jnp.arange(length, dtype=jnp.int32)
    places = place_rows(storage, order, half_rows).astype(F32)
    lane = jnp.arange(QKV, dtype=jnp.int32)
    freq = jnp.where(lane < QW + HEAD_DIM, THETA ** (-((lane % HALF).astype(F32) * 2.0 / HEAD_DIM)), 0.0)
    size = jnp.where(lane < QW, scale, 1.0)
    turn = places[:, None] * freq[None, :]
    sine = jnp.sin(turn) * size
    first = lane % HEAD_DIM < HALF
    tables = (jnp.cos(turn) * size, jnp.where(first, -sine, 0.0), jnp.where(first, 0.0, sine))
    turn_t = angles(storage).T
    cos_t, sin_t = jnp.cos(turn_t), jnp.sin(turn_t)
    slots = jnp.sum(jnp.where(order[None, :] == jnp.arange(order.shape[0])[:, None], jnp.arange(order.shape[0]), 0), axis=1)
    slots = slots.astype(jnp.int32)

    tok, dy_own = tokens[0], cotangent[0]
    x = tok.astype(F32)
    low_x1 = (x * lax.rsqrt(jnp.mean(x * x, axis=-1, keepdims=True) + EPS)).astype(BF16)
    folded_qkv = fold(head_at if one_team else ids, gain_a, (w_query, w_key, w_value))
    folded_gu = fold(ids, gain_f, (w_gate, w_up))
    if one_team:
        x1 = [lax.all_gather(jnp.concatenate([low_x1, w_out], axis=0), "ctx", axis=0)]
        mine_gu = lax.all_to_all(folded_gu, "dp", 0, 0, tiled=True)
        blocks = folded_qkv.reshape(n_ctx, mates, rows, QKV)
        blocks = jnp.stack([blocks[:, 0], swap(blocks[:, 1], 1)], axis=1)
        blocks, mine_gu = tie(blocks, mine_gu)
        piece = across(blocks)
        pieces = [piece, swap(piece, 2), swap(piece, 4), swap(piece, 6)]
        wqkv = rows_of(member, pieces)
        packed = lax.all_gather(pack(mine_gu, w_down), "ctx", axis=0)
    else:
        wqkv = by_rows(any_columns(folded_qkv, head))
        wgu = by_rows(any_columns(folded_gu, here)).reshape(TEAM, width // TEAM, -1)
        x1 = [lax.all_gather(low_x1, "ctx", axis=0)]
        wo, wd = any_rows(w_out), any_rows(w_down)
        packed = pack(wgu, wd)[None]

    dy_even = [dy_own, swap(dy_own, 2), swap(dy_own, 4)]
    x1[0], wqkv, tables, dy_even, cos_t, sin_t = tie(x1[0], wqkv, tables, dy_even, cos_t, sin_t)
    if one_team:
        wo = x1[0][:, span:].reshape(QW, width)
    if mates == 2:
        x1.append(swap(x1[0], 1))
    qkv = qkv_of(x1, span, wqkv, tables)
    other, lse_other = attend(slots, order, qkv, mates - 1, [])
    heads, lse = (other, lse_other) if mates == 1 else attend(slots, order, qkv, 0, [swap(other, 1)])
    dy_even.append(swap(dy_even[0], 6))
    heads, wo = tie(heads, wo)
    wo_all = chip_mates([wo, swap(wo, 2), swap(wo, 4), swap(wo, 6)])
    dy_all = stack(ids, chip_mates(dy_even))
    traded = across(heads)
    traded, wo_all, dy_all = tie(traded, wo_all, dy_all)

    traded = traded.reshape(TEAM, *traded.shape[2:])
    middle, top, low = middle_of(member_at, tok, traded, wo_all)
    even_a = [top, swap(top, 2), swap(top, 4)]
    even_a.append(swap(top, 6))
    x2_a = chip_mates(even_a)
    x2_a, low = tie(x2_a, low)
    even_b = [low, swap(low, 2), swap(low, 4), swap(low, 6)]
    *parts_a, hidden, dgu, x2_all = feed(0, x2_a, dy_all, packed, None)
    even_b, parts_a, hidden, dgu, x2_all = tie(even_b, parts_a, hidden, dgu, x2_all)
    odds_a = [swap(parts_a[1], 1), swap(parts_a[3], 1)]
    x2_b = chip_mates(even_b)
    x2_b, odds_a = tie(x2_b, odds_a)
    got_a = hop(mates_sum((parts_a[0], parts_a[2]), odds_a))
    *parts_b, hidden, dgu, x2_all = feed(1, x2_b, dy_all, packed, (hidden, dgu, x2_all))
    parts_b, got_a = tie(parts_b, got_a)
    dgu = flat(dgu)
    odds_b = [swap(parts_b[1], 1), swap(parts_b[3], 1)]
    g_gate = mm_tn(flat(x2_all), dgu[:, : dgu.shape[1] // 2]).astype(BF16)
    odds_b, g_gate = tie(odds_b, g_gate)

    got_b = mates_sum((parts_b[0], parts_b[2]), odds_b)
    *got_b, x2_all, dy_all, hidden = tie(*got_b, x2_all, dy_all, hidden)
    got_b = hop(got_b)
    g_up = mm_tn(flat(x2_all), dgu[:, dgu.shape[1] // 2 :]).astype(BF16)
    g_down = mm_tn(flat(hidden), flat(dy_all)).astype(BF16)
    mixed_parts = parts_of(hidden, packed, width)
    got_b, mixed_parts = tie(got_b, mixed_parts)
    if one_team:
        g_ff = pack_back(g_gate, g_up, g_down)
        got_b, packed_ff = tie(got_b, g_ff)
        g_ff = lax.psum_scatter(packed_ff.reshape(-1, g_ff.shape[-1]), "ctx", scatter_dimension=0, tiled=True)
    sums = (parts_a[0], odds_a[0], *got_a, parts_b[0], odds_b[0], *got_b)
    d_middle, d_low, d_heads = d_middle_of(member_at, sums, middle, dy_own, wo_all)

    hidden, d_low, d_heads = tie(hidden, d_low, d_heads)
    d_heads = across(d_heads.reshape(n_ctx, mates, *d_heads.shape[1:]))
    mixed_own, mixed_sums = mates_trade(mixed_parts)
    mixed_got = hop(mixed_sums)
    out_parts = grad_out_parts(member_at, traded, d_low)
    d_heads, mixed_got, out_parts = tie(d_heads, mixed_got, out_parts)

    d_other = d_heads if mates == 1 else swap(d_heads[:, 1:], 1)
    d_qkv, more = [attend_back(slots, qkv, mates - 1, d_other, lse_other, cos_t, sin_t)], []
    if mates == 2:
        more = [swap(input_all(d_qkv[0], wqkv), 1)]
        d_qkv = [attend_back(slots, qkv, 0, d_heads, lse, cos_t, sin_t), *d_qkv]
    d_qkv, more = tie(d_qkv, more)
    e1 = input_own(d_qkv[0], wqkv, more)
    e1, d_qkv, mixed_got, out_parts = tie(e1, d_qkv, mixed_got, out_parts)
    e1 = lax.psum_scatter(e1, "ctx", scatter_dimension=0)

    out_own, out_sums = mates_trade(out_parts)
    mixed = (middle + total_of(mixed_own, mixed_got)).astype(BF16)[None]
    g_qkv = mm_tn(flat(x1[0][:, :span]), flat(d_qkv[0]))
    for a, b in zip(x1[1:], d_qkv[1:]):
        g_qkv = g_qkv + mm_tn(flat(a[:, :span]), flat(b))
    if one_team:
        ff = g_ff.shape[1]
        cut = TEAM * rows
        ways, g_ff = tie(pieces_of(member, g_qkv), g_ff)
        g_gu = jnp.concatenate([g_ff[:cut].reshape(TEAM, rows, ff), g_ff[cut : 2 * cut].reshape(TEAM, rows, ff)], axis=2)
        g_gu = lax.all_to_all(g_gu, "dp", 0, 0, tiled=True)
        ways = [ways[0], *hop(ways[1:])]
        ways, out_sums = tie(ways, out_sums)
        home = ways[0].astype(F32)
        for way in ways[1:]:
            home = home + way.astype(F32)
        home = home.astype(BF16).reshape(mates, n_ctx, rows, QKV)
        home, g_gu = tie(jnp.stack([home[0], swap(home[1], 1)], axis=1), g_gu)
        home = across(home).reshape(TEAM, rows, QKV)
        g_out, home = tie(total_of(out_own, hop(out_sums)).astype(BF16), home)
        grad_out = jnp.sum(across(g_out.reshape(n_ctx, -1, width)).astype(F32), axis=0)
        down = g_ff[2 * cut :].reshape(width // ff, -1, ff)
        grad_down = jnp.concatenate([down[i] for i in range(width // ff)], axis=1).astype(F32)
    else:
        home = columns_out(g_qkv, head)
        g_gu = columns_out(jnp.concatenate([g_gate, g_up], axis=1), here)
        grad_down, grad_out = rows_out(g_down), rows_out(total_of(out_own, hop(out_sums)))
    *grads_qkv, gain_a_grad = gradients(head_at if one_team else ids, gain_a, home, (w_query, w_key, w_value))
    *grads_gu, gain_f_grad = gradients(ids, gain_f, g_gu, (w_gate, w_up))
    token_grad = token_gradient(e1, tok, d_middle)
    return (
        mixed,
        token_grad[None],
        gain_a_grad[0],
        *grads_qkv,
        grad_out,
        gain_f_grad[0],
        *grads_gu,
        grad_down,
    )


def solution(mesh):
    act = P("dp", "ctx", None)
    vec = P(("dp", "ctx"))
    mat = P(("dp", "ctx"), None)
    return jax.shard_map(
        local,
        mesh=mesh,
        in_specs=(act, act, vec, mat, mat, mat, mat, vec, mat, mat, mat, P()),
        out_specs=(act, act, vec, mat, mat, mat, mat, vec, mat, mat, mat),
        check_vma=False,
    )
```

```python
import functools

import jax
import jax.numpy as jnp
from jax import lax
from jax.experimental import pallas as pl
from jax.experimental.pallas import tpu as pltpu
from jax.sharding import PartitionSpec as P

HEADS = 16
KV_HEADS = 8
HEAD_DIM = 96
GROUPS = HEADS // KV_HEADS
HALF = HEAD_DIM // 2
QW = GROUPS * HEAD_DIM
QKV = QW + 2 * HEAD_DIM

EPS = 1e-05
THETA = 100000.0
F32 = jnp.float32
BF16 = jnp.bfloat16
CHUNKS = 4
VMEM_BYTES = 56 * 2**20
SMALL_BYTES = 24 * 2**20

TEAM = KV_HEADS
PAIRS = TEAM // 2


def dot(a, b, dims):
    return lax.dot_general(a, b, (dims, ((), ())), preferred_element_type=F32)


def mm(a, b):
    return dot(a, b, ((1,), (0,)))


def mm_nt(a, b):
    return dot(a, b, ((1,), (1,)))


def mm_tn(a, b):
    return dot(a, b, ((0,), (0,)))


def swap(value, bit):
    n = lax.axis_size("dp")
    return lax.ppermute(value, "dp", [(i, i ^ bit) for i in range(n)])


def after(value, *others):
    return lax.optimization_barrier((value, *others))[0]


def params(limit=VMEM_BYTES):
    return pltpu.CompilerParams(vmem_limit_bytes=limit)


def cost(flops, nbytes, exps=0):
    return pl.CostEstimate(flops=int(flops), bytes_accessed=int(nbytes), transcendentals=int(exps))


def whole(shape):
    return pl.BlockSpec(shape, lambda *_: (0,) * len(shape))


def join(even_ref, odd_ref):
    return jnp.concatenate([even_ref[...], odd_ref[...]], axis=0)


def qkv_kernel(x_ref, w_ref, cos_ref, sin_ref, out_ref):
    scale = HEAD_DIM**-0.5
    cosine, sine = cos_ref[...], sin_ref[...]
    cosine = jnp.concatenate([cosine * scale] * GROUPS + [cosine, jnp.ones_like(cosine)], axis=1)
    sine = jnp.concatenate([sine * scale] * GROUPS + [sine, jnp.zeros_like(sine)], axis=1)
    first = lax.broadcasted_iota(jnp.int32, cosine.shape, 1) % HEAD_DIM < HALF
    y = mm(x_ref[0], w_ref[...])
    partner = jnp.where(first, pltpu.roll(y, QKV - HALF, 1), pltpu.roll(y, HALF, 1))
    out_ref[0] = (y * cosine + partner * sine).astype(BF16)


def qkv_of(x, span, w, tables):
    n_ctx, _, width = x.shape
    return pl.pallas_call(
        qkv_kernel,
        grid=(n_ctx,),
        in_specs=[pl.BlockSpec((1, span, width), lambda i: (i, 0, 0)), whole(w.shape)]
        + [pl.BlockSpec((span, HEAD_DIM), lambda i: (i, 0))] * 2,
        out_specs=pl.BlockSpec((1, span, QKV), lambda i: (i, 0, 0)),
        out_shape=jax.ShapeDtypeStruct((n_ctx, span, QKV), BF16),
        compiler_params=params(SMALL_BYTES),
        cost_estimate=cost(2 * n_ctx * span * width * QKV, 2 * n_ctx * span * width + 2 * width * QKV),
        name="qkv",
    )(x, w, *tables)


def first_kernel(x_ref, w_ref, out_ref):
    rows = x_ref.shape[0]
    x = x_ref[...].astype(F32)
    r = lax.rsqrt(jnp.mean(x * x, axis=-1, keepdims=True) + EPS)
    out_ref[:rows] = (x * r).astype(BF16)
    out_ref[rows:] = w_ref[...]


def first_of(x, w):
    out = (x.shape[0] + w.shape[0], x.shape[1])
    return pl.pallas_call(
        first_kernel,
        grid=(1,),
        in_specs=[whole(x.shape), whole(w.shape)],
        out_specs=whole(out),
        out_shape=jax.ShapeDtypeStruct(out, BF16),
        compiler_params=params(SMALL_BYTES),
        cost_estimate=cost(6 * x.size, 4 * out[0] * out[1]),
        name="first",
    )(x, w)


def rows_kernel(member_ref, *refs):
    pieces, out_ref = refs[:-1], refs[-1]
    n_ctx, _, rows, _ = pieces[0].shape
    for p, piece in enumerate(pieces):
        for c in range(n_ctx):
            for j in range(2):
                at = pl.multiple_of((member_ref[2 * p + j] * n_ctx + c) * rows, 16)
                out_ref[pl.ds(at, rows), :] = piece[c, j]


def rows_of(member, pieces):
    n_ctx, two, rows, width = pieces[0].shape
    out = (len(pieces) * n_ctx * two * rows, width)
    return pl.pallas_call(
        rows_kernel,
        grid_spec=pltpu.PrefetchScalarGridSpec(
            num_scalar_prefetch=1,
            grid=(1,),
            in_specs=[whole(t.shape) for t in pieces],
            out_specs=whole(out),
        ),
        out_shape=jax.ShapeDtypeStruct(out, BF16),
        compiler_params=params(SMALL_BYTES),
        cost_estimate=cost(0, 4 * out[0] * out[1]),
        name="rows",
    )(member, *pieces)


def pieces_kernel(member_ref, grad_ref, *out_refs):
    for p, out_ref in enumerate(out_refs):
        for j in range(2):
            out_ref[j] = grad_ref[member_ref[2 * p + j]].astype(BF16)


def pieces_of(member, grad):
    rows, width = grad.shape[0] // TEAM, grad.shape[1]
    return pl.pallas_call(
        pieces_kernel,
        grid_spec=pltpu.PrefetchScalarGridSpec(
            num_scalar_prefetch=1,
            grid=(1,),
            in_specs=[whole((TEAM, rows, width))],
            out_specs=(whole((2, rows, width)),) * PAIRS,
        ),
        out_shape=(jax.ShapeDtypeStruct((2, rows, width), BF16),) * PAIRS,
        compiler_params=params(SMALL_BYTES),
        cost_estimate=cost(0, 6 * grad.size),
        name="pieces",
    )(member, grad.reshape(TEAM, rows, width))


def stack_kernel(order_ref, *refs):
    for k, ref in enumerate(refs[:-1]):
        refs[-1][order_ref[k]] = ref[...]


def stack(order, xs):
    rows, width = xs[0].shape
    steps = 4
    block = rows // steps
    return pl.pallas_call(
        stack_kernel,
        grid_spec=pltpu.PrefetchScalarGridSpec(
            num_scalar_prefetch=1,
            grid=(steps,),
            in_specs=[pl.BlockSpec((block, width), lambda i, m: (i, 0))] * len(xs),
            out_specs=pl.BlockSpec((len(xs), block, width), lambda i, m: (0, i, 0)),
        ),
        out_shape=jax.ShapeDtypeStruct((len(xs), rows, width), BF16),
        compiler_params=params(),
        cost_estimate=cost(0, 4 * len(xs) * rows * width),
        name="stack",
    )(order, *xs)


def in_order(slots_ref, ref, scratch, half):
    for b in range(slots_ref.shape[0]):
        slot = slots_ref[b]
        at = pl.multiple_of((slot % 2) * half, half)
        scratch[pl.ds(b * half, half), :] = ref[slot // 2, pl.ds(at, half), :]


def heads_in_order(slots_ref, ref, scratch, half):
    for b in range(slots_ref.shape[0]):
        slot = slots_ref[b]
        first, second = ref[slot // 2, 0, :, :QW], ref[slot // 2, 0, :, QW:]
        scratch[pl.ds(b * half, half), :] = jnp.where(slot % 2 == 0, first, second)


def heads_out_of_order(order_ref, ref, scratch, half):
    for c in range(ref.shape[0]):
        for j in range(2):
            at = pl.multiple_of(order_ref[2 * c + j] * half, half)
            ref[c, 0, :, j * QW : (j + 1) * QW] = scratch[pl.ds(at, half), :]


def out_of_order(slots_ref, ref, first, value, half):
    for b in range(value.shape[0] // half):
        slot = slots_ref[first // half + b]
        at = pl.multiple_of((slot % 2) * half, half)
        ref[slot // 2, pl.ds(at, half), :] = value[b * half : (b + 1) * half]


def flip(value):
    return value.astype(F32).T


def stacked_heads(ref, rows):
    return jnp.concatenate([ref[rows, g * HEAD_DIM : (g + 1) * HEAD_DIM] for g in range(GROUPS)], axis=0)


def causal(size):
    key = lax.broadcasted_iota(jnp.int32, (size, GROUPS * size), 0)
    query = lax.broadcasted_iota(jnp.int32, (size, GROUPS * size), 1) % size
    return key <= query


def attend_kernel(slots_ref, order_ref, qkv_ref, *refs):
    more, (out_ref, lse_ref, scratch, o_scr) = refs[:-4], refs[-4:]
    half = qkv_ref.shape[1] // 2
    size = scratch.shape[0] // CHUNKS
    in_order(slots_ref, qkv_ref, scratch, half)
    v_t = flip(scratch[:, QW + HEAD_DIM :]).astype(BF16)
    allowed = causal(size)
    for i in range(CHUNKS):
        lo, hi = i * size, (i + 1) * size
        q = stacked_heads(scratch, slice(lo, hi))
        k_near = scratch[lo:hi, QW : QW + HEAD_DIM]
        near = jnp.where(allowed, mm_nt(k_near, q), -1e30)
        top = jnp.max(near, axis=0, keepdims=True)
        if i > 0:
            far = mm_nt(scratch[:lo, QW : QW + HEAD_DIM], q)
            top = jnp.maximum(top, jnp.max(far, axis=0, keepdims=True))
        near = jnp.exp(near - top)
        total = jnp.sum(near, axis=0, keepdims=True)
        acc = mm(v_t[:, lo:hi], near.astype(BF16))
        if i > 0:
            far = jnp.exp(far - top)
            total = total + jnp.sum(far, axis=0, keepdims=True)
            acc = acc + mm(v_t[:, :lo], far.astype(BF16))
        lse_ref[pl.ds(i, 1), :] = top + jnp.log(total)
        o = (acc / total).T.astype(BF16)
        for g in range(GROUPS):
            o_scr[lo:hi, g * HEAD_DIM : (g + 1) * HEAD_DIM] = o[g * size : (g + 1) * size]
    heads_out_of_order(order_ref, out_ref, o_scr, half)
    for ref in more:
        out_ref[:, 1] = ref[:, 0]


def attend_back_kernel(slots_ref, qkv_ref, do_ref, lse_ref, cos_ref, sin_ref, out_ref, scratch, do_scr, dk_scr, dv_scr):
    half = qkv_ref.shape[1] // 2
    length = scratch.shape[0]
    size = length // CHUNKS
    scale = HEAD_DIM**-0.5
    in_order(slots_ref, qkv_ref, scratch, half)
    heads_in_order(slots_ref, do_ref, do_scr, half)
    k_t = flip(scratch[:, QW : QW + HEAD_DIM]).astype(BF16)
    allowed = causal(size)
    dk_scr[...] = jnp.zeros_like(dk_scr)
    dv_scr[...] = jnp.zeros_like(dv_scr)
    for i in range(CHUNKS):
        lo, hi = i * size, (i + 1) * size
        q = stacked_heads(scratch, slice(lo, hi))
        do = stacked_heads(do_scr, slice(lo, hi))
        lse = lse_ref[pl.ds(i, 1), :]
        spans = [(lo, hi)] + ([(0, lo)] if i > 0 else [])
        probs, prods = [], []
        delta = 0.0
        for at, (a, b) in enumerate(spans):
            p = jnp.exp(mm_nt(scratch[a:b, QW : QW + HEAD_DIM], q) - lse)
            if at == 0:
                p = jnp.where(allowed, p, 0.0)
            prod = p * mm_nt(scratch[a:b, QW + HEAD_DIM :], do)
            delta = delta + jnp.sum(prod, axis=0, keepdims=True)
            probs.append(p)
            prods.append(prod)
        dq_t = 0.0
        for (a, b), p, prod in zip(spans, probs, prods):
            ds = (prod - p * delta).astype(BF16)
            dk_scr[a:b, :] += mm(ds, q)
            dv_scr[a:b, :] += mm(p.astype(BF16), do)
            dq_t = dq_t + mm(k_t[:, a:b], ds)
        c = jnp.concatenate([cos_ref[:, lo:hi]] * GROUPS, axis=1) * scale
        s = jnp.concatenate([sin_ref[:, lo:hi]] * GROUPS, axis=1) * scale
        first, second = dq_t[:HALF], dq_t[HALF:]
        dq = jnp.concatenate([first * c + second * s, second * c - first * s], axis=0).T
        for g in range(GROUPS):
            do_scr[lo:hi, g * HEAD_DIM : (g + 1) * HEAD_DIM] = dq[g * size : (g + 1) * size].astype(BF16)
    for i in range(CHUNKS):
        lo, hi = i * size, (i + 1) * size
        dk_t = dk_scr[lo:hi, :].T
        first, second = dk_t[:HALF], dk_t[HALF:]
        c, s = cos_ref[:, lo:hi], sin_ref[:, lo:hi]
        dk = jnp.concatenate([first * c + second * s, second * c - first * s], axis=0).T
        value = jnp.concatenate([do_scr[lo:hi, :], dk.astype(BF16), dv_scr[lo:hi, :].astype(BF16)], axis=1)
        out_of_order(slots_ref, out_ref, lo, value, half)


def attend(slots, order, qkv, more):
    n_ctx, span, _ = qkv.shape
    length = n_ctx * span
    heads = (n_ctx, 1 + len(more), span // 2, 2 * QW)
    lse = (CHUNKS, GROUPS * length // CHUNKS)
    work = GROUPS * length * length
    return pl.pallas_call(
        attend_kernel,
        grid_spec=pltpu.PrefetchScalarGridSpec(
            num_scalar_prefetch=2,
            grid=(1,),
            in_specs=[whole(t.shape) for t in (qkv, *more)],
            out_specs=(whole(heads), whole(lse)),
            scratch_shapes=[pltpu.VMEM((length, QKV), BF16), pltpu.VMEM((length, QW), BF16)],
        ),
        out_shape=(jax.ShapeDtypeStruct(heads, BF16), jax.ShapeDtypeStruct(lse, F32)),
        compiler_params=params(SMALL_BYTES),
        cost_estimate=cost(work * 2 * HEAD_DIM * 3, 2 * length * (QKV + QW), work // 2),
        name="attend",
    )(slots, order, qkv, *more)


def attend_back(slots, qkv, d_heads, lse, cos_t, sin_t):
    n_ctx, span, _ = qkv.shape
    length = n_ctx * span
    work = GROUPS * length * length
    return pl.pallas_call(
        attend_back_kernel,
        grid_spec=pltpu.PrefetchScalarGridSpec(
            num_scalar_prefetch=1,
            grid=(1,),
            in_specs=[
                whole(qkv.shape),
                whole((n_ctx, 1, *d_heads.shape[2:])),
            ]
            + [whole(t.shape) for t in (lse, cos_t, sin_t)],
            out_specs=whole((n_ctx, span, QKV)),
            scratch_shapes=[
                pltpu.VMEM((length, QKV), BF16),
                pltpu.VMEM((length, QW), BF16),
                pltpu.VMEM((length, HEAD_DIM), F32),
                pltpu.VMEM((length, HEAD_DIM), F32),
            ],
        ),
        out_shape=jax.ShapeDtypeStruct((n_ctx, span, QKV), BF16),
        compiler_params=params(SMALL_BYTES),
        cost_estimate=cost(work * 2 * HEAD_DIM * 8, 4 * length * QKV, work // 2),
        name="attend_back",
    )(slots, qkv, d_heads, lse, cos_t, sin_t)


def parts_kernel(a_ref, packed, *refs):
    out_refs, (wd_ref, sem) = refs[:4], refs[4:]

    @pl.when(pl.program_id(0) == 0)
    def _():
        copies = [pltpu.make_async_copy(src, dst, sem.at[i]) for i, (src, dst) in enumerate(down_ways(packed, wd_ref))]
        for copy in copies:
            copy.start()
        for copy in copies:
            copy.wait()

    block = a_ref.shape[1]
    y = mm(jnp.concatenate([a_ref[k] for k in range(TEAM)], axis=0), wd_ref[...]).astype(BF16)
    for k in range(TEAM):
        out_refs[k // 4 * 2 + k % 2][k // 2 % 2] = y[k * block : (k + 1) * block]


def parts_of(a, packed, width):
    _, rows, depth = a.shape
    steps = 4
    block = rows // steps
    return pl.pallas_call(
        parts_kernel,
        grid=(steps,),
        in_specs=[pl.BlockSpec((TEAM, block, depth), lambda i: (0, i, 0)), pl.BlockSpec(memory_space=pl.ANY)],
        out_specs=(pl.BlockSpec((2, block, width), lambda i: (0, i, 0)),) * 4,
        out_shape=(jax.ShapeDtypeStruct((2, rows, width), BF16),) * 4,
        scratch_shapes=[
            pltpu.VMEM((depth, width), BF16),
            pltpu.SemaphoreType.DMA((packed.shape[0] * (width // depth),)),
        ],
        compiler_params=params(SMALL_BYTES),
        cost_estimate=cost(2 * TEAM * rows * depth * width, 2 * TEAM * rows * (width + depth) + 2 * depth * width),
        name="parts",
    )(a, packed)


def input_own_kernel(a_ref, w_ref, *refs):
    y = mm_nt(a_ref[0], w_ref[...])
    for ref in refs[:-1]:
        y = y + ref[0].astype(F32)
    refs[-1][0] = y.astype(BF16)


def input_own(a, w, more):
    n_ctx, span, depth = a.shape
    width = w.shape[0]
    blocked = lambda n: pl.BlockSpec((1, span, n), lambda i: (i, 0, 0))
    return pl.pallas_call(
        input_own_kernel,
        grid=(n_ctx,),
        in_specs=[blocked(depth), whole(w.shape)] + [blocked(width)] * len(more),
        out_specs=blocked(width),
        out_shape=jax.ShapeDtypeStruct((n_ctx, span, width), BF16),
        compiler_params=params(SMALL_BYTES),
        cost_estimate=cost(2 * n_ctx * span * depth * width, 4 * n_ctx * span * (width + depth) + 2 * depth * width),
        name="input_own",
    )(a, w, *more)


def input_all_kernel(a_ref, w_ref, out_ref):
    out_ref[0] = mm_nt(a_ref[0], w_ref[...]).astype(BF16)


def input_all(a, w):
    n_ctx, span, depth = a.shape
    width = w.shape[0]
    blocked = lambda n: pl.BlockSpec((1, span, n), lambda i: (i, 0, 0))
    return pl.pallas_call(
        input_all_kernel,
        grid=(n_ctx,),
        in_specs=[blocked(depth), whole(w.shape)],
        out_specs=blocked(width),
        out_shape=jax.ShapeDtypeStruct((n_ctx, span, width), BF16),
        compiler_params=params(SMALL_BYTES),
        cost_estimate=cost(2 * n_ctx * span * depth * width, 4 * n_ctx * span * (width + depth) + 2 * depth * width),
        name="input_all",
    )(a, w)


def grad_out_kernel(at_ref, heads_ref, dm_ref, *out_refs):
    dm = dm_ref[...]
    for k in range(TEAM):
        y = mm_tn(unfold(heads_ref[at_ref[k]]), dm)
        out_refs[k // 4 * 2 + k % 2][k // 2 % 2] = y.astype(BF16)


def grad_out_parts(member_at, heads, dm):
    rows, width = dm.shape
    return pl.pallas_call(
        grad_out_kernel,
        grid_spec=pltpu.PrefetchScalarGridSpec(
            num_scalar_prefetch=1,
            grid=(1,),
            in_specs=[whole(t.shape) for t in (heads, dm)],
            out_specs=(whole((2, QW, width)),) * 4,
        ),
        out_shape=(jax.ShapeDtypeStruct((2, QW, width), BF16),) * 4,
        compiler_params=params(),
        cost_estimate=cost(2 * TEAM * rows * QW * width, 2 * TEAM * QW * width),
        name="grad_out",
    )(member_at, heads, dm)


def unfold(block):
    return jnp.concatenate([block[:, :QW], block[:, QW:]], axis=0)


def fetch(any_refs, ref, sem):
    copies = [pltpu.make_async_copy(a, ref.at[k], sem.at[k]) for k, a in enumerate(any_refs)]
    for copy in copies:
        copy.start()
    return copies


def fetched(arrays):
    specs = [pl.BlockSpec(memory_space=pl.ANY)] * len(arrays)
    scratch = [pltpu.VMEM((len(arrays), *arrays[0].shape), BF16), pltpu.SemaphoreType.DMA((len(arrays),))]
    return specs, scratch


def middle_kernel(at_ref, heads_ref, x_ref, *refs):
    wo_any, (middle_ref, top_ref, low_ref, wo_ref, sem) = refs[:TEAM], refs[TEAM:]
    copies = fetch(wo_any, wo_ref, sem)
    heads = jnp.concatenate([unfold(heads_ref[at_ref[k]]) for k in range(TEAM)], axis=1)
    for copy in copies:
        copy.wait()
    acc = x_ref[...].astype(F32) + mm(heads, wo_ref[...].reshape(heads.shape[1], -1))
    middle_ref[...] = acc
    r = lax.rsqrt(jnp.mean(acc * acc, axis=-1, keepdims=True) + EPS)
    xhat = (acc * r).astype(BF16)
    half = top_ref.shape[0]
    top_ref[...] = xhat[:half]
    low_ref[...] = xhat[half:]


def middle_of(member_at, x, heads, wo):
    rows, width = x.shape
    specs, scratch = fetched(wo)
    return pl.pallas_call(
        middle_kernel,
        grid_spec=pltpu.PrefetchScalarGridSpec(
            num_scalar_prefetch=1,
            grid=(1,),
            in_specs=[whole(t.shape) for t in (heads, x)] + specs,
            out_specs=(whole(x.shape),) + (whole((rows // 2, width)),) * 2,
            scratch_shapes=scratch,
        ),
        out_shape=(jax.ShapeDtypeStruct(x.shape, F32),) + (jax.ShapeDtypeStruct((rows // 2, width), BF16),) * 2,
        compiler_params=params(),
        cost_estimate=cost(2 * rows * width * TEAM * QW, 2 * width * TEAM * QW + 12 * rows * width),
        name="middle",
    )(member_at, heads, x, *wo)


def d_middle_kernel(at_ref, *refs):
    middle_ref, dy_ref = refs[2:4]
    wo_any, (d_ref, low_ref, out_ref, wo_ref, sem) = refs[4 : 4 + TEAM], refs[4 + TEAM :]
    copies = fetch(wo_any, wo_ref, sem)
    middle = middle_ref[...]
    half = middle.shape[0] // 2
    r = lax.rsqrt(jnp.mean(middle * middle, axis=-1, keepdims=True) + EPS)
    d = dy_ref[...].astype(F32) + norm_back(team_total(refs[:2]), middle * r, r)
    d_ref[...] = d
    low = d.astype(BF16)
    low_ref[...] = low
    for copy in copies:
        copy.wait()
    y = mm_nt(low, wo_ref[...].reshape(TEAM * QW, -1)).astype(BF16)
    for k in range(TEAM):
        part = slice(k * QW, (k + 1) * QW)
        out_ref[at_ref[k], :, :QW] = y[:half, part]
        out_ref[at_ref[k], :, QW:] = y[half:, part]


def d_middle_of(member_at, sums, middle, dy, wo):
    rows, width = dy.shape
    heads = (TEAM, rows // 2, 2 * QW)
    specs, scratch = fetched(wo)
    return pl.pallas_call(
        d_middle_kernel,
        grid_spec=pltpu.PrefetchScalarGridSpec(
            num_scalar_prefetch=1,
            grid=(1,),
            in_specs=[whole(t.shape) for t in (*sums, middle, dy)] + specs,
            out_specs=(whole(dy.shape), whole(dy.shape), whole(heads)),
            scratch_shapes=scratch,
        ),
        out_shape=(
            jax.ShapeDtypeStruct(dy.shape, F32),
            jax.ShapeDtypeStruct(dy.shape, BF16),
            jax.ShapeDtypeStruct(heads, BF16),
        ),
        compiler_params=params(),
        cost_estimate=cost(2 * rows * width * TEAM * QW, 2 * width * TEAM * QW + 18 * rows * width),
        name="d_middle",
    )(member_at, *sums, middle, dy, *wo)


def mates_kernel(*refs):
    evens, odds, outs = refs[:2], refs[2:4], refs[4:]
    for j, k in enumerate((2, 4, 6)):
        r = evens[k // 4][k // 2 % 2].astype(F32) + odds[k // 4][k // 2 % 2].astype(F32)
        outs[j][...] = r.astype(BF16)


def mates_sum(evens, odds):
    _, rows, width = evens[0].shape
    steps = 2
    block = rows // steps
    return pl.pallas_call(
        mates_kernel,
        grid=(steps,),
        in_specs=[pl.BlockSpec((2, block, width), lambda i: (0, i, 0))] * 4,
        out_specs=(pl.BlockSpec((block, width), lambda i: (i, 0)),) * 3,
        out_shape=(jax.ShapeDtypeStruct((rows, width), BF16),) * 3,
        compiler_params=params(SMALL_BYTES),
        cost_estimate=cost(6 * rows * width, 36 * rows * width),
        name="mates_sum",
    )(*evens, *odds)


def mates_all_kernel(member_ref, *refs):
    evens, odds, out_ref = refs[:2], refs[2:4], refs[4]
    for k in (0, 2, 4, 6):
        r = evens[k // 4][k // 2 % 2].astype(F32) + odds[k // 4][k // 2 % 2].astype(F32)
        out_ref[member_ref[k] // 2] = r.astype(BF16)


def mates_all(member, evens, odds):
    _, rows, width = evens[0].shape
    steps = 2
    block = rows // steps
    return pl.pallas_call(
        mates_all_kernel,
        grid_spec=pltpu.PrefetchScalarGridSpec(
            num_scalar_prefetch=1,
            grid=(steps,),
            in_specs=[pl.BlockSpec((2, block, width), lambda i, m: (0, i, 0))] * 4,
            out_specs=pl.BlockSpec((PAIRS, block, width), lambda i, m: (0, i, 0)),
        ),
        out_shape=jax.ShapeDtypeStruct((PAIRS, rows, width), BF16),
        compiler_params=params(SMALL_BYTES),
        cost_estimate=cost(8 * rows * width, 48 * rows * width),
        name="mates_all",
    )(member, *evens, *odds)


def team_total(refs):
    return jnp.concatenate([jnp.sum(ref[...].astype(F32), axis=0) for ref in refs], axis=0)


def token_kernel(e_ref, x_ref, d_ref, out_ref):
    x = x_ref[...].astype(F32)
    r = lax.rsqrt(jnp.mean(x * x, axis=-1, keepdims=True) + EPS)
    out_ref[...] = d_ref[...] + norm_back(e_ref[...].astype(F32), x * r, r)


def token_gradient(e, x, d_middle):
    rows, width = x.shape
    block = rows // 2
    return pl.pallas_call(
        token_kernel,
        grid=(2,),
        in_specs=[pl.BlockSpec((block, width), lambda i: (i, 0))] * 3,
        out_specs=pl.BlockSpec((block, width), lambda i: (i, 0)),
        out_shape=jax.ShapeDtypeStruct(x.shape, F32),
        compiler_params=params(),
        cost_estimate=cost(12 * x.size, 20 * x.size),
        name="token_gradient",
    )(e, x, d_middle)


def pack(gate_up, down):
    _, rows, twice = gate_up.shape
    ff = twice // 2
    blocks = [gate_up[..., :ff].reshape(-1, ff), gate_up[..., ff:].reshape(-1, ff)]
    return jnp.concatenate(blocks + [down[:, i : i + ff] for i in range(0, down.shape[1], ff)], axis=0)


def pack_back(gate, up, down):
    n = lax.axis_size("ctx")
    width, ff = gate.shape
    by_ctx = lambda g: jnp.transpose(g.reshape(TEAM, n, -1, ff), (1, 0, 2, 3)).reshape(n, -1, ff)
    blocks = [by_ctx(gate), by_ctx(up)]
    down = down.reshape(n, ff // n, width)
    return jnp.concatenate(blocks + [down[..., i : i + ff] for i in range(0, width, ff)], axis=1)


def down_ways(packed, wd_ref):
    n_ctx, count, ff = packed.shape
    width = wd_ref.shape[1]
    down = ff // n_ctx
    first = count - width // ff * down
    return [
        (packed.at[c, pl.ds(first + i * down, down)], wd_ref.at[pl.ds(c * down, down), pl.ds(i * ff, ff)])
        for c in range(n_ctx)
        for i in range(width // ff)
    ]


def unpack(packed, wgu_ref, wd_ref, sem):
    n_ctx, _, ff = packed.shape
    rows = wgu_ref.shape[0] // (TEAM * n_ctx)
    ways = []
    for part in range(2):
        for c in range(n_ctx):
            for m in range(TEAM):
                out = wgu_ref.at[pl.ds((m * n_ctx + c) * rows, rows), pl.ds(part * ff, ff)]
                ways.append((packed.at[c, pl.ds((part * TEAM + m) * rows, rows)], out))
    ways += down_ways(packed, wd_ref)
    copies = [pltpu.make_async_copy(src, dst, sem.at[i]) for i, (src, dst) in enumerate(ways)]
    for copy in copies:
        copy.start()
    return copies


def feed_kernel(*refs):
    x_refs = refs[:TEAM]
    y_ref, packed = refs[TEAM : TEAM + 2]
    even0_ref, odd0_ref, even1_ref, odd1_ref, hidden_ref, dgu_ref, xc_ref, wgu_ref, wd_ref, sem = refs[-10:]
    ff = wd_ref.shape[0]
    block = x_refs[0].shape[0]

    @pl.when(pl.program_id(0) == 0)
    def _():
        for copy in unpack(packed, wgu_ref, wd_ref, sem):
            copy.wait()

    for j in range(TEAM):
        xc_ref[j] = x_refs[j][...]
    x = jnp.concatenate([ref[...] for ref in x_refs], axis=0)
    y = y_ref[...].reshape(TEAM * block, y_ref.shape[2])
    gate = mm(x, wgu_ref[:, :ff])
    upper = mm(x, wgu_ref[:, ff:])
    d_hidden = mm_nt(y, wd_ref[...])
    sigma = jax.nn.sigmoid(gate)
    act = gate * sigma
    hidden = (act * upper).astype(BF16)
    d_gate = (d_hidden * upper * sigma * (1.0 + gate * (1.0 - sigma))).astype(BF16)
    dgu = jnp.concatenate([d_gate, (d_hidden * act).astype(BF16)], axis=1)
    e = mm_nt(dgu, wgu_ref[...]).astype(BF16)
    outs = (even0_ref, odd0_ref, even1_ref, odd1_ref)
    for j in range(TEAM):
        part = slice(j * block, (j + 1) * block)
        hidden_ref[j] = hidden[part]
        dgu_ref[j] = dgu[part]
        outs[j // 4 * 2 + j % 2][j // 2 % 2] = e[part]


def feed(part, xs, y, packed, held):
    rows, width = xs[0].shape
    n_ctx, packed_rows, ff = packed.shape
    steps = 4
    block = rows // steps
    widths = (ff, 2 * ff, width)
    extra = [] if held is None else list(held)
    at_part = lambda n: pl.BlockSpec((TEAM, block, n), lambda i: (0, part * steps + i, 0))
    return pl.pallas_call(
        feed_kernel,
        grid=(steps,),
        in_specs=[pl.BlockSpec((block, width), lambda i: (i, 0))] * TEAM
        + [at_part(width)]
        + [pl.BlockSpec(memory_space=pl.ANY)] * (1 + len(extra)),
        out_specs=(pl.BlockSpec((2, block, width), lambda i: (0, i, 0)),) * 4 + tuple(at_part(n) for n in widths),
        out_shape=(jax.ShapeDtypeStruct((2, rows, width), BF16),) * 4
        + tuple(jax.ShapeDtypeStruct((TEAM, 2 * rows, n), BF16) for n in widths),
        input_output_aliases={TEAM + 2 + i: 4 + i for i in range(len(extra))},
        scratch_shapes=[
            pltpu.VMEM((width, 2 * ff), BF16),
            pltpu.VMEM((ff, width), BF16),
            pltpu.SemaphoreType.DMA((n_ctx * (2 * TEAM + width // ff),)),
        ],
        compiler_params=params(),
        cost_estimate=cost(2 * TEAM * rows * width * 5 * ff, 6 * width * ff + 18 * TEAM * rows * width, TEAM * rows * ff),
        name="feed",
    )(*xs, y, packed, *extra)


def fold_kernel(widths, at_ref, gain_ref, *refs):
    weights, out_ref = refs[:-1], refs[-1]
    gain = gain_ref[...]
    for m in range(TEAM):
        at = 0
        for n, ref in zip(widths, weights):
            out_ref[at_ref[m], :, at : at + n] = (ref[:, m * n : (m + 1) * n].astype(F32) * gain).astype(BF16)
            at += n


def fold(places, gain, weights):
    widths = tuple(w.shape[1] // TEAM for w in weights)
    out = (TEAM, weights[0].shape[0], sum(widths))
    return pl.pallas_call(
        functools.partial(fold_kernel, widths),
        grid_spec=pltpu.PrefetchScalarGridSpec(
            num_scalar_prefetch=1,
            grid=(1,),
            in_specs=[whole(t.shape) for t in (gain, *weights)],
            out_specs=whole(out),
        ),
        out_shape=jax.ShapeDtypeStruct(out, BF16),
        compiler_params=params(),
        cost_estimate=cost(out[0] * out[1] * out[2], 4 * out[0] * out[1] * out[2]),
        name="fold",
    )(places, gain, *weights)


def gradients_kernel(widths, at_ref, gain_ref, grad_ref, *refs):
    count = len(widths)
    weights, outs, gain_out = refs[:count], refs[count : 2 * count], refs[2 * count]
    gain = gain_ref[...]
    total = jnp.zeros(gain.shape, F32)
    for m in range(TEAM):
        at = 0
        for n, w_ref, out_ref in zip(widths, weights, outs):
            g = grad_ref[at_ref[m], :, at : at + n].astype(F32)
            here = slice(m * n, (m + 1) * n)
            total = total + jnp.sum(w_ref[:, here].astype(F32) * g, axis=1, keepdims=True)
            out_ref[:, here] = g * gain
            at += n
    gain_out[...] = jnp.broadcast_to(total, (total.shape[0], 128)).T[:1]


def gradients(places, gain, grad, weights):
    widths = tuple(w.shape[1] // TEAM for w in weights)
    outs = [w.shape for w in weights] + [(1, gain.shape[0])]
    return pl.pallas_call(
        functools.partial(gradients_kernel, widths),
        grid_spec=pltpu.PrefetchScalarGridSpec(
            num_scalar_prefetch=1,
            grid=(1,),
            in_specs=[whole(t.shape) for t in (gain, grad, *weights)],
            out_specs=tuple(whole(shape) for shape in outs),
        ),
        out_shape=tuple(jax.ShapeDtypeStruct(shape, F32) for shape in outs),
        compiler_params=params(SMALL_BYTES),
        cost_estimate=cost(4 * grad.size, 8 * grad.size),
        name="gradients",
    )(places, gain, grad, *weights)


def ring_sum(blocks):
    n, here = lax.axis_size("ctx"), lax.axis_index("ctx")
    total = lax.dynamic_index_in_dim(blocks, here, 0, False).astype(F32)
    for s in range(1, n):
        block = lax.dynamic_index_in_dim(blocks, (here + s) % n, 0, False)
        total = total + lax.ppermute(block, "ctx", [(i, (i + s) % n) for i in range(n)]).astype(F32)
    return total


def chip_mates(evens):
    pieces = []
    for even in evens:
        pieces += [even, swap(even, 1)]
    return pieces


def tie(*values):
    leaves, tree = jax.tree.flatten(values)
    return jax.tree.unflatten(tree, lax.optimization_barrier(leaves))


def mates_trade(parts):
    evens, odds = (parts[0], parts[2]), (swap(parts[1], 1), swap(parts[3], 1))
    return (evens[0], odds[0]), mates_sum(evens, odds)


def chip_sums(blocks):
    n = lax.axis_size("dp")
    groups = [list(range(f + c, f + TEAM, 2)) for f in range(0, n, TEAM) for c in range(2)]
    return lax.all_to_all(blocks, "dp", 0, 0, axis_index_groups=groups, tiled=True)


def hop(sums):
    return [swap(r, bit) for r, bit in zip(sums, (2, 4, 6))]


def total_of(own, got):
    total = own[0][0].astype(F32) + own[1][0].astype(F32)
    for part in got:
        total = total + part.astype(F32)
    return total


def place_rows(seq_rows, order, half_rows):
    slots = seq_rows // half_rows
    hit = slots[:, None] == jnp.arange(order.shape[0], dtype=jnp.int32)[None, :]
    return jnp.sum(jnp.where(hit, order[None, :], 0), axis=1) * half_rows + seq_rows % half_rows


def angles(places):
    freqs = THETA ** (-(jnp.arange(HALF).astype(F32) * 2.0 / HEAD_DIM))
    return places.astype(F32)[:, None] * freqs[None, :]


def member_columns(own):
    return lax.all_to_all(own, "dp", 0, 0, tiled=True)


def any_columns(own, index):
    n_dp, n_ctx = lax.axis_size("dp"), lax.axis_size("ctx")
    gathered = lax.all_gather(own, ("dp", "ctx"), axis=0)
    mine = lax.dynamic_index_in_dim(gathered, index, 1, False)
    per = n_dp // TEAM
    mine = mine.reshape(TEAM, n_ctx, per * own.shape[1], own.shape[2])
    return jnp.transpose(mine, (1, 0, 2, 3))


def by_rows(columns):
    return jnp.transpose(columns, (1, 0, 2, 3)).reshape(-1, columns.shape[-1])


def any_rows(own):
    gathered = lax.all_gather(own, ("dp", "ctx"), axis=0, tiled=True)
    count = gathered.shape[0] // TEAM
    return lax.dynamic_slice_in_dim(gathered, (lax.axis_index("dp") % TEAM) * count, count, 0)


def column_blocks(grad):
    n_dp, n_ctx = lax.axis_size("dp"), lax.axis_size("ctx")
    rows_all, width = grad.shape
    blocks = grad.astype(BF16).reshape(TEAM, n_ctx, rows_all // (n_dp * n_ctx), width)
    return jnp.transpose(blocks, (1, 0, 2, 3))


def columns_home(part):
    return lax.all_to_all(part.astype(BF16), "dp", 0, 0, tiled=True)


def columns_out(grad, index):
    hit = (jnp.arange(TEAM) == index)[None, :, None]
    spread = jnp.where(hit, grad.astype(BF16)[:, None, :], jnp.zeros((), BF16))
    out = lax.psum_scatter(spread, ("dp", "ctx"), scatter_dimension=0, tiled=True)
    return jnp.transpose(out, (1, 0, 2))


def rows_out(grad):
    grad = grad.astype(BF16)
    if lax.axis_size("dp") == TEAM:
        return lax.psum_scatter(grad, "ctx", scatter_dimension=0, tiled=True).astype(F32)
    member = lax.axis_index("dp") % TEAM
    hit = (jnp.arange(TEAM) == member)[:, None, None]
    spread = jnp.where(hit, grad[None], jnp.zeros((), BF16)).reshape(-1, grad.shape[1])
    return lax.psum_scatter(spread, ("dp", "ctx"), scatter_dimension=0, tiled=True).astype(F32)


def across(value):
    return lax.all_to_all(value, "ctx", 0, 0, tiled=True)


def ctx_gather(own):
    return across(jnp.broadcast_to(own, (lax.axis_size("ctx"), *own.shape)))


def flat(value):
    return value.reshape(-1, value.shape[-1])


def norm_back(e, xhat, r):
    return r * (e - xhat * jnp.mean(e * xhat, axis=-1, keepdims=True))


def local(
    tokens, cotangent, gain_attn, w_query, w_key, w_value, w_out, gain_ffn, w_gate, w_up, w_down, order
):
    _, span, width = tokens.shape
    n_ctx = lax.axis_size("ctx")
    rows = w_query.shape[0]
    length = span * n_ctx
    half_rows = span // 2
    scale = HEAD_DIM**-0.5

    gain_a = gain_attn.astype(F32)[:, None]
    gain_f = gain_ffn.astype(F32)[:, None]
    mates = TEAM // n_ctx
    here = lax.axis_index("dp") % TEAM
    mate = here % mates
    ids = jnp.arange(TEAM, dtype=jnp.int32)
    place_of = lambda head: head // mates * mates + (head % mates ^ mate)
    member, head_at = here ^ ids, place_of(ids)
    member_at = place_of(member)
    head = lax.axis_index("ctx") * mates + mate
    one_team = lax.axis_size("dp") == TEAM and mates == 2

    storage = jnp.arange(length, dtype=jnp.int32)
    turn = angles(place_rows(storage, order, half_rows))
    sine = jnp.sin(turn)
    tables = (jnp.concatenate([jnp.cos(turn)] * 2, axis=1), jnp.concatenate([-sine, sine], axis=1))
    turn_t = angles(storage).T
    cos_t, sin_t = jnp.cos(turn_t), jnp.sin(turn_t)
    slots = jnp.sum(jnp.where(order[None, :] == jnp.arange(order.shape[0])[:, None], jnp.arange(order.shape[0]), 0), axis=1)
    slots = slots.astype(jnp.int32)

    tok, dy_own = tokens[0], cotangent[0]
    x = tok.astype(F32)
    low_x1 = (x * lax.rsqrt(jnp.mean(x * x, axis=-1, keepdims=True) + EPS)).astype(BF16)
    folded_qkv = fold(head_at if one_team else ids, gain_a, (w_query, w_key, w_value))
    folded_gu = fold(ids, gain_f, (w_gate, w_up))
    if one_team:
        x1 = [lax.all_gather(first_of(tok, w_out), "ctx", axis=0)]
        blocks = folded_qkv.reshape(n_ctx, mates, rows, QKV)
        blocks = jnp.stack([blocks[:, 0], swap(blocks[:, 1], 1)], axis=1)
        piece = across(blocks)
        piece, folded_gu = tie(piece, folded_gu)
        mine_gu = lax.all_to_all(folded_gu, "dp", 0, 0, tiled=True)
        pieces = [piece, swap(piece, 2), swap(piece, 4), swap(piece, 6)]
        wqkv = rows_of(member, pieces)
        packed = lax.all_gather(pack(mine_gu, w_down), "ctx", axis=0)
    else:
        wqkv = by_rows(any_columns(folded_qkv, head))
        wgu = by_rows(any_columns(folded_gu, here)).reshape(TEAM, width // TEAM, -1)
        x1 = [lax.all_gather(low_x1, "ctx", axis=0)]
        wo, wd = any_rows(w_out), any_rows(w_down)
        packed = pack(wgu, wd)[None]

    dy_even = [dy_own, swap(dy_own, 2), swap(dy_own, 4)]
    x1[0], wqkv, tables, dy_even, cos_t, sin_t = tie(x1[0], wqkv, tables, dy_even, cos_t, sin_t)
    if one_team:
        wo = x1[0][:, span:].reshape(QW, width)
    qkv = [qkv_of(x1[0], span, wqkv, tables)]
    if mates == 2:
        theirs, qkv = tie(swap(x1[0], 1), qkv)
        x1.append(theirs)
        qkv.append(qkv_of(theirs, span, wqkv, tables))
    other, lse_other = attend(slots, order, qkv[-1], [])
    heads, lse = (other, lse_other) if mates == 1 else attend(slots, order, qkv[0], [swap(other, 1)])
    dy_even.append(swap(dy_even[0], 6))
    heads, wo = tie(heads, wo)
    wo_all = chip_mates([wo, swap(wo, 2), swap(wo, 4), swap(wo, 6)])
    dy_all = stack(ids, chip_mates(dy_even))
    traded = across(heads)
    traded, wo_all, dy_all = tie(traded, wo_all, dy_all)

    traded = traded.reshape(TEAM, *traded.shape[2:])
    middle, top, low = middle_of(member_at, tok, traded, wo_all)
    even_a = [top, swap(top, 2), swap(top, 4)]
    even_a.append(swap(top, 6))
    x2_a = chip_mates(even_a)
    x2_a, low = tie(x2_a, low)
    even_b = [low, swap(low, 2), swap(low, 4), swap(low, 6)]
    *parts_a, hidden, dgu, x2_all = feed(0, x2_a, dy_all, packed, None)
    even_b, parts_a, hidden, dgu, x2_all = tie(even_b, parts_a, hidden, dgu, x2_all)
    odds_a = [swap(parts_a[1], 1), swap(parts_a[3], 1)]
    x2_b = chip_mates(even_b)
    x2_b, odds_a = tie(x2_b, odds_a)
    got_a = chip_sums(mates_all(member, (parts_a[0], parts_a[2]), odds_a))
    *parts_b, hidden, dgu, x2_all = feed(1, x2_b, dy_all, packed, (hidden, dgu, x2_all))
    parts_b, got_a = tie(parts_b, got_a)
    dgu = flat(dgu)
    odds_b = [swap(parts_b[1], 1), swap(parts_b[3], 1)]
    g_gate = mm_tn(flat(x2_all), dgu[:, : dgu.shape[1] // 2]).astype(BF16)
    odds_b, g_gate = tie(odds_b, g_gate)

    got_b = mates_all(member, (parts_b[0], parts_b[2]), odds_b)
    got_b, x2_all, dy_all, hidden = tie(got_b, x2_all, dy_all, hidden)
    got_b = chip_sums(got_b)
    g_up = mm_tn(flat(x2_all), dgu[:, dgu.shape[1] // 2 :]).astype(BF16)
    g_down = mm_tn(flat(hidden), flat(dy_all)).astype(BF16)
    if one_team:
        g_ff = pack_back(g_gate, g_up, g_down)
        g_ff = lax.psum_scatter(g_ff.reshape(-1, g_ff.shape[-1]), "ctx", scatter_dimension=0, tiled=True)
    mixed_parts = parts_of(hidden, packed, width)
    got_b, mixed_parts = tie(got_b, mixed_parts)
    sums = (got_a, got_b)
    d_middle, d_low, d_heads = d_middle_of(member_at, sums, middle, dy_own, wo_all)

    hidden, d_low, d_heads = tie(hidden, d_low, d_heads)
    d_heads = across(d_heads.reshape(n_ctx, mates, *d_heads.shape[1:]))
    mixed_own, mixed_sums = mates_trade(mixed_parts)
    mixed_got = hop(mixed_sums)
    out_parts = grad_out_parts(member_at, traded, d_low)
    d_heads, mixed_got, out_parts = tie(d_heads, mixed_got, out_parts)

    d_other = d_heads if mates == 1 else swap(d_heads[:, 1:], 1)
    d_qkv, more = [attend_back(slots, qkv[-1], d_other, lse_other, cos_t, sin_t)], []
    if mates == 2:
        more = [swap(input_all(d_qkv[0], wqkv), 1)]
        d_qkv = [attend_back(slots, qkv[0], d_heads, lse, cos_t, sin_t), *d_qkv]
    d_qkv, more = tie(d_qkv, more)
    e1 = input_own(d_qkv[0], wqkv, more)
    e1, d_qkv, mixed_got, out_parts = tie(e1, d_qkv, mixed_got, out_parts)
    e1 = lax.psum_scatter(e1, "ctx", scatter_dimension=0)

    mixed = (middle + total_of(mixed_own, mixed_got)).astype(BF16)[None]
    g_qkv = mm_tn(flat(x1[0][:, :span]), flat(d_qkv[0]))
    for a, b in zip(x1[1:], d_qkv[1:]):
        g_qkv = g_qkv + mm_tn(flat(a[:, :span]), flat(b))
    if one_team:
        ff = g_ff.shape[1]
        cut = TEAM * rows
        ways, g_ff, out_parts = tie(pieces_of(member, g_qkv), g_ff, out_parts)
        g_gu = jnp.concatenate([g_ff[:cut].reshape(TEAM, rows, ff), g_ff[cut : 2 * cut].reshape(TEAM, rows, ff)], axis=2)
        g_gu = lax.all_to_all(g_gu, "dp", 0, 0, tiled=True)
        ways = [ways[0], *hop(ways[1:])]
        home = ways[0].astype(F32)
        for way in ways[1:]:
            home = home + way.astype(F32)
        home = home.astype(BF16).reshape(mates, n_ctx, rows, QKV)
        home, g_gu = tie(jnp.stack([home[0], swap(home[1], 1)], axis=1), g_gu)
        home = across(home).reshape(TEAM, rows, QKV)
        out_own, out_sums = mates_trade(out_parts)
        g_out = total_of(out_own, hop(out_sums)).astype(BF16)
        grad_out = ring_sum(g_out.reshape(n_ctx, -1, width))
        down = g_ff[2 * cut :].reshape(width // ff, -1, ff)
        grad_down = jnp.concatenate([down[i] for i in range(width // ff)], axis=1).astype(F32)
    else:
        home = columns_out(g_qkv, head)
        g_gu = columns_out(jnp.concatenate([g_gate, g_up], axis=1), here)
        out_own, out_sums = mates_trade(out_parts)
        grad_down, grad_out = rows_out(g_down), rows_out(total_of(out_own, hop(out_sums)))
    *grads_qkv, gain_a_grad = gradients(head_at if one_team else ids, gain_a, home, (w_query, w_key, w_value))
    *grads_gu, gain_f_grad = gradients(ids, gain_f, g_gu, (w_gate, w_up))
    token_grad = token_gradient(e1, tok, d_middle)
    return (
        mixed,
        token_grad[None],
        gain_a_grad[0],
        *grads_qkv,
        grad_out,
        gain_f_grad[0],
        *grads_gu,
        grad_down,
    )


def solution(mesh):
    act = P("dp", "ctx", None)
    vec = P(("dp", "ctx"))
    mat = P(("dp", "ctx"), None)
    return jax.shard_map(
        local,
        mesh=mesh,
        in_specs=(act, act, vec, mat, mat, mat, mat, vec, mat, mat, mat, P()),
        out_specs=(act, act, vec, mat, mat, mat, mat, vec, mat, mat, mat),
        check_vma=False,
    )
```

```python
import functools

import jax
import jax.numpy as jnp
from jax import lax
from jax.experimental import pallas as pl
from jax.experimental.pallas import tpu as pltpu
from jax.sharding import PartitionSpec as P

HEADS = 16
KV_HEADS = 8
HEAD_DIM = 96
GROUPS = HEADS // KV_HEADS
HALF = HEAD_DIM // 2
QW = GROUPS * HEAD_DIM
QKV = QW + 2 * HEAD_DIM

EPS = 1e-05
THETA = 100000.0
F32 = jnp.float32
BF16 = jnp.bfloat16
CHUNKS = 4
VMEM_BYTES = 56 * 2**20
SMALL_BYTES = 24 * 2**20

TEAM = KV_HEADS
PAIRS = TEAM // 2


def dot(a, b, dims):
    return lax.dot_general(a, b, (dims, ((), ())), preferred_element_type=F32)


def mm(a, b):
    return dot(a, b, ((1,), (0,)))


def mm_nt(a, b):
    return dot(a, b, ((1,), (1,)))


def mm_tn(a, b):
    return dot(a, b, ((0,), (0,)))


def swap(value, bit):
    n = lax.axis_size("dp")
    return lax.ppermute(value, "dp", [(i, i ^ bit) for i in range(n)])


def after(value, *others):
    return lax.optimization_barrier((value, *others))[0]


def params(limit=VMEM_BYTES):
    return pltpu.CompilerParams(vmem_limit_bytes=limit)


def cost(flops, nbytes, exps=0):
    return pl.CostEstimate(flops=int(flops), bytes_accessed=int(nbytes), transcendentals=int(exps))


def whole(shape):
    return pl.BlockSpec(shape, lambda *_: (0,) * len(shape))


def join(even_ref, odd_ref):
    return jnp.concatenate([even_ref[...], odd_ref[...]], axis=0)


def qkv_kernel(x_ref, w_ref, cos_ref, sin_ref, out_ref):
    scale = HEAD_DIM**-0.5
    cosine, sine = cos_ref[...], sin_ref[...]
    cosine = jnp.concatenate([cosine * scale] * GROUPS + [cosine, jnp.ones_like(cosine)], axis=1)
    sine = jnp.concatenate([sine * scale] * GROUPS + [sine, jnp.zeros_like(sine)], axis=1)
    first = lax.broadcasted_iota(jnp.int32, cosine.shape, 1) % HEAD_DIM < HALF
    y = mm(x_ref[0], w_ref[...])
    partner = jnp.where(first, pltpu.roll(y, QKV - HALF, 1), pltpu.roll(y, HALF, 1))
    out_ref[0] = (y * cosine + partner * sine).astype(BF16)


def qkv_of(x, span, w, tables):
    n_ctx, _, width = x.shape
    return pl.pallas_call(
        qkv_kernel,
        grid=(n_ctx,),
        in_specs=[pl.BlockSpec((1, span, width), lambda i: (i, 0, 0)), whole(w.shape)]
        + [pl.BlockSpec((span, HEAD_DIM), lambda i: (i, 0))] * 2,
        out_specs=pl.BlockSpec((1, span, QKV), lambda i: (i, 0, 0)),
        out_shape=jax.ShapeDtypeStruct((n_ctx, span, QKV), BF16),
        compiler_params=params(SMALL_BYTES),
        cost_estimate=cost(2 * n_ctx * span * width * QKV, 2 * n_ctx * span * width + 2 * width * QKV),
        name="qkv",
    )(x, w, *tables)


def first_kernel(x_ref, w_ref, out_ref):
    rows = x_ref.shape[0]
    x = x_ref[...].astype(F32)
    r = lax.rsqrt(jnp.mean(x * x, axis=-1, keepdims=True) + EPS)
    out_ref[:rows] = (x * r).astype(BF16)
    out_ref[rows:] = w_ref[...]


def first_of(x, w):
    out = (x.shape[0] + w.shape[0], x.shape[1])
    return pl.pallas_call(
        first_kernel,
        grid=(1,),
        in_specs=[whole(x.shape), whole(w.shape)],
        out_specs=whole(out),
        out_shape=jax.ShapeDtypeStruct(out, BF16),
        compiler_params=params(SMALL_BYTES),
        cost_estimate=cost(6 * x.size, 4 * out[0] * out[1]),
        name="first",
    )(x, w)


def rows_kernel(member_ref, *refs):
    pieces, out_ref = refs[:-1], refs[-1]
    n_ctx, _, rows, _ = pieces[0].shape
    for p, piece in enumerate(pieces):
        for c in range(n_ctx):
            for j in range(2):
                at = pl.multiple_of((member_ref[2 * p + j] * n_ctx + c) * rows, 16)
                out_ref[pl.ds(at, rows), :] = piece[c, j]


def rows_of(member, pieces):
    n_ctx, two, rows, width = pieces[0].shape
    out = (len(pieces) * n_ctx * two * rows, width)
    return pl.pallas_call(
        rows_kernel,
        grid_spec=pltpu.PrefetchScalarGridSpec(
            num_scalar_prefetch=1,
            grid=(1,),
            in_specs=[whole(t.shape) for t in pieces],
            out_specs=whole(out),
        ),
        out_shape=jax.ShapeDtypeStruct(out, BF16),
        compiler_params=params(SMALL_BYTES),
        cost_estimate=cost(0, 4 * out[0] * out[1]),
        name="rows",
    )(member, *pieces)


def pieces_kernel(member_ref, grad_ref, *out_refs):
    for p, out_ref in enumerate(out_refs):
        for j in range(2):
            out_ref[j] = grad_ref[member_ref[2 * p + j]].astype(BF16)


def pieces_of(member, grad):
    rows, width = grad.shape[0] // TEAM, grad.shape[1]
    return pl.pallas_call(
        pieces_kernel,
        grid_spec=pltpu.PrefetchScalarGridSpec(
            num_scalar_prefetch=1,
            grid=(1,),
            in_specs=[whole((TEAM, rows, width))],
            out_specs=(whole((2, rows, width)),) * PAIRS,
        ),
        out_shape=(jax.ShapeDtypeStruct((2, rows, width), BF16),) * PAIRS,
        compiler_params=params(SMALL_BYTES),
        cost_estimate=cost(0, 6 * grad.size),
        name="pieces",
    )(member, grad.reshape(TEAM, rows, width))


def stack_kernel(order_ref, *refs):
    for k, ref in enumerate(refs[:-1]):
        refs[-1][order_ref[k]] = ref[...]


def stack(order, xs):
    rows, width = xs[0].shape
    steps = 4
    block = rows // steps
    return pl.pallas_call(
        stack_kernel,
        grid_spec=pltpu.PrefetchScalarGridSpec(
            num_scalar_prefetch=1,
            grid=(steps,),
            in_specs=[pl.BlockSpec((block, width), lambda i, m: (i, 0))] * len(xs),
            out_specs=pl.BlockSpec((len(xs), block, width), lambda i, m: (0, i, 0)),
        ),
        out_shape=jax.ShapeDtypeStruct((len(xs), rows, width), BF16),
        compiler_params=params(),
        cost_estimate=cost(0, 4 * len(xs) * rows * width),
        name="stack",
    )(order, *xs)


def in_order(slots_ref, ref, scratch, half):
    for b in range(slots_ref.shape[0]):
        slot = slots_ref[b]
        at = pl.multiple_of((slot % 2) * half, half)
        scratch[pl.ds(b * half, half), :] = ref[slot // 2, pl.ds(at, half), :]


def heads_in_order(slots_ref, ref, scratch, half):
    for b in range(slots_ref.shape[0]):
        slot = slots_ref[b]
        first, second = ref[slot // 2, 0, :, :QW], ref[slot // 2, 0, :, QW:]
        scratch[pl.ds(b * half, half), :] = jnp.where(slot % 2 == 0, first, second)


def heads_out_of_order(order_ref, ref, scratch, half):
    for c in range(ref.shape[0]):
        for j in range(2):
            at = pl.multiple_of(order_ref[2 * c + j] * half, half)
            ref[c, 0, :, j * QW : (j + 1) * QW] = scratch[pl.ds(at, half), :]


def out_of_order(slots_ref, ref, first, value, half):
    for b in range(value.shape[0] // half):
        slot = slots_ref[first // half + b]
        at = pl.multiple_of((slot % 2) * half, half)
        ref[slot // 2, pl.ds(at, half), :] = value[b * half : (b + 1) * half]


def flip(value):
    return value.astype(F32).T


def stacked_heads(ref, rows):
    return jnp.concatenate([ref[rows, g * HEAD_DIM : (g + 1) * HEAD_DIM] for g in range(GROUPS)], axis=0)


def causal(size):
    key = lax.broadcasted_iota(jnp.int32, (size, GROUPS * size), 0)
    query = lax.broadcasted_iota(jnp.int32, (size, GROUPS * size), 1) % size
    return key <= query


def attend_kernel(slots_ref, order_ref, qkv_ref, *refs):
    more, (out_ref, lse_ref, scratch, o_scr) = refs[:-4], refs[-4:]
    half = qkv_ref.shape[1] // 2
    size = scratch.shape[0] // CHUNKS
    in_order(slots_ref, qkv_ref, scratch, half)
    v_t = flip(scratch[:, QW + HEAD_DIM :]).astype(BF16)
    allowed = causal(size)
    for i in range(CHUNKS):
        lo, hi = i * size, (i + 1) * size
        q = stacked_heads(scratch, slice(lo, hi))
        k_near = scratch[lo:hi, QW : QW + HEAD_DIM]
        near = jnp.where(allowed, mm_nt(k_near, q), -1e30)
        top = jnp.max(near, axis=0, keepdims=True)
        if i > 0:
            far = mm_nt(scratch[:lo, QW : QW + HEAD_DIM], q)
            top = jnp.maximum(top, jnp.max(far, axis=0, keepdims=True))
        near = jnp.exp(near - top)
        total = jnp.sum(near, axis=0, keepdims=True)
        acc = mm(v_t[:, lo:hi], near.astype(BF16))
        if i > 0:
            far = jnp.exp(far - top)
            total = total + jnp.sum(far, axis=0, keepdims=True)
            acc = acc + mm(v_t[:, :lo], far.astype(BF16))
        lse_ref[pl.ds(i, 1), :] = top + jnp.log(total)
        o = (acc / total).T.astype(BF16)
        for g in range(GROUPS):
            o_scr[lo:hi, g * HEAD_DIM : (g + 1) * HEAD_DIM] = o[g * size : (g + 1) * size]
    heads_out_of_order(order_ref, out_ref, o_scr, half)
    for ref in more:
        out_ref[:, 1] = ref[:, 0]


def attend_back_kernel(slots_ref, qkv_ref, do_ref, lse_ref, cos_ref, sin_ref, out_ref, scratch, do_scr, dk_scr, dv_scr):
    half = qkv_ref.shape[1] // 2
    length = scratch.shape[0]
    size = length // CHUNKS
    scale = HEAD_DIM**-0.5
    in_order(slots_ref, qkv_ref, scratch, half)
    heads_in_order(slots_ref, do_ref, do_scr, half)
    k_t = flip(scratch[:, QW : QW + HEAD_DIM]).astype(BF16)
    allowed = causal(size)
    dk_scr[...] = jnp.zeros_like(dk_scr)
    dv_scr[...] = jnp.zeros_like(dv_scr)
    for i in range(CHUNKS):
        lo, hi = i * size, (i + 1) * size
        q = stacked_heads(scratch, slice(lo, hi))
        do = stacked_heads(do_scr, slice(lo, hi))
        lse = lse_ref[pl.ds(i, 1), :]
        spans = [(lo, hi)] + ([(0, lo)] if i > 0 else [])
        probs, prods = [], []
        delta = 0.0
        for at, (a, b) in enumerate(spans):
            p = jnp.exp(mm_nt(scratch[a:b, QW : QW + HEAD_DIM], q) - lse)
            if at == 0:
                p = jnp.where(allowed, p, 0.0)
            prod = p * mm_nt(scratch[a:b, QW + HEAD_DIM :], do)
            delta = delta + jnp.sum(prod, axis=0, keepdims=True)
            probs.append(p)
            prods.append(prod)
        dq_t = 0.0
        for (a, b), p, prod in zip(spans, probs, prods):
            ds = (prod - p * delta).astype(BF16)
            dk_scr[a:b, :] += mm(ds, q)
            dv_scr[a:b, :] += mm(p.astype(BF16), do)
            dq_t = dq_t + mm(k_t[:, a:b], ds)
        c = jnp.concatenate([cos_ref[:, lo:hi]] * GROUPS, axis=1) * scale
        s = jnp.concatenate([sin_ref[:, lo:hi]] * GROUPS, axis=1) * scale
        first, second = dq_t[:HALF], dq_t[HALF:]
        dq = jnp.concatenate([first * c + second * s, second * c - first * s], axis=0).T
        for g in range(GROUPS):
            do_scr[lo:hi, g * HEAD_DIM : (g + 1) * HEAD_DIM] = dq[g * size : (g + 1) * size].astype(BF16)
    for i in range(CHUNKS):
        lo, hi = i * size, (i + 1) * size
        dk_t = dk_scr[lo:hi, :].T
        first, second = dk_t[:HALF], dk_t[HALF:]
        c, s = cos_ref[:, lo:hi], sin_ref[:, lo:hi]
        dk = jnp.concatenate([first * c + second * s, second * c - first * s], axis=0).T
        value = jnp.concatenate([do_scr[lo:hi, :], dk.astype(BF16), dv_scr[lo:hi, :].astype(BF16)], axis=1)
        out_of_order(slots_ref, out_ref, lo, value, half)


def attend(slots, order, qkv, more):
    n_ctx, span, _ = qkv.shape
    length = n_ctx * span
    heads = (n_ctx, 1 + len(more), span // 2, 2 * QW)
    lse = (CHUNKS, GROUPS * length // CHUNKS)
    work = GROUPS * length * length
    return pl.pallas_call(
        attend_kernel,
        grid_spec=pltpu.PrefetchScalarGridSpec(
            num_scalar_prefetch=2,
            grid=(1,),
            in_specs=[whole(t.shape) for t in (qkv, *more)],
            out_specs=(whole(heads), whole(lse)),
            scratch_shapes=[pltpu.VMEM((length, QKV), BF16), pltpu.VMEM((length, QW), BF16)],
        ),
        out_shape=(jax.ShapeDtypeStruct(heads, BF16), jax.ShapeDtypeStruct(lse, F32)),
        compiler_params=params(SMALL_BYTES),
        cost_estimate=cost(work * 2 * HEAD_DIM * 3, 2 * length * (QKV + QW), work // 2),
        name="attend",
    )(slots, order, qkv, *more)


def attend_back(slots, qkv, d_heads, lse, cos_t, sin_t):
    n_ctx, span, _ = qkv.shape
    length = n_ctx * span
    work = GROUPS * length * length
    return pl.pallas_call(
        attend_back_kernel,
        grid_spec=pltpu.PrefetchScalarGridSpec(
            num_scalar_prefetch=1,
            grid=(1,),
            in_specs=[
                whole(qkv.shape),
                whole((n_ctx, 1, *d_heads.shape[2:])),
            ]
            + [whole(t.shape) for t in (lse, cos_t, sin_t)],
            out_specs=whole((n_ctx, span, QKV)),
            scratch_shapes=[
                pltpu.VMEM((length, QKV), BF16),
                pltpu.VMEM((length, QW), BF16),
                pltpu.VMEM((length, HEAD_DIM), F32),
                pltpu.VMEM((length, HEAD_DIM), F32),
            ],
        ),
        out_shape=jax.ShapeDtypeStruct((n_ctx, span, QKV), BF16),
        compiler_params=params(SMALL_BYTES),
        cost_estimate=cost(work * 2 * HEAD_DIM * 8, 4 * length * QKV, work // 2),
        name="attend_back",
    )(slots, qkv, d_heads, lse, cos_t, sin_t)


def parts_kernel(a_ref, packed, *refs):
    out_refs, (wd_ref, sem) = refs[:4], refs[4:]

    @pl.when(pl.program_id(0) == 0)
    def _():
        copies = [pltpu.make_async_copy(src, dst, sem.at[i]) for i, (src, dst) in enumerate(down_ways(packed, wd_ref))]
        for copy in copies:
            copy.start()
        for copy in copies:
            copy.wait()

    block = a_ref.shape[1]
    y = mm(jnp.concatenate([a_ref[k] for k in range(TEAM)], axis=0), wd_ref[...]).astype(BF16)
    for k in range(TEAM):
        out_refs[k // 4 * 2 + k % 2][k // 2 % 2] = y[k * block : (k + 1) * block]


def parts_of(a, packed, width):
    _, rows, depth = a.shape
    steps = 4
    block = rows // steps
    return pl.pallas_call(
        parts_kernel,
        grid=(steps,),
        in_specs=[pl.BlockSpec((TEAM, block, depth), lambda i: (0, i, 0)), pl.BlockSpec(memory_space=pl.ANY)],
        out_specs=(pl.BlockSpec((2, block, width), lambda i: (0, i, 0)),) * 4,
        out_shape=(jax.ShapeDtypeStruct((2, rows, width), BF16),) * 4,
        scratch_shapes=[
            pltpu.VMEM((depth, width), BF16),
            pltpu.SemaphoreType.DMA((packed.shape[0] * (width // depth),)),
        ],
        compiler_params=params(SMALL_BYTES),
        cost_estimate=cost(2 * TEAM * rows * depth * width, 2 * TEAM * rows * (width + depth) + 2 * depth * width),
        name="parts",
    )(a, packed)


def input_own_kernel(a_ref, w_ref, *refs):
    y = mm_nt(a_ref[0], w_ref[...])
    for ref in refs[:-1]:
        y = y + ref[0].astype(F32)
    refs[-1][0] = y.astype(BF16)


def input_own(a, w, more):
    n_ctx, span, depth = a.shape
    width = w.shape[0]
    blocked = lambda n: pl.BlockSpec((1, span, n), lambda i: (i, 0, 0))
    return pl.pallas_call(
        input_own_kernel,
        grid=(n_ctx,),
        in_specs=[blocked(depth), whole(w.shape)] + [blocked(width)] * len(more),
        out_specs=blocked(width),
        out_shape=jax.ShapeDtypeStruct((n_ctx, span, width), BF16),
        compiler_params=params(SMALL_BYTES),
        cost_estimate=cost(2 * n_ctx * span * depth * width, 4 * n_ctx * span * (width + depth) + 2 * depth * width),
        name="input_own",
    )(a, w, *more)


def input_all_kernel(a_ref, w_ref, out_ref):
    out_ref[0] = mm_nt(a_ref[0], w_ref[...]).astype(BF16)


def input_all(a, w):
    n_ctx, span, depth = a.shape
    width = w.shape[0]
    blocked = lambda n: pl.BlockSpec((1, span, n), lambda i: (i, 0, 0))
    return pl.pallas_call(
        input_all_kernel,
        grid=(n_ctx,),
        in_specs=[blocked(depth), whole(w.shape)],
        out_specs=blocked(width),
        out_shape=jax.ShapeDtypeStruct((n_ctx, span, width), BF16),
        compiler_params=params(SMALL_BYTES),
        cost_estimate=cost(2 * n_ctx * span * depth * width, 4 * n_ctx * span * (width + depth) + 2 * depth * width),
        name="input_all",
    )(a, w)


def grad_out_kernel(at_ref, heads_ref, dm_ref, *out_refs):
    dm = dm_ref[...]
    for k in range(TEAM):
        y = mm_tn(unfold(heads_ref[at_ref[k]]), dm)
        out_refs[k // 4 * 2 + k % 2][k // 2 % 2] = y.astype(BF16)


def grad_out_parts(member_at, heads, dm):
    rows, width = dm.shape
    return pl.pallas_call(
        grad_out_kernel,
        grid_spec=pltpu.PrefetchScalarGridSpec(
            num_scalar_prefetch=1,
            grid=(1,),
            in_specs=[whole(t.shape) for t in (heads, dm)],
            out_specs=(whole((2, QW, width)),) * 4,
        ),
        out_shape=(jax.ShapeDtypeStruct((2, QW, width), BF16),) * 4,
        compiler_params=params(),
        cost_estimate=cost(2 * TEAM * rows * QW * width, 2 * TEAM * QW * width),
        name="grad_out",
    )(member_at, heads, dm)


def unfold(block):
    return jnp.concatenate([block[:, :QW], block[:, QW:]], axis=0)


def fetch(any_refs, ref, sem):
    copies = [pltpu.make_async_copy(a, ref.at[k], sem.at[k]) for k, a in enumerate(any_refs)]
    for copy in copies:
        copy.start()
    return copies


def fetched(arrays):
    specs = [pl.BlockSpec(memory_space=pl.ANY)] * len(arrays)
    scratch = [pltpu.VMEM((len(arrays), *arrays[0].shape), BF16), pltpu.SemaphoreType.DMA((len(arrays),))]
    return specs, scratch


def middle_kernel(at_ref, heads_ref, x_ref, *refs):
    wo_any, (middle_ref, top_ref, low_ref, wo_ref, sem) = refs[:TEAM], refs[TEAM:]
    copies = fetch(wo_any, wo_ref, sem)
    heads = jnp.concatenate([unfold(heads_ref[at_ref[k]]) for k in range(TEAM)], axis=1)
    for copy in copies:
        copy.wait()
    acc = x_ref[...].astype(F32) + mm(heads, wo_ref[...].reshape(heads.shape[1], -1))
    middle_ref[...] = acc
    r = lax.rsqrt(jnp.mean(acc * acc, axis=-1, keepdims=True) + EPS)
    xhat = (acc * r).astype(BF16)
    half = top_ref.shape[0]
    top_ref[...] = xhat[:half]
    low_ref[...] = xhat[half:]


def middle_of(member_at, x, heads, wo):
    rows, width = x.shape
    specs, scratch = fetched(wo)
    return pl.pallas_call(
        middle_kernel,
        grid_spec=pltpu.PrefetchScalarGridSpec(
            num_scalar_prefetch=1,
            grid=(1,),
            in_specs=[whole(t.shape) for t in (heads, x)] + specs,
            out_specs=(whole(x.shape),) + (whole((rows // 2, width)),) * 2,
            scratch_shapes=scratch,
        ),
        out_shape=(jax.ShapeDtypeStruct(x.shape, F32),) + (jax.ShapeDtypeStruct((rows // 2, width), BF16),) * 2,
        compiler_params=params(),
        cost_estimate=cost(2 * rows * width * TEAM * QW, 2 * width * TEAM * QW + 12 * rows * width),
        name="middle",
    )(member_at, heads, x, *wo)


def d_middle_kernel(at_ref, *refs):
    middle_ref, dy_ref = refs[2:4]
    wo_any, (d_ref, low_ref, out_ref, wo_ref, sem) = refs[4 : 4 + TEAM], refs[4 + TEAM :]
    copies = fetch(wo_any, wo_ref, sem)
    middle = middle_ref[...]
    half = middle.shape[0] // 2
    r = lax.rsqrt(jnp.mean(middle * middle, axis=-1, keepdims=True) + EPS)
    d = dy_ref[...].astype(F32) + norm_back(team_total(refs[:2]), middle * r, r)
    d_ref[...] = d
    low = d.astype(BF16)
    low_ref[...] = low
    for copy in copies:
        copy.wait()
    y = mm_nt(low, wo_ref[...].reshape(TEAM * QW, -1)).astype(BF16)
    for k in range(TEAM):
        part = slice(k * QW, (k + 1) * QW)
        out_ref[at_ref[k], :, :QW] = y[:half, part]
        out_ref[at_ref[k], :, QW:] = y[half:, part]


def d_middle_of(member_at, sums, middle, dy, wo):
    rows, width = dy.shape
    heads = (TEAM, rows // 2, 2 * QW)
    specs, scratch = fetched(wo)
    return pl.pallas_call(
        d_middle_kernel,
        grid_spec=pltpu.PrefetchScalarGridSpec(
            num_scalar_prefetch=1,
            grid=(1,),
            in_specs=[whole(t.shape) for t in (*sums, middle, dy)] + specs,
            out_specs=(whole(dy.shape), whole(dy.shape), whole(heads)),
            scratch_shapes=scratch,
        ),
        out_shape=(
            jax.ShapeDtypeStruct(dy.shape, F32),
            jax.ShapeDtypeStruct(dy.shape, BF16),
            jax.ShapeDtypeStruct(heads, BF16),
        ),
        compiler_params=params(),
        cost_estimate=cost(2 * rows * width * TEAM * QW, 2 * width * TEAM * QW + 18 * rows * width),
        name="d_middle",
    )(member_at, *sums, middle, dy, *wo)


def mates_kernel(*refs):
    evens, odds, outs = refs[:2], refs[2:4], refs[4:]
    for j, k in enumerate((2, 4, 6)):
        r = evens[k // 4][k // 2 % 2].astype(F32) + odds[k // 4][k // 2 % 2].astype(F32)
        outs[j][...] = r.astype(BF16)


def mates_sum(evens, odds):
    _, rows, width = evens[0].shape
    steps = 2
    block = rows // steps
    return pl.pallas_call(
        mates_kernel,
        grid=(steps,),
        in_specs=[pl.BlockSpec((2, block, width), lambda i: (0, i, 0))] * 4,
        out_specs=(pl.BlockSpec((block, width), lambda i: (i, 0)),) * 3,
        out_shape=(jax.ShapeDtypeStruct((rows, width), BF16),) * 3,
        compiler_params=params(SMALL_BYTES),
        cost_estimate=cost(6 * rows * width, 36 * rows * width),
        name="mates_sum",
    )(*evens, *odds)


def mates_all_kernel(member_ref, *refs):
    evens, odds, out_ref = refs[:2], refs[2:4], refs[4]
    for k in (0, 2, 4, 6):
        r = evens[k // 4][k // 2 % 2].astype(F32) + odds[k // 4][k // 2 % 2].astype(F32)
        out_ref[member_ref[k] // 2] = r.astype(BF16)


def mates_all(member, evens, odds):
    _, rows, width = evens[0].shape
    steps = 2
    block = rows // steps
    return pl.pallas_call(
        mates_all_kernel,
        grid_spec=pltpu.PrefetchScalarGridSpec(
            num_scalar_prefetch=1,
            grid=(steps,),
            in_specs=[pl.BlockSpec((2, block, width), lambda i, m: (0, i, 0))] * 4,
            out_specs=pl.BlockSpec((PAIRS, block, width), lambda i, m: (0, i, 0)),
        ),
        out_shape=jax.ShapeDtypeStruct((PAIRS, rows, width), BF16),
        compiler_params=params(SMALL_BYTES),
        cost_estimate=cost(8 * rows * width, 48 * rows * width),
        name="mates_all",
    )(member, *evens, *odds)


def team_total(refs):
    return jnp.concatenate([jnp.sum(ref[...].astype(F32), axis=0) for ref in refs], axis=0)


def token_kernel(e_ref, x_ref, d_ref, out_ref):
    x = x_ref[...].astype(F32)
    r = lax.rsqrt(jnp.mean(x * x, axis=-1, keepdims=True) + EPS)
    out_ref[...] = d_ref[...] + norm_back(e_ref[...].astype(F32), x * r, r)


def token_gradient(e, x, d_middle):
    rows, width = x.shape
    block = rows // 2
    return pl.pallas_call(
        token_kernel,
        grid=(2,),
        in_specs=[pl.BlockSpec((block, width), lambda i: (i, 0))] * 3,
        out_specs=pl.BlockSpec((block, width), lambda i: (i, 0)),
        out_shape=jax.ShapeDtypeStruct(x.shape, F32),
        compiler_params=params(),
        cost_estimate=cost(12 * x.size, 20 * x.size),
        name="token_gradient",
    )(e, x, d_middle)


def pack(gate_up, down):
    _, rows, twice = gate_up.shape
    ff = twice // 2
    blocks = [gate_up[..., :ff].reshape(-1, ff), gate_up[..., ff:].reshape(-1, ff)]
    return jnp.concatenate(blocks + [down[:, i : i + ff] for i in range(0, down.shape[1], ff)], axis=0)


def pack_back(gate, up, down):
    n = lax.axis_size("ctx")
    width, ff = gate.shape
    by_ctx = lambda g: jnp.transpose(g.reshape(TEAM, n, -1, ff), (1, 0, 2, 3)).reshape(n, -1, ff)
    blocks = [by_ctx(gate), by_ctx(up)]
    down = down.reshape(n, ff // n, width)
    return jnp.concatenate(blocks + [down[..., i : i + ff] for i in range(0, width, ff)], axis=1)


def down_ways(packed, wd_ref):
    n_ctx, count, ff = packed.shape
    width = wd_ref.shape[1]
    down = ff // n_ctx
    first = count - width // ff * down
    return [
        (packed.at[c, pl.ds(first + i * down, down)], wd_ref.at[pl.ds(c * down, down), pl.ds(i * ff, ff)])
        for c in range(n_ctx)
        for i in range(width // ff)
    ]


def unpack(packed, wgu_ref, wd_ref, sem):
    n_ctx, _, ff = packed.shape
    rows = wgu_ref.shape[0] // (TEAM * n_ctx)
    ways = []
    for part in range(2):
        for c in range(n_ctx):
            for m in range(TEAM):
                out = wgu_ref.at[pl.ds((m * n_ctx + c) * rows, rows), pl.ds(part * ff, ff)]
                ways.append((packed.at[c, pl.ds((part * TEAM + m) * rows, rows)], out))
    ways += down_ways(packed, wd_ref)
    copies = [pltpu.make_async_copy(src, dst, sem.at[i]) for i, (src, dst) in enumerate(ways)]
    for copy in copies:
        copy.start()
    return copies


def feed_kernel(*refs):
    x_refs = refs[:TEAM]
    y_ref, packed = refs[TEAM : TEAM + 2]
    even0_ref, odd0_ref, even1_ref, odd1_ref, hidden_ref, dgu_ref, xc_ref, wgu_ref, wd_ref, sem = refs[-10:]
    ff = wd_ref.shape[0]
    block = x_refs[0].shape[0]

    @pl.when(pl.program_id(0) == 0)
    def _():
        for copy in unpack(packed, wgu_ref, wd_ref, sem):
            copy.wait()

    for j in range(TEAM):
        xc_ref[j] = x_refs[j][...]
    x = jnp.concatenate([ref[...] for ref in x_refs], axis=0)
    y = y_ref[...].reshape(TEAM * block, y_ref.shape[2])
    gate = mm(x, wgu_ref[:, :ff])
    upper = mm(x, wgu_ref[:, ff:])
    d_hidden = mm_nt(y, wd_ref[...])
    sigma = jax.nn.sigmoid(gate)
    act = gate * sigma
    hidden = (act * upper).astype(BF16)
    d_gate = (d_hidden * upper * sigma * (1.0 + gate * (1.0 - sigma))).astype(BF16)
    dgu = jnp.concatenate([d_gate, (d_hidden * act).astype(BF16)], axis=1)
    e = mm_nt(dgu, wgu_ref[...]).astype(BF16)
    outs = (even0_ref, odd0_ref, even1_ref, odd1_ref)
    for j in range(TEAM):
        part = slice(j * block, (j + 1) * block)
        hidden_ref[j] = hidden[part]
        dgu_ref[j] = dgu[part]
        outs[j // 4 * 2 + j % 2][j // 2 % 2] = e[part]


def feed(part, xs, y, packed, held):
    rows, width = xs[0].shape
    n_ctx, packed_rows, ff = packed.shape
    steps = 4
    block = rows // steps
    widths = (ff, 2 * ff, width)
    extra = [] if held is None else list(held)
    at_part = lambda n: pl.BlockSpec((TEAM, block, n), lambda i: (0, part * steps + i, 0))
    return pl.pallas_call(
        feed_kernel,
        grid=(steps,),
        in_specs=[pl.BlockSpec((block, width), lambda i: (i, 0))] * TEAM
        + [at_part(width)]
        + [pl.BlockSpec(memory_space=pl.ANY)] * (1 + len(extra)),
        out_specs=(pl.BlockSpec((2, block, width), lambda i: (0, i, 0)),) * 4 + tuple(at_part(n) for n in widths),
        out_shape=(jax.ShapeDtypeStruct((2, rows, width), BF16),) * 4
        + tuple(jax.ShapeDtypeStruct((TEAM, 2 * rows, n), BF16) for n in widths),
        input_output_aliases={TEAM + 2 + i: 4 + i for i in range(len(extra))},
        scratch_shapes=[
            pltpu.VMEM((width, 2 * ff), BF16),
            pltpu.VMEM((ff, width), BF16),
            pltpu.SemaphoreType.DMA((n_ctx * (2 * TEAM + width // ff),)),
        ],
        compiler_params=params(),
        cost_estimate=cost(2 * TEAM * rows * width * 5 * ff, 6 * width * ff + 18 * TEAM * rows * width, TEAM * rows * ff),
        name="feed",
    )(*xs, y, packed, *extra)


def fold_kernel(widths, at_ref, gain_ref, *refs):
    weights, out_ref = refs[:-1], refs[-1]
    gain = gain_ref[...]
    for m in range(TEAM):
        at = 0
        for n, ref in zip(widths, weights):
            out_ref[at_ref[m], :, at : at + n] = (ref[:, m * n : (m + 1) * n].astype(F32) * gain).astype(BF16)
            at += n


def fold(places, gain, weights):
    widths = tuple(w.shape[1] // TEAM for w in weights)
    out = (TEAM, weights[0].shape[0], sum(widths))
    return pl.pallas_call(
        functools.partial(fold_kernel, widths),
        grid_spec=pltpu.PrefetchScalarGridSpec(
            num_scalar_prefetch=1,
            grid=(1,),
            in_specs=[whole(t.shape) for t in (gain, *weights)],
            out_specs=whole(out),
        ),
        out_shape=jax.ShapeDtypeStruct(out, BF16),
        compiler_params=params(),
        cost_estimate=cost(out[0] * out[1] * out[2], 4 * out[0] * out[1] * out[2]),
        name="fold",
    )(places, gain, *weights)


def gradients_kernel(widths, at_ref, gain_ref, grad_ref, *refs):
    count = len(widths)
    weights, outs, gain_out = refs[:count], refs[count : 2 * count], refs[2 * count]
    gain = gain_ref[...]
    total = jnp.zeros(gain.shape, F32)
    for m in range(TEAM):
        at = 0
        for n, w_ref, out_ref in zip(widths, weights, outs):
            g = grad_ref[at_ref[m], :, at : at + n].astype(F32)
            here = slice(m * n, (m + 1) * n)
            total = total + jnp.sum(w_ref[:, here].astype(F32) * g, axis=1, keepdims=True)
            out_ref[:, here] = g * gain
            at += n
    gain_out[...] = jnp.broadcast_to(total, (total.shape[0], 128)).T[:1]


def gradients(places, gain, grad, weights):
    widths = tuple(w.shape[1] // TEAM for w in weights)
    outs = [w.shape for w in weights] + [(1, gain.shape[0])]
    return pl.pallas_call(
        functools.partial(gradients_kernel, widths),
        grid_spec=pltpu.PrefetchScalarGridSpec(
            num_scalar_prefetch=1,
            grid=(1,),
            in_specs=[whole(t.shape) for t in (gain, grad, *weights)],
            out_specs=tuple(whole(shape) for shape in outs),
        ),
        out_shape=tuple(jax.ShapeDtypeStruct(shape, F32) for shape in outs),
        compiler_params=params(SMALL_BYTES),
        cost_estimate=cost(4 * grad.size, 8 * grad.size),
        name="gradients",
    )(places, gain, grad, *weights)


def ring_trade(blocks):
    n, here = lax.axis_size("ctx"), lax.axis_index("ctx")
    got = [lax.dynamic_index_in_dim(blocks, here, 0, False)]
    for s in range(1, n):
        block = lax.dynamic_index_in_dim(blocks, (here + s) % n, 0, False)
        got.append(lax.ppermute(block, "ctx", [(i, (i + s) % n) for i in range(n)]))
    return got


def chip_mates(evens):
    pieces = []
    for even in evens:
        pieces += [even, swap(even, 1)]
    return pieces


def tie(*values):
    leaves, tree = jax.tree.flatten(values)
    return jax.tree.unflatten(tree, lax.optimization_barrier(leaves))


def mates_trade(parts):
    evens, odds = (parts[0], parts[2]), (swap(parts[1], 1), swap(parts[3], 1))
    return (evens[0], odds[0]), mates_sum(evens, odds)


def chip_sums(blocks):
    n = lax.axis_size("dp")
    groups = [list(range(f + c, f + TEAM, 2)) for f in range(0, n, TEAM) for c in range(2)]
    return lax.all_to_all(blocks, "dp", 0, 0, axis_index_groups=groups, tiled=True)


def hop(sums):
    return [swap(r, bit) for r, bit in zip(sums, (2, 4, 6))]


def total_of(own, got):
    total = own[0][0].astype(F32) + own[1][0].astype(F32)
    for part in got:
        total = total + part.astype(F32)
    return total


def place_rows(seq_rows, order, half_rows):
    slots = seq_rows // half_rows
    hit = slots[:, None] == jnp.arange(order.shape[0], dtype=jnp.int32)[None, :]
    return jnp.sum(jnp.where(hit, order[None, :], 0), axis=1) * half_rows + seq_rows % half_rows


def angles(places):
    freqs = THETA ** (-(jnp.arange(HALF).astype(F32) * 2.0 / HEAD_DIM))
    return places.astype(F32)[:, None] * freqs[None, :]


def member_columns(own):
    return lax.all_to_all(own, "dp", 0, 0, tiled=True)


def any_columns(own, index):
    n_dp, n_ctx = lax.axis_size("dp"), lax.axis_size("ctx")
    gathered = lax.all_gather(own, ("dp", "ctx"), axis=0)
    mine = lax.dynamic_index_in_dim(gathered, index, 1, False)
    per = n_dp // TEAM
    mine = mine.reshape(TEAM, n_ctx, per * own.shape[1], own.shape[2])
    return jnp.transpose(mine, (1, 0, 2, 3))


def by_rows(columns):
    return jnp.transpose(columns, (1, 0, 2, 3)).reshape(-1, columns.shape[-1])


def any_rows(own):
    gathered = lax.all_gather(own, ("dp", "ctx"), axis=0, tiled=True)
    count = gathered.shape[0] // TEAM
    return lax.dynamic_slice_in_dim(gathered, (lax.axis_index("dp") % TEAM) * count, count, 0)


def column_blocks(grad):
    n_dp, n_ctx = lax.axis_size("dp"), lax.axis_size("ctx")
    rows_all, width = grad.shape
    blocks = grad.astype(BF16).reshape(TEAM, n_ctx, rows_all // (n_dp * n_ctx), width)
    return jnp.transpose(blocks, (1, 0, 2, 3))


def columns_home(part):
    return lax.all_to_all(part.astype(BF16), "dp", 0, 0, tiled=True)


def columns_out(grad, index):
    hit = (jnp.arange(TEAM) == index)[None, :, None]
    spread = jnp.where(hit, grad.astype(BF16)[:, None, :], jnp.zeros((), BF16))
    out = lax.psum_scatter(spread, ("dp", "ctx"), scatter_dimension=0, tiled=True)
    return jnp.transpose(out, (1, 0, 2))


def rows_out(grad):
    grad = grad.astype(BF16)
    if lax.axis_size("dp") == TEAM:
        return lax.psum_scatter(grad, "ctx", scatter_dimension=0, tiled=True).astype(F32)
    member = lax.axis_index("dp") % TEAM
    hit = (jnp.arange(TEAM) == member)[:, None, None]
    spread = jnp.where(hit, grad[None], jnp.zeros((), BF16)).reshape(-1, grad.shape[1])
    return lax.psum_scatter(spread, ("dp", "ctx"), scatter_dimension=0, tiled=True).astype(F32)


def across(value):
    return lax.all_to_all(value, "ctx", 0, 0, tiled=True)


def ctx_gather(own):
    return across(jnp.broadcast_to(own, (lax.axis_size("ctx"), *own.shape)))


def flat(value):
    return value.reshape(-1, value.shape[-1])


def norm_back(e, xhat, r):
    return r * (e - xhat * jnp.mean(e * xhat, axis=-1, keepdims=True))


def local(
    tokens, cotangent, gain_attn, w_query, w_key, w_value, w_out, gain_ffn, w_gate, w_up, w_down, order
):
    _, span, width = tokens.shape
    n_ctx = lax.axis_size("ctx")
    rows = w_query.shape[0]
    length = span * n_ctx
    half_rows = span // 2
    scale = HEAD_DIM**-0.5

    gain_a = gain_attn.astype(F32)[:, None]
    gain_f = gain_ffn.astype(F32)[:, None]
    mates = TEAM // n_ctx
    here = lax.axis_index("dp") % TEAM
    mate = here % mates
    ids = jnp.arange(TEAM, dtype=jnp.int32)
    place_of = lambda head: head // mates * mates + (head % mates ^ mate)
    member, head_at = here ^ ids, place_of(ids)
    member_at = place_of(member)
    head = lax.axis_index("ctx") * mates + mate
    one_team = lax.axis_size("dp") == TEAM and mates == 2

    storage = jnp.arange(length, dtype=jnp.int32)
    turn = angles(place_rows(storage, order, half_rows))
    sine = jnp.sin(turn)
    tables = (jnp.concatenate([jnp.cos(turn)] * 2, axis=1), jnp.concatenate([-sine, sine], axis=1))
    turn_t = angles(storage).T
    cos_t, sin_t = jnp.cos(turn_t), jnp.sin(turn_t)
    slots = jnp.sum(jnp.where(order[None, :] == jnp.arange(order.shape[0])[:, None], jnp.arange(order.shape[0]), 0), axis=1)
    slots = slots.astype(jnp.int32)

    tok, dy_own = tokens[0], cotangent[0]
    x = tok.astype(F32)
    low_x1 = (x * lax.rsqrt(jnp.mean(x * x, axis=-1, keepdims=True) + EPS)).astype(BF16)
    folded_qkv = fold(head_at if one_team else ids, gain_a, (w_query, w_key, w_value))
    folded_gu = fold(ids, gain_f, (w_gate, w_up))
    if one_team:
        x1 = [lax.all_gather(first_of(tok, w_out), "ctx", axis=0)]
        blocks = folded_qkv.reshape(n_ctx, mates, rows, QKV)
        blocks = jnp.stack([blocks[:, 0], swap(blocks[:, 1], 1)], axis=1)
        piece = across(blocks)
        piece, folded_gu = tie(piece, folded_gu)
        mine_gu = lax.all_to_all(folded_gu, "dp", 0, 0, tiled=True)
        pieces = [piece, swap(piece, 2), swap(piece, 4), swap(piece, 6)]
        wqkv = rows_of(member, pieces)
        packed = lax.all_gather(pack(mine_gu, w_down), "ctx", axis=0)
    else:
        wqkv = by_rows(any_columns(folded_qkv, head))
        wgu = by_rows(any_columns(folded_gu, here)).reshape(TEAM, width // TEAM, -1)
        x1 = [lax.all_gather(low_x1, "ctx", axis=0)]
        wo, wd = any_rows(w_out), any_rows(w_down)
        packed = pack(wgu, wd)[None]

    dy_even = [dy_own, swap(dy_own, 2), swap(dy_own, 4)]
    x1[0], wqkv, tables, dy_even, cos_t, sin_t = tie(x1[0], wqkv, tables, dy_even, cos_t, sin_t)
    if one_team:
        wo = x1[0][:, span:].reshape(QW, width)
    qkv = [qkv_of(x1[0], span, wqkv, tables)]
    if mates == 2:
        theirs, qkv = tie(swap(x1[0], 1), qkv)
        x1.append(theirs)
        qkv.append(qkv_of(theirs, span, wqkv, tables))
    other, lse_other = attend(slots, order, qkv[-1], [])
    heads, lse = (other, lse_other) if mates == 1 else attend(slots, order, qkv[0], [swap(other, 1)])
    dy_even.append(swap(dy_even[0], 6))
    heads, wo = tie(heads, wo)
    wo_all = chip_mates([wo, swap(wo, 2), swap(wo, 4), swap(wo, 6)])
    dy_all = stack(ids, chip_mates(dy_even))
    traded = across(heads)
    traded, wo_all, dy_all = tie(traded, wo_all, dy_all)

    traded = traded.reshape(TEAM, *traded.shape[2:])
    middle, top, low = middle_of(member_at, tok, traded, wo_all)
    even_a = [top, swap(top, 2), swap(top, 4)]
    even_a.append(swap(top, 6))
    x2_a = chip_mates(even_a)
    x2_a, low = tie(x2_a, low)
    even_b = [low, swap(low, 2), swap(low, 4), swap(low, 6)]
    *parts_a, hidden, dgu, x2_all = feed(0, x2_a, dy_all, packed, None)
    even_b, parts_a, hidden, dgu, x2_all = tie(even_b, parts_a, hidden, dgu, x2_all)
    odds_a = [swap(parts_a[1], 1), swap(parts_a[3], 1)]
    x2_b = chip_mates(even_b)
    x2_b, odds_a = tie(x2_b, odds_a)
    got_a = chip_sums(mates_all(member, (parts_a[0], parts_a[2]), odds_a))
    *parts_b, hidden, dgu, x2_all = feed(1, x2_b, dy_all, packed, (hidden, dgu, x2_all))
    parts_b, got_a = tie(parts_b, got_a)
    dgu = flat(dgu)
    odds_b = [swap(parts_b[1], 1), swap(parts_b[3], 1)]
    g_gate = mm_tn(flat(x2_all), dgu[:, : dgu.shape[1] // 2]).astype(BF16)
    odds_b, g_gate = tie(odds_b, g_gate)

    got_b = mates_all(member, (parts_b[0], parts_b[2]), odds_b)
    got_b, x2_all, dy_all, hidden = tie(got_b, x2_all, dy_all, hidden)
    got_b = chip_sums(got_b)
    g_up = mm_tn(flat(x2_all), dgu[:, dgu.shape[1] // 2 :]).astype(BF16)
    g_down = mm_tn(flat(hidden), flat(dy_all)).astype(BF16)
    if one_team:
        g_ff = pack_back(g_gate, g_up, g_down)
        g_ff = lax.psum_scatter(g_ff.reshape(-1, g_ff.shape[-1]), "ctx", scatter_dimension=0, tiled=True)
    mixed_parts = parts_of(hidden, packed, width)
    got_b, mixed_parts = tie(got_b, mixed_parts)
    sums = (got_a, got_b)
    d_middle, d_low, d_heads = d_middle_of(member_at, sums, middle, dy_own, wo_all)

    hidden, d_low, d_heads = tie(hidden, d_low, d_heads)
    d_heads = across(d_heads.reshape(n_ctx, mates, *d_heads.shape[1:]))
    mixed_own, mixed_sums = mates_trade(mixed_parts)
    mixed_got = hop(mixed_sums)
    out_parts = grad_out_parts(member_at, traded, d_low)
    d_heads, mixed_got, out_parts = tie(d_heads, mixed_got, out_parts)

    d_other = d_heads if mates == 1 else swap(d_heads[:, 1:], 1)
    d_qkv, more = [attend_back(slots, qkv[-1], d_other, lse_other, cos_t, sin_t)], []
    if mates == 2:
        more = [swap(input_all(d_qkv[0], wqkv), 1)]
        d_qkv = [attend_back(slots, qkv[0], d_heads, lse, cos_t, sin_t), *d_qkv]
    d_qkv, more = tie(d_qkv, more)
    e1 = input_own(d_qkv[0], wqkv, more)
    e1, d_qkv, mixed_got, out_parts = tie(e1, d_qkv, mixed_got, out_parts)
    e1 = lax.psum_scatter(e1, "ctx", scatter_dimension=0)

    g_qkv = mm_tn(flat(x1[0][:, :span]), flat(d_qkv[0]))
    for a, b in zip(x1[1:], d_qkv[1:]):
        g_qkv = g_qkv + mm_tn(flat(a[:, :span]), flat(b))
    if one_team:
        ff = g_ff.shape[1]
        cut = TEAM * rows
        ways, g_ff, out_parts = tie(pieces_of(member, g_qkv), g_ff, out_parts)
        g_gu = jnp.concatenate([g_ff[:cut].reshape(TEAM, rows, ff), g_ff[cut : 2 * cut].reshape(TEAM, rows, ff)], axis=2)
        g_gu = lax.all_to_all(g_gu, "dp", 0, 0, tiled=True)
        out_own, out_sums = mates_trade(out_parts)
        ways, out_sums = tie([ways[0], *hop(ways[1:])], out_sums)
        home = ways[0].astype(F32)
        for way in ways[1:]:
            home = home + way.astype(F32)
        home = home.astype(BF16).reshape(mates, n_ctx, rows, QKV)
        home, g_gu = tie(jnp.stack([home[0], swap(home[1], 1)], axis=1), g_gu)
        home = across(home).reshape(TEAM, rows, QKV)
        home, mixed_got = tie(home, mixed_got)
        g_out = total_of(out_own, hop(out_sums)).astype(BF16)
        out_ring = ring_trade(g_out.reshape(n_ctx, -1, width))
        down = g_ff[2 * cut :].reshape(width // ff, -1, ff)
        grad_down = jnp.concatenate([down[i] for i in range(width // ff)], axis=1).astype(F32)
    else:
        home = columns_out(g_qkv, head)
        g_gu = columns_out(jnp.concatenate([g_gate, g_up], axis=1), here)
        out_own, out_sums = mates_trade(out_parts)
        grad_down, grad_out = rows_out(g_down), rows_out(total_of(out_own, hop(out_sums)))
    *grads_qkv, gain_a_grad = gradients(head_at if one_team else ids, gain_a, home, (w_query, w_key, w_value))
    *grads_gu, gain_f_grad = gradients(ids, gain_f, g_gu, (w_gate, w_up))
    mixed = (middle + total_of(mixed_own, mixed_got)).astype(BF16)[None]
    token_grad = token_gradient(e1, tok, d_middle)
    if one_team:
        out_ring, token_grad, gain_a_grad, gain_f_grad = tie(out_ring, token_grad, gain_a_grad, gain_f_grad)
        grad_out = sum(t.astype(F32) for t in out_ring[1:]) + out_ring[0].astype(F32)
    return (
        mixed,
        token_grad[None],
        gain_a_grad[0],
        *grads_qkv,
        grad_out,
        gain_f_grad[0],
        *grads_gu,
        grad_down,
    )


def solution(mesh):
    act = P("dp", "ctx", None)
    vec = P(("dp", "ctx"))
    mat = P(("dp", "ctx"), None)
    return jax.shard_map(
        local,
        mesh=mesh,
        in_specs=(act, act, vec, mat, mat, mat, mat, vec, mat, mat, mat, P()),
        out_specs=(act, act, vec, mat, mat, mat, mat, vec, mat, mat, mat),
        check_vma=False,
    )
```

```python
import functools

import jax
import jax.numpy as jnp
from jax import lax
from jax.experimental import pallas as pl
from jax.experimental.pallas import tpu as pltpu
from jax.sharding import PartitionSpec as P

HEADS = 16
KV_HEADS = 8
HEAD_DIM = 96
GROUPS = HEADS // KV_HEADS
HALF = HEAD_DIM // 2
QW = GROUPS * HEAD_DIM
QKV = QW + 2 * HEAD_DIM

EPS = 1e-05
THETA = 100000.0
F32 = jnp.float32
BF16 = jnp.bfloat16
CHUNKS = 4
VMEM_BYTES = 56 * 2**20
SMALL_BYTES = 24 * 2**20

TEAM = KV_HEADS
PAIRS = TEAM // 2


def dot(a, b, dims):
    return lax.dot_general(a, b, (dims, ((), ())), preferred_element_type=F32)


def mm(a, b):
    return dot(a, b, ((1,), (0,)))


def mm_nt(a, b):
    return dot(a, b, ((1,), (1,)))


def mm_tn(a, b):
    return dot(a, b, ((0,), (0,)))


def swap(value, bit):
    n = lax.axis_size("dp")
    return lax.ppermute(value, "dp", [(i, i ^ bit) for i in range(n)])


def after(value, *others):
    return lax.optimization_barrier((value, *others))[0]


def params(limit=VMEM_BYTES):
    return pltpu.CompilerParams(vmem_limit_bytes=limit)


def cost(flops, nbytes, exps=0):
    return pl.CostEstimate(flops=int(3 * flops), bytes_accessed=int(3 * nbytes), transcendentals=int(exps))


def whole(shape):
    return pl.BlockSpec(shape, lambda *_: (0,) * len(shape))


def join(even_ref, odd_ref):
    return jnp.concatenate([even_ref[...], odd_ref[...]], axis=0)


def qkv_kernel(x_ref, w_ref, cos_ref, sin_ref, out_ref):
    scale = HEAD_DIM**-0.5
    cosine, sine = cos_ref[...], sin_ref[...]
    cosine = jnp.concatenate([cosine * scale] * GROUPS + [cosine, jnp.ones_like(cosine)], axis=1)
    sine = jnp.concatenate([sine * scale] * GROUPS + [sine, jnp.zeros_like(sine)], axis=1)
    first = lax.broadcasted_iota(jnp.int32, cosine.shape, 1) % HEAD_DIM < HALF
    y = mm(x_ref[0], w_ref[...])
    partner = jnp.where(first, pltpu.roll(y, QKV - HALF, 1), pltpu.roll(y, HALF, 1))
    out_ref[0] = (y * cosine + partner * sine).astype(BF16)


def qkv_of(x, span, w, tables):
    n_ctx, _, width = x.shape
    return pl.pallas_call(
        qkv_kernel,
        grid=(n_ctx,),
        in_specs=[pl.BlockSpec((1, span, width), lambda i: (i, 0, 0)), whole(w.shape)]
        + [pl.BlockSpec((span, HEAD_DIM), lambda i: (i, 0))] * 2,
        out_specs=pl.BlockSpec((1, span, QKV), lambda i: (i, 0, 0)),
        out_shape=jax.ShapeDtypeStruct((n_ctx, span, QKV), BF16),
        compiler_params=params(SMALL_BYTES),
        cost_estimate=cost(2 * n_ctx * span * width * QKV, 2 * n_ctx * span * width + 2 * width * QKV),
        name="qkv",
    )(x, w, *tables)


def first_kernel(x_ref, w_ref, out_ref):
    rows = x_ref.shape[0]
    x = x_ref[...].astype(F32)
    r = lax.rsqrt(jnp.mean(x * x, axis=-1, keepdims=True) + EPS)
    out_ref[:rows] = (x * r).astype(BF16)
    out_ref[rows:] = w_ref[...]


def first_of(x, w):
    out = (x.shape[0] + w.shape[0], x.shape[1])
    return pl.pallas_call(
        first_kernel,
        grid=(1,),
        in_specs=[whole(x.shape), whole(w.shape)],
        out_specs=whole(out),
        out_shape=jax.ShapeDtypeStruct(out, BF16),
        compiler_params=params(SMALL_BYTES),
        cost_estimate=cost(6 * x.size, 4 * out[0] * out[1]),
        name="first",
    )(x, w)


def rows_kernel(member_ref, *refs):
    pieces, out_ref = refs[:-1], refs[-1]
    n_ctx, _, rows, _ = pieces[0].shape
    for p, piece in enumerate(pieces):
        for c in range(n_ctx):
            for j in range(2):
                at = pl.multiple_of((member_ref[2 * p + j] * n_ctx + c) * rows, 16)
                out_ref[pl.ds(at, rows), :] = piece[c, j]


def rows_of(member, pieces):
    n_ctx, two, rows, width = pieces[0].shape
    out = (len(pieces) * n_ctx * two * rows, width)
    return pl.pallas_call(
        rows_kernel,
        grid_spec=pltpu.PrefetchScalarGridSpec(
            num_scalar_prefetch=1,
            grid=(1,),
            in_specs=[whole(t.shape) for t in pieces],
            out_specs=whole(out),
        ),
        out_shape=jax.ShapeDtypeStruct(out, BF16),
        compiler_params=params(SMALL_BYTES),
        cost_estimate=cost(0, 4 * out[0] * out[1]),
        name="rows",
    )(member, *pieces)


def pieces_kernel(member_ref, grad_ref, *out_refs):
    for p, out_ref in enumerate(out_refs):
        for j in range(2):
            out_ref[j] = grad_ref[member_ref[2 * p + j]].astype(BF16)


def pieces_of(member, grad):
    rows, width = grad.shape[0] // TEAM, grad.shape[1]
    return pl.pallas_call(
        pieces_kernel,
        grid_spec=pltpu.PrefetchScalarGridSpec(
            num_scalar_prefetch=1,
            grid=(1,),
            in_specs=[whole((TEAM, rows, width))],
            out_specs=(whole((2, rows, width)),) * PAIRS,
        ),
        out_shape=(jax.ShapeDtypeStruct((2, rows, width), BF16),) * PAIRS,
        compiler_params=params(SMALL_BYTES),
        cost_estimate=cost(0, 6 * grad.size),
        name="pieces",
    )(member, grad.reshape(TEAM, rows, width))


def stack_kernel(order_ref, *refs):
    for k, ref in enumerate(refs[:-1]):
        refs[-1][order_ref[k]] = ref[...]


def stack(order, xs):
    rows, width = xs[0].shape
    steps = 4
    block = rows // steps
    return pl.pallas_call(
        stack_kernel,
        grid_spec=pltpu.PrefetchScalarGridSpec(
            num_scalar_prefetch=1,
            grid=(steps,),
            in_specs=[pl.BlockSpec((block, width), lambda i, m: (i, 0))] * len(xs),
            out_specs=pl.BlockSpec((len(xs), block, width), lambda i, m: (0, i, 0)),
        ),
        out_shape=jax.ShapeDtypeStruct((len(xs), rows, width), BF16),
        compiler_params=params(),
        cost_estimate=cost(0, 4 * len(xs) * rows * width),
        name="stack",
    )(order, *xs)


def in_order(slots_ref, ref, scratch, half):
    for b in range(slots_ref.shape[0]):
        slot = slots_ref[b]
        at = pl.multiple_of((slot % 2) * half, half)
        scratch[pl.ds(b * half, half), :] = ref[slot // 2, pl.ds(at, half), :]


def heads_in_order(slots_ref, ref, scratch, half):
    for b in range(slots_ref.shape[0]):
        slot = slots_ref[b]
        first, second = ref[slot // 2, 0, :, :QW], ref[slot // 2, 0, :, QW:]
        scratch[pl.ds(b * half, half), :] = jnp.where(slot % 2 == 0, first, second)


def heads_out_of_order(order_ref, ref, scratch, half):
    for c in range(ref.shape[0]):
        for j in range(2):
            at = pl.multiple_of(order_ref[2 * c + j] * half, half)
            ref[c, 0, :, j * QW : (j + 1) * QW] = scratch[pl.ds(at, half), :]


def out_of_order(slots_ref, ref, first, value, half):
    for b in range(value.shape[0] // half):
        slot = slots_ref[first // half + b]
        at = pl.multiple_of((slot % 2) * half, half)
        ref[slot // 2, pl.ds(at, half), :] = value[b * half : (b + 1) * half]


def flip(value):
    return value.astype(F32).T


def stacked_heads(ref, rows):
    return jnp.concatenate([ref[rows, g * HEAD_DIM : (g + 1) * HEAD_DIM] for g in range(GROUPS)], axis=0)


def causal(size):
    key = lax.broadcasted_iota(jnp.int32, (size, GROUPS * size), 0)
    query = lax.broadcasted_iota(jnp.int32, (size, GROUPS * size), 1) % size
    return key <= query


def attend_kernel(slots_ref, order_ref, qkv_ref, *refs):
    more, (out_ref, lse_ref, scratch, o_scr) = refs[:-4], refs[-4:]
    half = qkv_ref.shape[1] // 2
    size = scratch.shape[0] // CHUNKS
    in_order(slots_ref, qkv_ref, scratch, half)
    v_t = flip(scratch[:, QW + HEAD_DIM :]).astype(BF16)
    allowed = causal(size)
    for i in range(CHUNKS):
        lo, hi = i * size, (i + 1) * size
        q = stacked_heads(scratch, slice(lo, hi))
        k_near = scratch[lo:hi, QW : QW + HEAD_DIM]
        near = jnp.where(allowed, mm_nt(k_near, q), -1e30)
        top = jnp.max(near, axis=0, keepdims=True)
        if i > 0:
            far = mm_nt(scratch[:lo, QW : QW + HEAD_DIM], q)
            top = jnp.maximum(top, jnp.max(far, axis=0, keepdims=True))
        near = jnp.exp(near - top)
        total = jnp.sum(near, axis=0, keepdims=True)
        acc = mm(v_t[:, lo:hi], near.astype(BF16))
        if i > 0:
            far = jnp.exp(far - top)
            total = total + jnp.sum(far, axis=0, keepdims=True)
            acc = acc + mm(v_t[:, :lo], far.astype(BF16))
        lse_ref[pl.ds(i, 1), :] = top + jnp.log(total)
        o = (acc / total).T.astype(BF16)
        for g in range(GROUPS):
            o_scr[lo:hi, g * HEAD_DIM : (g + 1) * HEAD_DIM] = o[g * size : (g + 1) * size]
    heads_out_of_order(order_ref, out_ref, o_scr, half)
    for ref in more:
        out_ref[:, 1] = ref[:, 0]


def attend_back_kernel(slots_ref, qkv_ref, do_ref, lse_ref, turn_ref, out_ref, scratch, do_scr, dk_scr, dv_scr):
    half = qkv_ref.shape[1] // 2
    length = scratch.shape[0]
    cos_ref, sin_ref = turn_ref.at[:HALF], turn_ref.at[HALF:]
    size = length // CHUNKS
    scale = HEAD_DIM**-0.5
    in_order(slots_ref, qkv_ref, scratch, half)
    heads_in_order(slots_ref, do_ref, do_scr, half)
    k_t = flip(scratch[:, QW : QW + HEAD_DIM]).astype(BF16)
    allowed = causal(size)
    dk_scr[...] = jnp.zeros_like(dk_scr)
    dv_scr[...] = jnp.zeros_like(dv_scr)
    for i in range(CHUNKS):
        lo, hi = i * size, (i + 1) * size
        q = stacked_heads(scratch, slice(lo, hi))
        do = stacked_heads(do_scr, slice(lo, hi))
        lse = lse_ref[pl.ds(i, 1), :]
        spans = [(lo, hi)] + ([(0, lo)] if i > 0 else [])
        probs, prods = [], []
        delta = 0.0
        for at, (a, b) in enumerate(spans):
            p = jnp.exp(mm_nt(scratch[a:b, QW : QW + HEAD_DIM], q) - lse)
            if at == 0:
                p = jnp.where(allowed, p, 0.0)
            prod = p * mm_nt(scratch[a:b, QW + HEAD_DIM :], do)
            delta = delta + jnp.sum(prod, axis=0, keepdims=True)
            probs.append(p)
            prods.append(prod)
        dq_t = 0.0
        for (a, b), p, prod in zip(spans, probs, prods):
            ds = (prod - p * delta).astype(BF16)
            dk_scr[a:b, :] += mm(ds, q)
            dv_scr[a:b, :] += mm(p.astype(BF16), do)
            dq_t = dq_t + mm(k_t[:, a:b], ds)
        c = jnp.concatenate([cos_ref[:, lo:hi]] * GROUPS, axis=1) * scale
        s = jnp.concatenate([sin_ref[:, lo:hi]] * GROUPS, axis=1) * scale
        first, second = dq_t[:HALF], dq_t[HALF:]
        dq = jnp.concatenate([first * c + second * s, second * c - first * s], axis=0).T
        for g in range(GROUPS):
            do_scr[lo:hi, g * HEAD_DIM : (g + 1) * HEAD_DIM] = dq[g * size : (g + 1) * size].astype(BF16)
    for i in range(CHUNKS):
        lo, hi = i * size, (i + 1) * size
        dk_t = dk_scr[lo:hi, :].T
        first, second = dk_t[:HALF], dk_t[HALF:]
        c, s = cos_ref[:, lo:hi], sin_ref[:, lo:hi]
        dk = jnp.concatenate([first * c + second * s, second * c - first * s], axis=0).T
        value = jnp.concatenate([do_scr[lo:hi, :], dk.astype(BF16), dv_scr[lo:hi, :].astype(BF16)], axis=1)
        out_of_order(slots_ref, out_ref, lo, value, half)


def attend(slots, order, qkv, more):
    n_ctx, span, _ = qkv.shape
    length = n_ctx * span
    heads = (n_ctx, 1 + len(more), span // 2, 2 * QW)
    lse = (CHUNKS, GROUPS * length // CHUNKS)
    work = GROUPS * length * length
    return pl.pallas_call(
        attend_kernel,
        grid_spec=pltpu.PrefetchScalarGridSpec(
            num_scalar_prefetch=2,
            grid=(1,),
            in_specs=[whole(t.shape) for t in (qkv, *more)],
            out_specs=(whole(heads), whole(lse)),
            scratch_shapes=[pltpu.VMEM((length, QKV), BF16), pltpu.VMEM((length, QW), BF16)],
        ),
        out_shape=(jax.ShapeDtypeStruct(heads, BF16), jax.ShapeDtypeStruct(lse, F32)),
        compiler_params=params(SMALL_BYTES),
        cost_estimate=cost(work * 2 * HEAD_DIM * 3, 2 * length * (QKV + QW), work // 2),
        name="attend",
    )(slots, order, qkv, *more)


def attend_back(slots, qkv, d_heads, lse, turn_t):
    n_ctx, span, _ = qkv.shape
    length = n_ctx * span
    work = GROUPS * length * length
    return pl.pallas_call(
        attend_back_kernel,
        grid_spec=pltpu.PrefetchScalarGridSpec(
            num_scalar_prefetch=1,
            grid=(1,),
            in_specs=[
                whole(qkv.shape),
                whole((n_ctx, 1, *d_heads.shape[2:])),
            ]
            + [whole(t.shape) for t in (lse, turn_t)],
            out_specs=whole((n_ctx, span, QKV)),
            scratch_shapes=[
                pltpu.VMEM((length, QKV), BF16),
                pltpu.VMEM((length, QW), BF16),
                pltpu.VMEM((length, HEAD_DIM), F32),
                pltpu.VMEM((length, HEAD_DIM), F32),
            ],
        ),
        out_shape=jax.ShapeDtypeStruct((n_ctx, span, QKV), BF16),
        compiler_params=params(SMALL_BYTES),
        cost_estimate=cost(work * 2 * HEAD_DIM * 8, 4 * length * QKV, work // 2),
        name="attend_back",
    )(slots, qkv, d_heads, lse, turn_t)


def parts_kernel(a_ref, packed, *refs):
    out_refs, (wd_ref, sem) = refs[:4], refs[4:]

    @pl.when(pl.program_id(0) == 0)
    def _():
        copies = [pltpu.make_async_copy(src, dst, sem.at[i]) for i, (src, dst) in enumerate(down_ways(packed, wd_ref))]
        for copy in copies:
            copy.start()
        for copy in copies:
            copy.wait()

    block = a_ref.shape[1]
    y = mm(jnp.concatenate([a_ref[k] for k in range(TEAM)], axis=0), wd_ref[...]).astype(BF16)
    for k in range(TEAM):
        out_refs[k // 4 * 2 + k % 2][k // 2 % 2] = y[k * block : (k + 1) * block]


def parts_of(a, packed, width):
    _, rows, depth = a.shape
    steps = 4
    block = rows // steps
    return pl.pallas_call(
        parts_kernel,
        grid=(steps,),
        in_specs=[pl.BlockSpec((TEAM, block, depth), lambda i: (0, i, 0)), pl.BlockSpec(memory_space=pl.ANY)],
        out_specs=(pl.BlockSpec((2, block, width), lambda i: (0, i, 0)),) * 4,
        out_shape=(jax.ShapeDtypeStruct((2, rows, width), BF16),) * 4,
        scratch_shapes=[
            pltpu.VMEM((depth, width), BF16),
            pltpu.SemaphoreType.DMA((packed.shape[0] * (width // depth),)),
        ],
        compiler_params=params(SMALL_BYTES),
        cost_estimate=cost(2 * TEAM * rows * depth * width, 2 * TEAM * rows * (width + depth) + 2 * depth * width),
        name="parts",
    )(a, packed)


def input_own_kernel(a_ref, w_ref, *refs):
    y = mm_nt(a_ref[0], w_ref[...])
    for ref in refs[:-1]:
        y = y + ref[0].astype(F32)
    refs[-1][0] = y.astype(BF16)


def input_own(a, w, more):
    n_ctx, span, depth = a.shape
    width = w.shape[0]
    blocked = lambda n: pl.BlockSpec((1, span, n), lambda i: (i, 0, 0))
    return pl.pallas_call(
        input_own_kernel,
        grid=(n_ctx,),
        in_specs=[blocked(depth), whole(w.shape)] + [blocked(width)] * len(more),
        out_specs=blocked(width),
        out_shape=jax.ShapeDtypeStruct((n_ctx, span, width), BF16),
        compiler_params=params(SMALL_BYTES),
        cost_estimate=cost(2 * n_ctx * span * depth * width, 4 * n_ctx * span * (width + depth) + 2 * depth * width),
        name="input_own",
    )(a, w, *more)


def input_all_kernel(a_ref, w_ref, out_ref):
    out_ref[0] = mm_nt(a_ref[0], w_ref[...]).astype(BF16)


def input_all(a, w):
    n_ctx, span, depth = a.shape
    width = w.shape[0]
    blocked = lambda n: pl.BlockSpec((1, span, n), lambda i: (i, 0, 0))
    return pl.pallas_call(
        input_all_kernel,
        grid=(n_ctx,),
        in_specs=[blocked(depth), whole(w.shape)],
        out_specs=blocked(width),
        out_shape=jax.ShapeDtypeStruct((n_ctx, span, width), BF16),
        compiler_params=params(SMALL_BYTES),
        cost_estimate=cost(2 * n_ctx * span * depth * width, 4 * n_ctx * span * (width + depth) + 2 * depth * width),
        name="input_all",
    )(a, w)


def grad_out_kernel(at_ref, heads_ref, dm_ref, *out_refs):
    dm = dm_ref[...]
    for k in range(TEAM):
        y = mm_tn(unfold(heads_ref[at_ref[k]]), dm)
        out_refs[k // 4 * 2 + k % 2][k // 2 % 2] = y.astype(BF16)


def grad_out_parts(member_at, heads, dm):
    rows, width = dm.shape
    return pl.pallas_call(
        grad_out_kernel,
        grid_spec=pltpu.PrefetchScalarGridSpec(
            num_scalar_prefetch=1,
            grid=(1,),
            in_specs=[whole(t.shape) for t in (heads, dm)],
            out_specs=(whole((2, QW, width)),) * 4,
        ),
        out_shape=(jax.ShapeDtypeStruct((2, QW, width), BF16),) * 4,
        compiler_params=params(),
        cost_estimate=cost(2 * TEAM * rows * QW * width, 2 * TEAM * QW * width),
        name="grad_out",
    )(member_at, heads, dm)


def unfold(block):
    return jnp.concatenate([block[:, :QW], block[:, QW:]], axis=0)


def fetch(any_refs, ref, sem):
    copies = [pltpu.make_async_copy(a, ref.at[k], sem.at[k]) for k, a in enumerate(any_refs)]
    for copy in copies:
        copy.start()
    return copies


def fetched(arrays):
    specs = [pl.BlockSpec(memory_space=pl.ANY)] * len(arrays)
    scratch = [pltpu.VMEM((len(arrays), *arrays[0].shape), BF16), pltpu.SemaphoreType.DMA((len(arrays),))]
    return specs, scratch


def middle_kernel(at_ref, heads_ref, x_ref, *refs):
    wo_any, (middle_ref, top_ref, low_ref, wo_ref, sem) = refs[:TEAM], refs[TEAM:]
    copies = fetch(wo_any, wo_ref, sem)
    heads = jnp.concatenate([unfold(heads_ref[at_ref[k]]) for k in range(TEAM)], axis=1)
    for copy in copies:
        copy.wait()
    acc = x_ref[...].astype(F32) + mm(heads, wo_ref[...].reshape(heads.shape[1], -1))
    middle_ref[...] = acc
    r = lax.rsqrt(jnp.mean(acc * acc, axis=-1, keepdims=True) + EPS)
    xhat = (acc * r).astype(BF16)
    half = top_ref.shape[0]
    top_ref[...] = xhat[:half]
    low_ref[...] = xhat[half:]


def middle_of(member_at, x, heads, wo):
    rows, width = x.shape
    specs, scratch = fetched(wo)
    return pl.pallas_call(
        middle_kernel,
        grid_spec=pltpu.PrefetchScalarGridSpec(
            num_scalar_prefetch=1,
            grid=(1,),
            in_specs=[whole(t.shape) for t in (heads, x)] + specs,
            out_specs=(whole(x.shape),) + (whole((rows // 2, width)),) * 2,
            scratch_shapes=scratch,
        ),
        out_shape=(jax.ShapeDtypeStruct(x.shape, F32),) + (jax.ShapeDtypeStruct((rows // 2, width), BF16),) * 2,
        compiler_params=params(),
        cost_estimate=cost(2 * rows * width * TEAM * QW, 2 * width * TEAM * QW + 12 * rows * width),
        name="middle",
    )(member_at, heads, x, *wo)


def d_middle_kernel(at_ref, *refs):
    middle_ref, dy_ref = refs[1:3]
    wo_any, (d_ref, low_ref, out_ref, wo_ref, sem) = refs[3 : 3 + TEAM], refs[3 + TEAM :]
    copies = fetch(wo_any, wo_ref, sem)
    middle = middle_ref[...]
    half = middle.shape[0] // 2
    r = lax.rsqrt(jnp.mean(middle * middle, axis=-1, keepdims=True) + EPS)
    d = dy_ref[...].astype(F32) + norm_back(team_total(refs[:1]), middle * r, r)
    d_ref[...] = d
    low = d.astype(BF16)
    low_ref[...] = low
    for copy in copies:
        copy.wait()
    y = mm_nt(low, wo_ref[...].reshape(TEAM * QW, -1)).astype(BF16)
    for k in range(TEAM):
        part = slice(k * QW, (k + 1) * QW)
        out_ref[at_ref[k], :, :QW] = y[:half, part]
        out_ref[at_ref[k], :, QW:] = y[half:, part]


def d_middle_of(member_at, sums, middle, dy, wo):
    rows, width = dy.shape
    heads = (TEAM, rows // 2, 2 * QW)
    specs, scratch = fetched(wo)
    return pl.pallas_call(
        d_middle_kernel,
        grid_spec=pltpu.PrefetchScalarGridSpec(
            num_scalar_prefetch=1,
            grid=(1,),
            in_specs=[whole(t.shape) for t in (*sums, middle, dy)] + specs,
            out_specs=(whole(dy.shape), whole(dy.shape), whole(heads)),
            scratch_shapes=scratch,
        ),
        out_shape=(
            jax.ShapeDtypeStruct(dy.shape, F32),
            jax.ShapeDtypeStruct(dy.shape, BF16),
            jax.ShapeDtypeStruct(heads, BF16),
        ),
        compiler_params=params(),
        cost_estimate=cost(2 * rows * width * TEAM * QW, 2 * width * TEAM * QW + 18 * rows * width),
        name="d_middle",
    )(member_at, *sums, middle, dy, *wo)


def mates_kernel(*refs):
    evens, odds, outs = refs[:2], refs[2:4], refs[4:]
    for j, k in enumerate((2, 4, 6)):
        r = evens[k // 4][k // 2 % 2].astype(F32) + odds[k // 4][k // 2 % 2].astype(F32)
        outs[j][...] = r.astype(BF16)


def mates_sum(evens, odds):
    _, rows, width = evens[0].shape
    steps = 2
    block = rows // steps
    return pl.pallas_call(
        mates_kernel,
        grid=(steps,),
        in_specs=[pl.BlockSpec((2, block, width), lambda i: (0, i, 0))] * 4,
        out_specs=(pl.BlockSpec((block, width), lambda i: (i, 0)),) * 3,
        out_shape=(jax.ShapeDtypeStruct((rows, width), BF16),) * 3,
        compiler_params=params(SMALL_BYTES),
        cost_estimate=cost(6 * rows * width, 36 * rows * width),
        name="mates_sum",
    )(*evens, *odds)


def mates_all_kernel(member_ref, *refs):
    out_ref = refs[-1]
    for half in range(2):
        evens, odds = refs[4 * half : 4 * half + 2], refs[4 * half + 2 : 4 * half + 4]
        rows = evens[0].shape[1]
        for k in (0, 2, 4, 6):
            r = evens[k // 4][k // 2 % 2].astype(F32) + odds[k // 4][k // 2 % 2].astype(F32)
            out_ref[member_ref[k] // 2, half * rows : (half + 1) * rows] = r.astype(BF16)


def mates_all(member, parts):
    _, rows, width = parts[0].shape
    out = (PAIRS, 2 * rows, width)
    return pl.pallas_call(
        mates_all_kernel,
        grid_spec=pltpu.PrefetchScalarGridSpec(
            num_scalar_prefetch=1,
            grid=(1,),
            in_specs=[whole(t.shape) for t in parts],
            out_specs=whole(out),
        ),
        out_shape=jax.ShapeDtypeStruct(out, BF16),
        compiler_params=params(SMALL_BYTES),
        cost_estimate=cost(16 * rows * width, 96 * rows * width),
        name="mates_all",
    )(member, *parts)


def team_total(refs):
    return jnp.sum(refs[0][...].astype(F32), axis=0)


def token_kernel(e_ref, x_ref, d_ref, out_ref):
    x = x_ref[...].astype(F32)
    r = lax.rsqrt(jnp.mean(x * x, axis=-1, keepdims=True) + EPS)
    out_ref[...] = d_ref[...] + norm_back(e_ref[...].astype(F32), x * r, r)


def token_gradient(e, x, d_middle):
    rows, width = x.shape
    block = rows // 2
    return pl.pallas_call(
        token_kernel,
        grid=(2,),
        in_specs=[pl.BlockSpec((block, width), lambda i: (i, 0))] * 3,
        out_specs=pl.BlockSpec((block, width), lambda i: (i, 0)),
        out_shape=jax.ShapeDtypeStruct(x.shape, F32),
        compiler_params=params(),
        cost_estimate=cost(12 * x.size, 20 * x.size),
        name="token_gradient",
    )(e, x, d_middle)


def pack(gate_up, down):
    _, rows, twice = gate_up.shape
    ff = twice // 2
    blocks = [gate_up[..., :ff].reshape(-1, ff), gate_up[..., ff:].reshape(-1, ff)]
    return jnp.concatenate(blocks + [down[:, i : i + ff] for i in range(0, down.shape[1], ff)], axis=0)


def pack_back(gate, up, down):
    n = lax.axis_size("ctx")
    width, ff = gate.shape
    by_ctx = lambda g: jnp.transpose(g.reshape(TEAM, n, -1, ff), (1, 0, 2, 3)).reshape(n, -1, ff)
    blocks = [by_ctx(gate), by_ctx(up)]
    down = down.reshape(n, ff // n, width)
    return jnp.concatenate(blocks + [down[..., i : i + ff] for i in range(0, width, ff)], axis=1)


def down_ways(packed, wd_ref):
    n_ctx, count, ff = packed.shape
    width = wd_ref.shape[1]
    down = ff // n_ctx
    first = count - width // ff * down
    return [
        (packed.at[c, pl.ds(first + i * down, down)], wd_ref.at[pl.ds(c * down, down), pl.ds(i * ff, ff)])
        for c in range(n_ctx)
        for i in range(width // ff)
    ]


def unpack(packed, wgu_ref, wd_ref, sem):
    n_ctx, _, ff = packed.shape
    rows = wgu_ref.shape[0] // (TEAM * n_ctx)
    ways = []
    for part in range(2):
        for c in range(n_ctx):
            for m in range(TEAM):
                out = wgu_ref.at[pl.ds((m * n_ctx + c) * rows, rows), pl.ds(part * ff, ff)]
                ways.append((packed.at[c, pl.ds((part * TEAM + m) * rows, rows)], out))
    ways += down_ways(packed, wd_ref)
    copies = [pltpu.make_async_copy(src, dst, sem.at[i]) for i, (src, dst) in enumerate(ways)]
    for copy in copies:
        copy.start()
    return copies


def feed_kernel(*refs):
    x_refs = refs[:TEAM]
    y_ref, packed = refs[TEAM : TEAM + 2]
    even0_ref, odd0_ref, even1_ref, odd1_ref, hidden_ref, dgu_ref, xc_ref, wgu_ref, wd_ref, sem = refs[-10:]
    ff = wd_ref.shape[0]
    block = x_refs[0].shape[0]

    @pl.when(pl.program_id(0) == 0)
    def _():
        for copy in unpack(packed, wgu_ref, wd_ref, sem):
            copy.wait()

    for j in range(TEAM):
        xc_ref[j] = x_refs[j][...]
    x = jnp.concatenate([ref[...] for ref in x_refs], axis=0)
    y = y_ref[...].reshape(TEAM * block, y_ref.shape[2])
    gate = mm(x, wgu_ref[:, :ff])
    upper = mm(x, wgu_ref[:, ff:])
    d_hidden = mm_nt(y, wd_ref[...])
    sigma = jax.nn.sigmoid(gate)
    act = gate * sigma
    hidden = (act * upper).astype(BF16)
    d_gate = (d_hidden * upper * sigma * (1.0 + gate * (1.0 - sigma))).astype(BF16)
    dgu = jnp.concatenate([d_gate, (d_hidden * act).astype(BF16)], axis=1)
    e = mm_nt(dgu, wgu_ref[...]).astype(BF16)
    outs = (even0_ref, odd0_ref, even1_ref, odd1_ref)
    for j in range(TEAM):
        part = slice(j * block, (j + 1) * block)
        hidden_ref[j] = hidden[part]
        dgu_ref[j] = dgu[part]
        outs[j // 4 * 2 + j % 2][j // 2 % 2] = e[part]


def feed(part, xs, y, packed, held):
    rows, width = xs[0].shape
    n_ctx, packed_rows, ff = packed.shape
    steps = 4
    block = rows // steps
    widths = (ff, 2 * ff, width)
    extra = [] if held is None else list(held)
    at_part = lambda n: pl.BlockSpec((TEAM, block, n), lambda i: (0, part * steps + i, 0))
    return pl.pallas_call(
        feed_kernel,
        grid=(steps,),
        in_specs=[pl.BlockSpec((block, width), lambda i: (i, 0))] * TEAM
        + [at_part(width)]
        + [pl.BlockSpec(memory_space=pl.ANY)] * (1 + len(extra)),
        out_specs=(pl.BlockSpec((2, block, width), lambda i: (0, i, 0)),) * 4 + tuple(at_part(n) for n in widths),
        out_shape=(jax.ShapeDtypeStruct((2, rows, width), BF16),) * 4
        + tuple(jax.ShapeDtypeStruct((TEAM, 2 * rows, n), BF16) for n in widths),
        input_output_aliases={TEAM + 2 + i: 4 + i for i in range(len(extra))},
        scratch_shapes=[
            pltpu.VMEM((width, 2 * ff), BF16),
            pltpu.VMEM((ff, width), BF16),
            pltpu.SemaphoreType.DMA((n_ctx * (2 * TEAM + width // ff),)),
        ],
        compiler_params=params(),
        cost_estimate=cost(2 * TEAM * rows * width * 5 * ff, 6 * width * ff + 18 * TEAM * rows * width, TEAM * rows * ff),
        name="feed",
    )(*xs, y, packed, *extra)


def fold_kernel(widths, at_ref, gain_ref, *refs):
    weights, out_ref = refs[:-1], refs[-1]
    gain = gain_ref[...]
    for m in range(TEAM):
        at = 0
        for n, ref in zip(widths, weights):
            out_ref[at_ref[m], :, at : at + n] = (ref[:, m * n : (m + 1) * n].astype(F32) * gain).astype(BF16)
            at += n


def fold(places, gain, weights):
    widths = tuple(w.shape[1] // TEAM for w in weights)
    out = (TEAM, weights[0].shape[0], sum(widths))
    return pl.pallas_call(
        functools.partial(fold_kernel, widths),
        grid_spec=pltpu.PrefetchScalarGridSpec(
            num_scalar_prefetch=1,
            grid=(1,),
            in_specs=[whole(t.shape) for t in (gain, *weights)],
            out_specs=whole(out),
        ),
        out_shape=jax.ShapeDtypeStruct(out, BF16),
        compiler_params=params(),
        cost_estimate=cost(out[0] * out[1] * out[2], 4 * out[0] * out[1] * out[2]),
        name="fold",
    )(places, gain, *weights)


def gradients_kernel(widths, at_ref, gain_ref, grad_ref, *refs):
    count = len(widths)
    weights, outs, gain_out = refs[:count], refs[count : 2 * count], refs[2 * count]
    gain = gain_ref[...]
    total = jnp.zeros(gain.shape, F32)
    for m in range(TEAM):
        at = 0
        for n, w_ref, out_ref in zip(widths, weights, outs):
            g = grad_ref[at_ref[m], :, at : at + n].astype(F32)
            here = slice(m * n, (m + 1) * n)
            total = total + jnp.sum(w_ref[:, here].astype(F32) * g, axis=1, keepdims=True)
            out_ref[:, here] = g * gain
            at += n
    gain_out[...] = jnp.broadcast_to(total, (total.shape[0], 128)).T[:1]


def gradients(places, gain, grad, weights):
    widths = tuple(w.shape[1] // TEAM for w in weights)
    outs = [w.shape for w in weights] + [(1, gain.shape[0])]
    return pl.pallas_call(
        functools.partial(gradients_kernel, widths),
        grid_spec=pltpu.PrefetchScalarGridSpec(
            num_scalar_prefetch=1,
            grid=(1,),
            in_specs=[whole(t.shape) for t in (gain, grad, *weights)],
            out_specs=tuple(whole(shape) for shape in outs),
        ),
        out_shape=tuple(jax.ShapeDtypeStruct(shape, F32) for shape in outs),
        compiler_params=params(SMALL_BYTES),
        cost_estimate=cost(4 * grad.size, 8 * grad.size),
        name="gradients",
    )(places, gain, grad, *weights)


def ring_trade(blocks):
    n, here = lax.axis_size("ctx"), lax.axis_index("ctx")
    got = [lax.dynamic_index_in_dim(blocks, here, 0, False)]
    for s in range(1, n):
        block = lax.dynamic_index_in_dim(blocks, (here + s) % n, 0, False)
        got.append(lax.ppermute(block, "ctx", [(i, (i + s) % n) for i in range(n)]))
    return got


def chip_mates(evens):
    pieces = []
    for even in evens:
        pieces += [even, swap(even, 1)]
    return pieces


def tie(*values):
    leaves, tree = jax.tree.flatten(values)
    return jax.tree.unflatten(tree, lax.optimization_barrier(leaves))


def mates_trade(parts):
    evens, odds = (parts[0], parts[2]), (swap(parts[1], 1), swap(parts[3], 1))
    return (evens[0], odds[0]), mates_sum(evens, odds)


def chip_sums(blocks):
    n = lax.axis_size("dp")
    groups = [list(range(f + c, f + TEAM, 2)) for f in range(0, n, TEAM) for c in range(2)]
    return lax.all_to_all(blocks, "dp", 0, 0, axis_index_groups=groups, tiled=True)


def hop(sums):
    return [swap(r, bit) for r, bit in zip(sums, (2, 4, 6))]


def total_of(own, got):
    total = own[0][0].astype(F32) + own[1][0].astype(F32)
    for part in got:
        total = total + part.astype(F32)
    return total


def place_rows(seq_rows, order, half_rows):
    slots = seq_rows // half_rows
    hit = slots[:, None] == jnp.arange(order.shape[0], dtype=jnp.int32)[None, :]
    return jnp.sum(jnp.where(hit, order[None, :], 0), axis=1) * half_rows + seq_rows % half_rows


def angles(places):
    freqs = THETA ** (-(jnp.arange(HALF).astype(F32) * 2.0 / HEAD_DIM))
    return places.astype(F32)[:, None] * freqs[None, :]


def member_columns(own):
    return lax.all_to_all(own, "dp", 0, 0, tiled=True)


def any_columns(own, index):
    n_dp, n_ctx = lax.axis_size("dp"), lax.axis_size("ctx")
    gathered = lax.all_gather(own, ("dp", "ctx"), axis=0)
    mine = lax.dynamic_index_in_dim(gathered, index, 1, False)
    per = n_dp // TEAM
    mine = mine.reshape(TEAM, n_ctx, per * own.shape[1], own.shape[2])
    return jnp.transpose(mine, (1, 0, 2, 3))


def by_rows(columns):
    return jnp.transpose(columns, (1, 0, 2, 3)).reshape(-1, columns.shape[-1])


def any_rows(own):
    gathered = lax.all_gather(own, ("dp", "ctx"), axis=0, tiled=True)
    count = gathered.shape[0] // TEAM
    return lax.dynamic_slice_in_dim(gathered, (lax.axis_index("dp") % TEAM) * count, count, 0)


def column_blocks(grad):
    n_dp, n_ctx = lax.axis_size("dp"), lax.axis_size("ctx")
    rows_all, width = grad.shape
    blocks = grad.astype(BF16).reshape(TEAM, n_ctx, rows_all // (n_dp * n_ctx), width)
    return jnp.transpose(blocks, (1, 0, 2, 3))


def columns_home(part):
    return lax.all_to_all(part.astype(BF16), "dp", 0, 0, tiled=True)


def columns_out(grad, index):
    hit = (jnp.arange(TEAM) == index)[None, :, None]
    spread = jnp.where(hit, grad.astype(BF16)[:, None, :], jnp.zeros((), BF16))
    out = lax.psum_scatter(spread, ("dp", "ctx"), scatter_dimension=0, tiled=True)
    return jnp.transpose(out, (1, 0, 2))


def rows_out(grad):
    grad = grad.astype(BF16)
    if lax.axis_size("dp") == TEAM:
        return lax.psum_scatter(grad, "ctx", scatter_dimension=0, tiled=True).astype(F32)
    member = lax.axis_index("dp") % TEAM
    hit = (jnp.arange(TEAM) == member)[:, None, None]
    spread = jnp.where(hit, grad[None], jnp.zeros((), BF16)).reshape(-1, grad.shape[1])
    return lax.psum_scatter(spread, ("dp", "ctx"), scatter_dimension=0, tiled=True).astype(F32)


def across(value):
    return lax.all_to_all(value, "ctx", 0, 0, tiled=True)


def ctx_gather(own):
    return across(jnp.broadcast_to(own, (lax.axis_size("ctx"), *own.shape)))


def flat(value):
    return value.reshape(-1, value.shape[-1])


def norm_back(e, xhat, r):
    return r * (e - xhat * jnp.mean(e * xhat, axis=-1, keepdims=True))


def local(
    tokens, cotangent, gain_attn, w_query, w_key, w_value, w_out, gain_ffn, w_gate, w_up, w_down, order
):
    _, span, width = tokens.shape
    n_ctx = lax.axis_size("ctx")
    rows = w_query.shape[0]
    length = span * n_ctx
    half_rows = span // 2
    scale = HEAD_DIM**-0.5

    gain_a = gain_attn.astype(F32)[:, None]
    gain_f = gain_ffn.astype(F32)[:, None]
    mates = TEAM // n_ctx
    here = lax.axis_index("dp") % TEAM
    mate = here % mates
    ids = jnp.arange(TEAM, dtype=jnp.int32)
    place_of = lambda head: head // mates * mates + (head % mates ^ mate)
    member, head_at = here ^ ids, place_of(ids)
    member_at = place_of(member)
    head = lax.axis_index("ctx") * mates + mate
    one_team = lax.axis_size("dp") == TEAM and mates == 2

    storage = jnp.arange(length, dtype=jnp.int32)
    turn = angles(place_rows(storage, order, half_rows))
    sine = jnp.sin(turn)
    tables = (jnp.concatenate([jnp.cos(turn)] * 2, axis=1), jnp.concatenate([-sine, sine], axis=1))
    turn_t = angles(storage).T
    turn_t = jnp.concatenate([jnp.cos(turn_t), jnp.sin(turn_t)], axis=0)
    slots = jnp.sum(jnp.where(order[None, :] == jnp.arange(order.shape[0])[:, None], jnp.arange(order.shape[0]), 0), axis=1)
    slots = slots.astype(jnp.int32)

    tok, dy_own = tokens[0], cotangent[0]
    x = tok.astype(F32)
    low_x1 = (x * lax.rsqrt(jnp.mean(x * x, axis=-1, keepdims=True) + EPS)).astype(BF16)
    folded_qkv = fold(head_at if one_team else ids, gain_a, (w_query, w_key, w_value))
    folded_gu = fold(ids, gain_f, (w_gate, w_up))
    if one_team:
        x1 = [lax.all_gather(first_of(tok, w_out), "ctx", axis=0)]
        blocks = folded_qkv.reshape(n_ctx, mates, rows, QKV)
        blocks = jnp.stack([blocks[:, 0], swap(blocks[:, 1], 1)], axis=1)
        piece = across(blocks)
        piece, folded_gu = tie(piece, folded_gu)
        mine_gu = lax.all_to_all(folded_gu, "dp", 0, 0, tiled=True)
        pieces = [piece, swap(piece, 2), swap(piece, 4), swap(piece, 6)]
        wqkv = rows_of(member, pieces)
        packed = lax.all_gather(pack(mine_gu, w_down), "ctx", axis=0)
    else:
        wqkv = by_rows(any_columns(folded_qkv, head))
        wgu = by_rows(any_columns(folded_gu, here)).reshape(TEAM, width // TEAM, -1)
        x1 = [lax.all_gather(low_x1, "ctx", axis=0)]
        wo, wd = any_rows(w_out), any_rows(w_down)
        packed = pack(wgu, wd)[None]

    dy_even = [dy_own, swap(dy_own, 2), swap(dy_own, 4)]
    x1[0], wqkv, tables, dy_even, turn_t = tie(x1[0], wqkv, tables, dy_even, turn_t)
    if one_team:
        wo = x1[0][:, span:].reshape(QW, width)
    qkv = [qkv_of(x1[0], span, wqkv, tables)]
    if mates == 2:
        theirs, qkv = tie(swap(x1[0], 1), qkv)
        x1.append(theirs)
        qkv.append(qkv_of(theirs, span, wqkv, tables))
    other, lse_other = attend(slots, order, qkv[-1], [])
    heads, lse = (other, lse_other) if mates == 1 else attend(slots, order, qkv[0], [swap(other, 1)])
    dy_even.append(swap(dy_even[0], 6))
    heads, wo = tie(heads, wo)
    wo_all = chip_mates([wo, swap(wo, 2), swap(wo, 4), swap(wo, 6)])
    dy_all = stack(ids, chip_mates(dy_even))
    traded = across(heads)
    traded, wo_all, dy_all = tie(traded, wo_all, dy_all)

    traded = traded.reshape(TEAM, *traded.shape[2:])
    middle, top, low = middle_of(member_at, tok, traded, wo_all)
    even_a = [top, swap(top, 2), swap(top, 4)]
    even_a.append(swap(top, 6))
    x2_a = chip_mates(even_a)
    x2_a, low = tie(x2_a, low)
    even_b = [low, swap(low, 2), swap(low, 4), swap(low, 6)]
    *parts_a, hidden, dgu, x2_all = feed(0, x2_a, dy_all, packed, None)
    even_b, parts_a, hidden, dgu, x2_all = tie(even_b, parts_a, hidden, dgu, x2_all)
    odds_a = [swap(parts_a[1], 1), swap(parts_a[3], 1)]
    x2_b = chip_mates(even_b)
    *parts_b, hidden, dgu, x2_all = feed(1, x2_b, dy_all, packed, (hidden, dgu, x2_all))
    dgu = flat(dgu)
    odds_b = [swap(parts_b[1], 1), swap(parts_b[3], 1)]
    g_gate = mm_tn(flat(x2_all), dgu[:, : dgu.shape[1] // 2]).astype(BF16)
    odds_a, odds_b, g_gate = tie(odds_a, odds_b, g_gate)
    got_b = mates_all(member, [parts_a[0], parts_a[2], *odds_a, parts_b[0], parts_b[2], *odds_b])
    got_b, x2_all, dy_all, hidden = tie(got_b, x2_all, dy_all, hidden)
    got_b = chip_sums(got_b)
    g_up = mm_tn(flat(x2_all), dgu[:, dgu.shape[1] // 2 :]).astype(BF16)
    g_down = mm_tn(flat(hidden), flat(dy_all)).astype(BF16)
    if one_team:
        g_ff = pack_back(g_gate, g_up, g_down)
        g_ff = lax.psum_scatter(g_ff.reshape(-1, g_ff.shape[-1]), "ctx", scatter_dimension=0, tiled=True)
    mixed_parts = parts_of(hidden, packed, width)
    got_b, mixed_parts = tie(got_b, mixed_parts)
    sums = (got_b,)
    d_middle, d_low, d_heads = d_middle_of(member_at, sums, middle, dy_own, wo_all)

    hidden, d_low, d_heads = tie(hidden, d_low, d_heads)
    d_heads = across(d_heads.reshape(n_ctx, mates, *d_heads.shape[1:]))
    mixed_own, mixed_sums = mates_trade(mixed_parts)
    mixed_got = hop(mixed_sums)
    out_parts = grad_out_parts(member_at, traded, d_low)
    d_heads, mixed_got, out_parts = tie(d_heads, mixed_got, out_parts)

    d_other = d_heads if mates == 1 else swap(d_heads[:, 1:], 1)
    d_qkv, more = [attend_back(slots, qkv[-1], d_other, lse_other, turn_t)], []
    if mates == 2:
        more = [swap(input_all(d_qkv[0], wqkv), 1)]
        d_qkv = [attend_back(slots, qkv[0], d_heads, lse, turn_t), *d_qkv]
    d_qkv, more = tie(d_qkv, more)
    e1 = input_own(d_qkv[0], wqkv, more)
    e1, d_qkv, mixed_got, out_parts = tie(e1, d_qkv, mixed_got, out_parts)
    e1 = lax.psum_scatter(e1, "ctx", scatter_dimension=0)

    g_qkv = mm_tn(flat(x1[0][:, :span]), flat(d_qkv[0]))
    for a, b in zip(x1[1:], d_qkv[1:]):
        g_qkv = g_qkv + mm_tn(flat(a[:, :span]), flat(b))
    if one_team:
        ff = g_ff.shape[1]
        cut = TEAM * rows
        ways, g_ff, out_parts = tie(pieces_of(member, g_qkv), g_ff, out_parts)
        g_gu = jnp.concatenate([g_ff[:cut].reshape(TEAM, rows, ff), g_ff[cut : 2 * cut].reshape(TEAM, rows, ff)], axis=2)
        g_gu = lax.all_to_all(g_gu, "dp", 0, 0, tiled=True)
        out_own, out_sums = mates_trade(out_parts)
        ways, out_sums = tie([ways[0], *hop(ways[1:])], out_sums)
        home = ways[0].astype(F32)
        for way in ways[1:]:
            home = home + way.astype(F32)
        home = home.astype(BF16).reshape(mates, n_ctx, rows, QKV)
        home, g_gu = tie(jnp.stack([home[0], swap(home[1], 1)], axis=1), g_gu)
        home = across(home).reshape(TEAM, rows, QKV)
        g_gu, mixed_got = tie(g_gu, mixed_got)
        g_out = total_of(out_own, hop(out_sums)).astype(BF16)
        out_ring = ring_trade(g_out.reshape(n_ctx, -1, width))
        down = g_ff[2 * cut :].reshape(width // ff, -1, ff)
        grad_down = jnp.concatenate([down[i] for i in range(width // ff)], axis=1).astype(F32)
    else:
        home = columns_out(g_qkv, head)
        g_gu = columns_out(jnp.concatenate([g_gate, g_up], axis=1), here)
        out_own, out_sums = mates_trade(out_parts)
        grad_down, grad_out = rows_out(g_down), rows_out(total_of(out_own, hop(out_sums)))
    mixed = (middle + total_of(mixed_own, mixed_got)).astype(BF16)[None]
    token_grad = token_gradient(e1, tok, d_middle)
    *grads_gu, gain_f_grad = gradients(ids, gain_f, g_gu, (w_gate, w_up))
    if one_team:
        home, token_grad, mixed, gain_f_grad = tie(home, token_grad, mixed, gain_f_grad)
    *grads_qkv, gain_a_grad = gradients(head_at if one_team else ids, gain_a, home, (w_query, w_key, w_value))
    if one_team:
        out_ring, gain_a_grad = tie(out_ring, gain_a_grad)
        grad_out = sum(t.astype(F32) for t in out_ring[1:]) + out_ring[0].astype(F32)
    return (
        mixed,
        token_grad[None],
        gain_a_grad[0],
        *grads_qkv,
        grad_out,
        gain_f_grad[0],
        *grads_gu,
        grad_down,
    )


def solution(mesh):
    act = P("dp", "ctx", None)
    vec = P(("dp", "ctx"))
    mat = P(("dp", "ctx"), None)
    return jax.shard_map(
        local,
        mesh=mesh,
        in_specs=(act, act, vec, mat, mat, mat, mat, vec, mat, mat, mat, P()),
        out_specs=(act, act, vec, mat, mat, mat, mat, vec, mat, mat, mat),
        check_vma=False,
    )
```

```python
import functools

import jax
import jax.numpy as jnp
from jax import lax
from jax.experimental import pallas as pl
from jax.experimental.pallas import tpu as pltpu
from jax.sharding import PartitionSpec as P

HEADS = 16
KV_HEADS = 8
HEAD_DIM = 96
GROUPS = HEADS // KV_HEADS
HALF = HEAD_DIM // 2
QW = GROUPS * HEAD_DIM
QKV = QW + 2 * HEAD_DIM

EPS = 1e-05
THETA = 100000.0
F32 = jnp.float32
BF16 = jnp.bfloat16
CHUNKS = 4
VMEM_BYTES = 56 * 2**20
SMALL_BYTES = 24 * 2**20

TEAM = KV_HEADS
PAIRS = TEAM // 2


def dot(a, b, dims):
    return lax.dot_general(a, b, (dims, ((), ())), preferred_element_type=F32)


def mm(a, b):
    return dot(a, b, ((1,), (0,)))


def mm_nt(a, b):
    return dot(a, b, ((1,), (1,)))


def mm_tn(a, b):
    return dot(a, b, ((0,), (0,)))


def swap(value, bit):
    n = lax.axis_size("dp")
    return lax.ppermute(value, "dp", [(i, i ^ bit) for i in range(n)])


def after(value, *others):
    return lax.optimization_barrier((value, *others))[0]


def params(limit=VMEM_BYTES):
    return pltpu.CompilerParams(vmem_limit_bytes=limit)


def cost(flops, nbytes, exps=0):
    return pl.CostEstimate(flops=int(3 * flops), bytes_accessed=int(3 * nbytes), transcendentals=int(exps))


def whole(shape):
    return pl.BlockSpec(shape, lambda *_: (0,) * len(shape))


def join(even_ref, odd_ref):
    return jnp.concatenate([even_ref[...], odd_ref[...]], axis=0)


def qkv_kernel(x_ref, w_ref, cos_ref, sin_ref, out_ref):
    scale = HEAD_DIM**-0.5
    cosine, sine = cos_ref[...], sin_ref[...]
    cosine = jnp.concatenate([cosine * scale] * GROUPS + [cosine, jnp.ones_like(cosine)], axis=1)
    sine = jnp.concatenate([sine * scale] * GROUPS + [sine, jnp.zeros_like(sine)], axis=1)
    first = lax.broadcasted_iota(jnp.int32, cosine.shape, 1) % HEAD_DIM < HALF
    y = mm(x_ref[0], w_ref[...])
    partner = jnp.where(first, pltpu.roll(y, QKV - HALF, 1), pltpu.roll(y, HALF, 1))
    out_ref[0] = (y * cosine + partner * sine).astype(BF16)


def qkv_of(x, span, w, tables):
    n_ctx, _, width = x.shape
    return pl.pallas_call(
        qkv_kernel,
        grid=(n_ctx,),
        in_specs=[pl.BlockSpec((1, span, width), lambda i: (i, 0, 0)), whole(w.shape)]
        + [pl.BlockSpec((span, HEAD_DIM), lambda i: (i, 0))] * 2,
        out_specs=pl.BlockSpec((1, span, QKV), lambda i: (i, 0, 0)),
        out_shape=jax.ShapeDtypeStruct((n_ctx, span, QKV), BF16),
        compiler_params=params(SMALL_BYTES),
        cost_estimate=cost(2 * n_ctx * span * width * QKV, 2 * n_ctx * span * width + 2 * width * QKV),
        name="qkv",
    )(x, w, *tables)


def first_kernel(x_ref, w_ref, out_ref):
    rows = x_ref.shape[0]
    x = x_ref[...].astype(F32)
    r = lax.rsqrt(jnp.mean(x * x, axis=-1, keepdims=True) + EPS)
    out_ref[:rows] = (x * r).astype(BF16)
    out_ref[rows:] = w_ref[...]


def first_of(x, w):
    out = (x.shape[0] + w.shape[0], x.shape[1])
    return pl.pallas_call(
        first_kernel,
        grid=(1,),
        in_specs=[whole(x.shape), whole(w.shape)],
        out_specs=whole(out),
        out_shape=jax.ShapeDtypeStruct(out, BF16),
        compiler_params=params(),
        cost_estimate=cost(6 * x.size, 4 * out[0] * out[1]),
        name="first",
    )(x, w)


def rows_kernel(member_ref, *refs):
    pieces, out_ref = refs[:-1], refs[-1]
    n_ctx, _, rows, _ = pieces[0].shape
    for p, piece in enumerate(pieces):
        for c in range(n_ctx):
            for j in range(2):
                at = pl.multiple_of((member_ref[2 * p + j] * n_ctx + c) * rows, 16)
                out_ref[pl.ds(at, rows), :] = piece[c, j]


def rows_of(member, pieces):
    n_ctx, two, rows, width = pieces[0].shape
    out = (len(pieces) * n_ctx * two * rows, width)
    return pl.pallas_call(
        rows_kernel,
        grid_spec=pltpu.PrefetchScalarGridSpec(
            num_scalar_prefetch=1,
            grid=(1,),
            in_specs=[whole(t.shape) for t in pieces],
            out_specs=whole(out),
        ),
        out_shape=jax.ShapeDtypeStruct(out, BF16),
        compiler_params=params(SMALL_BYTES),
        cost_estimate=cost(0, 4 * out[0] * out[1]),
        name="rows",
    )(member, *pieces)


def pieces_kernel(member_ref, grad_ref, *out_refs):
    for p, out_ref in enumerate(out_refs):
        for j in range(2):
            out_ref[j] = grad_ref[member_ref[2 * p + j]].astype(BF16)


def pieces_of(member, grad):
    rows, width = grad.shape[0] // TEAM, grad.shape[1]
    return pl.pallas_call(
        pieces_kernel,
        grid_spec=pltpu.PrefetchScalarGridSpec(
            num_scalar_prefetch=1,
            grid=(1,),
            in_specs=[whole((TEAM, rows, width))],
            out_specs=(whole((2, rows, width)),) * PAIRS,
        ),
        out_shape=(jax.ShapeDtypeStruct((2, rows, width), BF16),) * PAIRS,
        compiler_params=params(SMALL_BYTES),
        cost_estimate=cost(0, 6 * grad.size),
        name="pieces",
    )(member, grad.reshape(TEAM, rows, width))


def stack_kernel(order_ref, *refs):
    for k, ref in enumerate(refs[:-1]):
        refs[-1][order_ref[k]] = ref[...]


def stack(order, xs):
    rows, width = xs[0].shape
    steps = 4
    block = rows // steps
    return pl.pallas_call(
        stack_kernel,
        grid_spec=pltpu.PrefetchScalarGridSpec(
            num_scalar_prefetch=1,
            grid=(steps,),
            in_specs=[pl.BlockSpec((block, width), lambda i, m: (i, 0))] * len(xs),
            out_specs=pl.BlockSpec((len(xs), block, width), lambda i, m: (0, i, 0)),
        ),
        out_shape=jax.ShapeDtypeStruct((len(xs), rows, width), BF16),
        compiler_params=params(),
        cost_estimate=cost(0, 4 * len(xs) * rows * width),
        name="stack",
    )(order, *xs)


def in_order(slots_ref, ref, scratch, half):
    for b in range(slots_ref.shape[0]):
        slot = slots_ref[b]
        at = pl.multiple_of((slot % 2) * half, half)
        scratch[pl.ds(b * half, half), :] = ref[slot // 2, pl.ds(at, half), :]


def heads_in_order(slots_ref, ref, scratch, half):
    for b in range(slots_ref.shape[0]):
        slot = slots_ref[b]
        first, second = ref[slot // 2, 0, :, :QW], ref[slot // 2, 0, :, QW:]
        scratch[pl.ds(b * half, half), :] = jnp.where(slot % 2 == 0, first, second)


def heads_out_of_order(order_ref, ref, scratch, half):
    for c in range(ref.shape[0]):
        for j in range(2):
            at = pl.multiple_of(order_ref[2 * c + j] * half, half)
            ref[c, 0, :, j * QW : (j + 1) * QW] = scratch[pl.ds(at, half), :]


def out_of_order(slots_ref, ref, first, value, half):
    for b in range(value.shape[0] // half):
        slot = slots_ref[first // half + b]
        at = pl.multiple_of((slot % 2) * half, half)
        ref[slot // 2, pl.ds(at, half), :] = value[b * half : (b + 1) * half]


def flip(value):
    return value.astype(F32).T


def stacked_heads(ref, rows):
    return jnp.concatenate([ref[rows, g * HEAD_DIM : (g + 1) * HEAD_DIM] for g in range(GROUPS)], axis=0)


def causal(size):
    key = lax.broadcasted_iota(jnp.int32, (size, GROUPS * size), 0)
    query = lax.broadcasted_iota(jnp.int32, (size, GROUPS * size), 1) % size
    return key <= query


def attend_kernel(slots_ref, order_ref, qkv_ref, *refs):
    more, (out_ref, lse_ref, scratch, o_scr) = refs[:-4], refs[-4:]
    half = qkv_ref.shape[1] // 2
    size = scratch.shape[0] // CHUNKS
    in_order(slots_ref, qkv_ref, scratch, half)
    v_t = flip(scratch[:, QW + HEAD_DIM :]).astype(BF16)
    allowed = causal(size)
    for i in range(CHUNKS):
        lo, hi = i * size, (i + 1) * size
        q = stacked_heads(scratch, slice(lo, hi))
        k_near = scratch[lo:hi, QW : QW + HEAD_DIM]
        near = jnp.where(allowed, mm_nt(k_near, q), -1e30)
        top = jnp.max(near, axis=0, keepdims=True)
        if i > 0:
            far = mm_nt(scratch[:lo, QW : QW + HEAD_DIM], q)
            top = jnp.maximum(top, jnp.max(far, axis=0, keepdims=True))
        near = jnp.exp(near - top)
        total = jnp.sum(near, axis=0, keepdims=True)
        acc = mm(v_t[:, lo:hi], near.astype(BF16))
        if i > 0:
            far = jnp.exp(far - top)
            total = total + jnp.sum(far, axis=0, keepdims=True)
            acc = acc + mm(v_t[:, :lo], far.astype(BF16))
        lse_ref[pl.ds(i, 1), :] = top + jnp.log(total)
        o = (acc / total).T.astype(BF16)
        for g in range(GROUPS):
            o_scr[lo:hi, g * HEAD_DIM : (g + 1) * HEAD_DIM] = o[g * size : (g + 1) * size]
    heads_out_of_order(order_ref, out_ref, o_scr, half)
    for ref in more:
        out_ref[:, 1] = ref[:, 0]


def attend_back_kernel(slots_ref, qkv_ref, do_ref, lse_ref, turn_ref, out_ref, scratch, do_scr, dk_scr, dv_scr):
    half = qkv_ref.shape[1] // 2
    length = scratch.shape[0]
    cos_ref, sin_ref = turn_ref.at[:HALF], turn_ref.at[HALF:]
    size = length // CHUNKS
    scale = HEAD_DIM**-0.5
    in_order(slots_ref, qkv_ref, scratch, half)
    heads_in_order(slots_ref, do_ref, do_scr, half)
    k_t = flip(scratch[:, QW : QW + HEAD_DIM]).astype(BF16)
    allowed = causal(size)
    dk_scr[...] = jnp.zeros_like(dk_scr)
    dv_scr[...] = jnp.zeros_like(dv_scr)
    for i in range(CHUNKS):
        lo, hi = i * size, (i + 1) * size
        q = stacked_heads(scratch, slice(lo, hi))
        do = stacked_heads(do_scr, slice(lo, hi))
        lse = lse_ref[pl.ds(i, 1), :]
        spans = [(lo, hi)] + ([(0, lo)] if i > 0 else [])
        probs, prods = [], []
        delta = 0.0
        for at, (a, b) in enumerate(spans):
            p = jnp.exp(mm_nt(scratch[a:b, QW : QW + HEAD_DIM], q) - lse)
            if at == 0:
                p = jnp.where(allowed, p, 0.0)
            prod = p * mm_nt(scratch[a:b, QW + HEAD_DIM :], do)
            delta = delta + jnp.sum(prod, axis=0, keepdims=True)
            probs.append(p)
            prods.append(prod)
        dq_t = 0.0
        for (a, b), p, prod in zip(spans, probs, prods):
            ds = (prod - p * delta).astype(BF16)
            dk_scr[a:b, :] += mm(ds, q)
            dv_scr[a:b, :] += mm(p.astype(BF16), do)
            dq_t = dq_t + mm(k_t[:, a:b], ds)
        c = jnp.concatenate([cos_ref[:, lo:hi]] * GROUPS, axis=1) * scale
        s = jnp.concatenate([sin_ref[:, lo:hi]] * GROUPS, axis=1) * scale
        first, second = dq_t[:HALF], dq_t[HALF:]
        dq = jnp.concatenate([first * c + second * s, second * c - first * s], axis=0).T
        for g in range(GROUPS):
            do_scr[lo:hi, g * HEAD_DIM : (g + 1) * HEAD_DIM] = dq[g * size : (g + 1) * size].astype(BF16)
    for i in range(CHUNKS):
        lo, hi = i * size, (i + 1) * size
        dk_t = dk_scr[lo:hi, :].T
        first, second = dk_t[:HALF], dk_t[HALF:]
        c, s = cos_ref[:, lo:hi], sin_ref[:, lo:hi]
        dk = jnp.concatenate([first * c + second * s, second * c - first * s], axis=0).T
        value = jnp.concatenate([do_scr[lo:hi, :], dk.astype(BF16), dv_scr[lo:hi, :].astype(BF16)], axis=1)
        out_of_order(slots_ref, out_ref, lo, value, half)


def attend(slots, order, qkv, more):
    n_ctx, span, _ = qkv.shape
    length = n_ctx * span
    heads = (n_ctx, 1 + len(more), span // 2, 2 * QW)
    lse = (CHUNKS, GROUPS * length // CHUNKS)
    work = GROUPS * length * length
    return pl.pallas_call(
        attend_kernel,
        grid_spec=pltpu.PrefetchScalarGridSpec(
            num_scalar_prefetch=2,
            grid=(1,),
            in_specs=[whole(t.shape) for t in (qkv, *more)],
            out_specs=(whole(heads), whole(lse)),
            scratch_shapes=[pltpu.VMEM((length, QKV), BF16), pltpu.VMEM((length, QW), BF16)],
        ),
        out_shape=(jax.ShapeDtypeStruct(heads, BF16), jax.ShapeDtypeStruct(lse, F32)),
        compiler_params=params(SMALL_BYTES),
        cost_estimate=cost(work * 2 * HEAD_DIM * 3, 2 * length * (QKV + QW), work // 2),
        name="attend",
    )(slots, order, qkv, *more)


def attend_back(slots, qkv, d_heads, lse, turn_t):
    n_ctx, span, _ = qkv.shape
    length = n_ctx * span
    work = GROUPS * length * length
    return pl.pallas_call(
        attend_back_kernel,
        grid_spec=pltpu.PrefetchScalarGridSpec(
            num_scalar_prefetch=1,
            grid=(1,),
            in_specs=[
                whole(qkv.shape),
                whole((n_ctx, 1, *d_heads.shape[2:])),
            ]
            + [whole(t.shape) for t in (lse, turn_t)],
            out_specs=whole((n_ctx, span, QKV)),
            scratch_shapes=[
                pltpu.VMEM((length, QKV), BF16),
                pltpu.VMEM((length, QW), BF16),
                pltpu.VMEM((length, HEAD_DIM), F32),
                pltpu.VMEM((length, HEAD_DIM), F32),
            ],
        ),
        out_shape=jax.ShapeDtypeStruct((n_ctx, span, QKV), BF16),
        compiler_params=params(SMALL_BYTES),
        cost_estimate=cost(work * 2 * HEAD_DIM * 8, 4 * length * QKV, work // 2),
        name="attend_back",
    )(slots, qkv, d_heads, lse, turn_t)


def parts_kernel(a_ref, packed, *refs):
    out_refs, (wd_ref, sem) = refs[:4], refs[4:]

    @pl.when(pl.program_id(0) == 0)
    def _():
        copies = [pltpu.make_async_copy(src, dst, sem.at[i]) for i, (src, dst) in enumerate(down_ways(packed, wd_ref))]
        for copy in copies:
            copy.start()
        for copy in copies:
            copy.wait()

    block = a_ref.shape[1]
    y = mm(jnp.concatenate([a_ref[k] for k in range(TEAM)], axis=0), wd_ref[...]).astype(BF16)
    for k in range(TEAM):
        out_refs[k // 4 * 2 + k % 2][k // 2 % 2] = y[k * block : (k + 1) * block]


def parts_of(a, packed, width):
    _, rows, depth = a.shape
    steps = 4
    block = rows // steps
    return pl.pallas_call(
        parts_kernel,
        grid=(steps,),
        in_specs=[pl.BlockSpec((TEAM, block, depth), lambda i: (0, i, 0)), pl.BlockSpec(memory_space=pl.ANY)],
        out_specs=(pl.BlockSpec((2, block, width), lambda i: (0, i, 0)),) * 4,
        out_shape=(jax.ShapeDtypeStruct((2, rows, width), BF16),) * 4,
        scratch_shapes=[
            pltpu.VMEM((depth, width), BF16),
            pltpu.SemaphoreType.DMA((packed.shape[0] * (width // depth),)),
        ],
        compiler_params=params(SMALL_BYTES),
        cost_estimate=cost(2 * TEAM * rows * depth * width, 2 * TEAM * rows * (width + depth) + 2 * depth * width),
        name="parts",
    )(a, packed)


def input_own_kernel(a_ref, w_ref, *refs):
    y = mm_nt(a_ref[0], w_ref[...])
    for ref in refs[:-1]:
        y = y + ref[0].astype(F32)
    refs[-1][0] = y.astype(BF16)


def input_own(a, w, more):
    n_ctx, span, depth = a.shape
    width = w.shape[0]
    blocked = lambda n: pl.BlockSpec((1, span, n), lambda i: (i, 0, 0))
    return pl.pallas_call(
        input_own_kernel,
        grid=(n_ctx,),
        in_specs=[blocked(depth), whole(w.shape)] + [blocked(width)] * len(more),
        out_specs=blocked(width),
        out_shape=jax.ShapeDtypeStruct((n_ctx, span, width), BF16),
        compiler_params=params(SMALL_BYTES),
        cost_estimate=cost(2 * n_ctx * span * depth * width, 4 * n_ctx * span * (width + depth) + 2 * depth * width),
        name="input_own",
    )(a, w, *more)


def input_all_kernel(a_ref, w_ref, out_ref):
    out_ref[0] = mm_nt(a_ref[0], w_ref[...]).astype(BF16)


def input_all(a, w):
    n_ctx, span, depth = a.shape
    width = w.shape[0]
    blocked = lambda n: pl.BlockSpec((1, span, n), lambda i: (i, 0, 0))
    return pl.pallas_call(
        input_all_kernel,
        grid=(n_ctx,),
        in_specs=[blocked(depth), whole(w.shape)],
        out_specs=blocked(width),
        out_shape=jax.ShapeDtypeStruct((n_ctx, span, width), BF16),
        compiler_params=params(SMALL_BYTES),
        cost_estimate=cost(2 * n_ctx * span * depth * width, 4 * n_ctx * span * (width + depth) + 2 * depth * width),
        name="input_all",
    )(a, w)


def grad_out_kernel(at_ref, heads_ref, dm_ref, *out_refs):
    dm = dm_ref[...]
    for k in range(TEAM):
        y = mm_tn(unfold(heads_ref[at_ref[k]]), dm)
        out_refs[k // 4 * 2 + k % 2][k // 2 % 2] = y.astype(BF16)


def grad_out_parts(member_at, heads, dm):
    rows, width = dm.shape
    return pl.pallas_call(
        grad_out_kernel,
        grid_spec=pltpu.PrefetchScalarGridSpec(
            num_scalar_prefetch=1,
            grid=(1,),
            in_specs=[whole(t.shape) for t in (heads, dm)],
            out_specs=(whole((2, QW, width)),) * 4,
        ),
        out_shape=(jax.ShapeDtypeStruct((2, QW, width), BF16),) * 4,
        compiler_params=params(),
        cost_estimate=cost(2 * TEAM * rows * QW * width, 2 * TEAM * QW * width),
        name="grad_out",
    )(member_at, heads, dm)


def unfold(block):
    return jnp.concatenate([block[:, :QW], block[:, QW:]], axis=0)


def fetch(any_refs, ref, sem):
    copies = [pltpu.make_async_copy(a, ref.at[k], sem.at[k]) for k, a in enumerate(any_refs)]
    for copy in copies:
        copy.start()
    return copies


def fetched(arrays):
    specs = [pl.BlockSpec(memory_space=pl.ANY)] * len(arrays)
    scratch = [pltpu.VMEM((len(arrays), *arrays[0].shape), BF16), pltpu.SemaphoreType.DMA((len(arrays),))]
    return specs, scratch


def middle_kernel(at_ref, heads_ref, x_ref, *refs):
    wo_any, (middle_ref, top_ref, low_ref, wo_ref, sem) = refs[:TEAM], refs[TEAM:]
    copies = fetch(wo_any, wo_ref, sem)
    heads = jnp.concatenate([unfold(heads_ref[at_ref[k]]) for k in range(TEAM)], axis=1)
    acc = x_ref[...].astype(F32)
    for first in (0, PAIRS):
        some = slice(first, first + PAIRS)
        for copy in copies[some]:
            copy.wait()
        acc = acc + mm(heads[:, first * QW : (first + PAIRS) * QW], wo_ref[some].reshape(PAIRS * QW, -1))
    middle_ref[...] = acc
    r = lax.rsqrt(jnp.mean(acc * acc, axis=-1, keepdims=True) + EPS)
    xhat = (acc * r).astype(BF16)
    half = top_ref.shape[0]
    top_ref[...] = xhat[:half]
    low_ref[...] = xhat[half:]


def middle_of(member_at, x, heads, wo):
    rows, width = x.shape
    specs, scratch = fetched(wo)
    return pl.pallas_call(
        middle_kernel,
        grid_spec=pltpu.PrefetchScalarGridSpec(
            num_scalar_prefetch=1,
            grid=(1,),
            in_specs=[whole(t.shape) for t in (heads, x)] + specs,
            out_specs=(whole(x.shape),) + (whole((rows // 2, width)),) * 2,
            scratch_shapes=scratch,
        ),
        out_shape=(jax.ShapeDtypeStruct(x.shape, F32),) + (jax.ShapeDtypeStruct((rows // 2, width), BF16),) * 2,
        compiler_params=params(),
        cost_estimate=cost(2 * rows * width * TEAM * QW, 2 * width * TEAM * QW + 12 * rows * width),
        name="middle",
    )(member_at, heads, x, *wo)


def d_middle_kernel(at_ref, *refs):
    middle_ref, dy_ref = refs[1:3]
    wo_any, (low_ref, out_ref, wo_ref, sem) = refs[3 : 3 + TEAM], refs[3 + TEAM :]
    copies = fetch(wo_any, wo_ref, sem)
    middle = middle_ref[...]
    half = middle.shape[0] // 2
    r = lax.rsqrt(jnp.mean(middle * middle, axis=-1, keepdims=True) + EPS)
    d = dy_ref[...].astype(F32) + norm_back(team_total(refs[:1]), middle * r, r)
    low = d.astype(BF16)
    low_ref[...] = low
    for first in (0, PAIRS):
        some = slice(first, first + PAIRS)
        for copy in copies[some]:
            copy.wait()
        y = mm_nt(low, wo_ref[some].reshape(PAIRS * QW, -1)).astype(BF16)
        for k in range(PAIRS):
            part = slice(k * QW, (k + 1) * QW)
            out_ref[at_ref[first + k], :, :QW] = y[:half, part]
            out_ref[at_ref[first + k], :, QW:] = y[half:, part]


def d_middle_of(member_at, sums, middle, dy, wo):
    rows, width = dy.shape
    heads = (TEAM, rows // 2, 2 * QW)
    specs, scratch = fetched(wo)
    return pl.pallas_call(
        d_middle_kernel,
        grid_spec=pltpu.PrefetchScalarGridSpec(
            num_scalar_prefetch=1,
            grid=(1,),
            in_specs=[whole(t.shape) for t in (*sums, middle, dy)] + specs,
            out_specs=(whole(dy.shape), whole(heads)),
            scratch_shapes=scratch,
        ),
        out_shape=(
            jax.ShapeDtypeStruct(dy.shape, BF16),
            jax.ShapeDtypeStruct(heads, BF16),
        ),
        compiler_params=params(),
        cost_estimate=cost(2 * rows * width * TEAM * QW, 2 * width * TEAM * QW + 18 * rows * width),
        name="d_middle",
    )(member_at, *sums, middle, dy, *wo)


def mates_kernel(*refs):
    evens, odds, outs = refs[:2], refs[2:4], refs[4:]
    for j, k in enumerate((2, 4, 6)):
        r = evens[k // 4][k // 2 % 2].astype(F32) + odds[k // 4][k // 2 % 2].astype(F32)
        outs[j][...] = r.astype(BF16)


def mates_sum(evens, odds):
    _, rows, width = evens[0].shape
    steps = 2
    block = rows // steps
    return pl.pallas_call(
        mates_kernel,
        grid=(steps,),
        in_specs=[pl.BlockSpec((2, block, width), lambda i: (0, i, 0))] * 4,
        out_specs=(pl.BlockSpec((block, width), lambda i: (i, 0)),) * 3,
        out_shape=(jax.ShapeDtypeStruct((rows, width), BF16),) * 3,
        compiler_params=params(SMALL_BYTES),
        cost_estimate=cost(6 * rows * width, 36 * rows * width),
        name="mates_sum",
    )(*evens, *odds)


def mates_all_kernel(member_ref, *refs):
    out_ref = refs[-1]
    for half in range(2):
        evens, odds = refs[4 * half : 4 * half + 2], refs[4 * half + 2 : 4 * half + 4]
        rows = evens[0].shape[1]
        for k in (0, 2, 4, 6):
            r = evens[k // 4][k // 2 % 2].astype(F32) + odds[k // 4][k // 2 % 2].astype(F32)
            out_ref[member_ref[k] // 2, half * rows : (half + 1) * rows] = r.astype(BF16)


def mates_all(member, parts):
    _, rows, width = parts[0].shape
    out = (PAIRS, 2 * rows, width)
    return pl.pallas_call(
        mates_all_kernel,
        grid_spec=pltpu.PrefetchScalarGridSpec(
            num_scalar_prefetch=1,
            grid=(1,),
            in_specs=[whole(t.shape) for t in parts],
            out_specs=whole(out),
        ),
        out_shape=jax.ShapeDtypeStruct(out, BF16),
        compiler_params=params(SMALL_BYTES),
        cost_estimate=cost(16 * rows * width, 96 * rows * width),
        name="mates_all",
    )(member, *parts)


def team_total(refs):
    return jnp.sum(refs[0][...].astype(F32), axis=0)


def token_kernel(e_ref, x_ref, d_ref, out_ref):
    x = x_ref[...].astype(F32)
    r = lax.rsqrt(jnp.mean(x * x, axis=-1, keepdims=True) + EPS)
    out_ref[...] = d_ref[...].astype(F32) + norm_back(e_ref[...].astype(F32), x * r, r)


def token_gradient(e, x, d_middle):
    rows, width = x.shape
    block = rows // 2
    return pl.pallas_call(
        token_kernel,
        grid=(2,),
        in_specs=[pl.BlockSpec((block, width), lambda i: (i, 0))] * 3,
        out_specs=pl.BlockSpec((block, width), lambda i: (i, 0)),
        out_shape=jax.ShapeDtypeStruct(x.shape, F32),
        compiler_params=params(),
        cost_estimate=cost(12 * x.size, 20 * x.size),
        name="token_gradient",
    )(e, x, d_middle)


def pack(gate_up, down):
    _, rows, twice = gate_up.shape
    ff = twice // 2
    blocks = [gate_up[..., :ff].reshape(-1, ff), gate_up[..., ff:].reshape(-1, ff)]
    return jnp.concatenate(blocks + [down[:, i : i + ff] for i in range(0, down.shape[1], ff)], axis=0)


def pack_back(gate, up, down):
    n = lax.axis_size("ctx")
    width, ff = gate.shape
    by_ctx = lambda g: jnp.transpose(g.reshape(TEAM, n, -1, ff), (1, 0, 2, 3)).reshape(n, -1, ff)
    blocks = [by_ctx(gate), by_ctx(up)]
    down = down.reshape(n, ff // n, width)
    return jnp.concatenate(blocks + [down[..., i : i + ff] for i in range(0, width, ff)], axis=1)


def down_ways(packed, wd_ref):
    n_ctx, count, ff = packed.shape
    width = wd_ref.shape[1]
    down = ff // n_ctx
    first = count - width // ff * down
    return [
        (packed.at[c, pl.ds(first + i * down, down)], wd_ref.at[pl.ds(c * down, down), pl.ds(i * ff, ff)])
        for c in range(n_ctx)
        for i in range(width // ff)
    ]


def unpack(packed, wgu_ref, wd_ref, sem):
    n_ctx, _, ff = packed.shape
    rows = wgu_ref.shape[0] // (TEAM * n_ctx)
    ways = []
    for part in range(2):
        for c in range(n_ctx):
            for m in range(TEAM):
                out = wgu_ref.at[pl.ds((m * n_ctx + c) * rows, rows), pl.ds(part * ff, ff)]
                ways.append((packed.at[c, pl.ds((part * TEAM + m) * rows, rows)], out))
    ways += down_ways(packed, wd_ref)
    copies = [pltpu.make_async_copy(src, dst, sem.at[i]) for i, (src, dst) in enumerate(ways)]
    for copy in copies:
        copy.start()
    return copies


def feed_kernel(*refs):
    x_refs = refs[:TEAM]
    y_ref, packed = refs[TEAM : TEAM + 2]
    even0_ref, odd0_ref, even1_ref, odd1_ref, hidden_ref, dgu_ref, xc_ref, wgu_ref, wd_ref, sem = refs[-10:]
    ff = wd_ref.shape[0]
    block = x_refs[0].shape[0]

    @pl.when(pl.program_id(0) == 0)
    def _():
        for copy in unpack(packed, wgu_ref, wd_ref, sem):
            copy.wait()

    for j in range(TEAM):
        xc_ref[j] = x_refs[j][...]
    x = jnp.concatenate([ref[...] for ref in x_refs], axis=0)
    y = y_ref[...].reshape(TEAM * block, y_ref.shape[2])
    gate = mm(x, wgu_ref[:, :ff])
    upper = mm(x, wgu_ref[:, ff:])
    d_hidden = mm_nt(y, wd_ref[...])
    sigma = jax.nn.sigmoid(gate)
    act = gate * sigma
    hidden = (act * upper).astype(BF16)
    d_gate = (d_hidden * upper * sigma * (1.0 + gate * (1.0 - sigma))).astype(BF16)
    dgu = jnp.concatenate([d_gate, (d_hidden * act).astype(BF16)], axis=1)
    e = mm_nt(dgu, wgu_ref[...]).astype(BF16)
    outs = (even0_ref, odd0_ref, even1_ref, odd1_ref)
    for j in range(TEAM):
        part = slice(j * block, (j + 1) * block)
        hidden_ref[j] = hidden[part]
        dgu_ref[j] = dgu[part]
        outs[j // 4 * 2 + j % 2][j // 2 % 2] = e[part]


def feed(part, xs, y, packed, held):
    rows, width = xs[0].shape
    n_ctx, packed_rows, ff = packed.shape
    steps = 4
    block = rows // steps
    widths = (ff, 2 * ff, width)
    extra = [] if held is None else list(held)
    at_part = lambda n: pl.BlockSpec((TEAM, block, n), lambda i: (0, part * steps + i, 0))
    return pl.pallas_call(
        feed_kernel,
        grid=(steps,),
        in_specs=[pl.BlockSpec((block, width), lambda i: (i, 0))] * TEAM
        + [at_part(width)]
        + [pl.BlockSpec(memory_space=pl.ANY)] * (1 + len(extra)),
        out_specs=(pl.BlockSpec((2, block, width), lambda i: (0, i, 0)),) * 4 + tuple(at_part(n) for n in widths),
        out_shape=(jax.ShapeDtypeStruct((2, rows, width), BF16),) * 4
        + tuple(jax.ShapeDtypeStruct((TEAM, 2 * rows, n), BF16) for n in widths),
        input_output_aliases={TEAM + 2 + i: 4 + i for i in range(len(extra))},
        scratch_shapes=[
            pltpu.VMEM((width, 2 * ff), BF16),
            pltpu.VMEM((ff, width), BF16),
            pltpu.SemaphoreType.DMA((n_ctx * (2 * TEAM + width // ff),)),
        ],
        compiler_params=params(),
        cost_estimate=cost(2 * TEAM * rows * width * 5 * ff, 6 * width * ff + 18 * TEAM * rows * width, TEAM * rows * ff),
        name="feed",
    )(*xs, y, packed, *extra)


def fold_kernel(widths, at_ref, gain_ref, *refs):
    weights, out_ref = refs[:-1], refs[-1]
    gain = gain_ref[...]
    for m in range(TEAM):
        at = 0
        for n, ref in zip(widths, weights):
            out_ref[at_ref[m], :, at : at + n] = (ref[:, m * n : (m + 1) * n].astype(F32) * gain).astype(BF16)
            at += n


def fold(places, gain, weights):
    widths = tuple(w.shape[1] // TEAM for w in weights)
    out = (TEAM, weights[0].shape[0], sum(widths))
    return pl.pallas_call(
        functools.partial(fold_kernel, widths),
        grid_spec=pltpu.PrefetchScalarGridSpec(
            num_scalar_prefetch=1,
            grid=(1,),
            in_specs=[whole(t.shape) for t in (gain, *weights)],
            out_specs=whole(out),
        ),
        out_shape=jax.ShapeDtypeStruct(out, BF16),
        compiler_params=params(),
        cost_estimate=cost(out[0] * out[1] * out[2], 4 * out[0] * out[1] * out[2]),
        name="fold",
    )(places, gain, *weights)


def gradients_kernel(widths, at_ref, gain_ref, grad_ref, *refs):
    count = len(widths)
    weights, outs, gain_out = refs[:count], refs[count : 2 * count], refs[2 * count]
    gain = gain_ref[...]
    total = jnp.zeros(gain.shape, F32)
    for m in range(TEAM):
        at = 0
        for n, w_ref, out_ref in zip(widths, weights, outs):
            g = grad_ref[at_ref[m], :, at : at + n].astype(F32)
            here = slice(m * n, (m + 1) * n)
            total = total + jnp.sum(w_ref[:, here].astype(F32) * g, axis=1, keepdims=True)
            out_ref[:, here] = g * gain
            at += n
    gain_out[...] = jnp.broadcast_to(total, (total.shape[0], 128)).T[:1]


def gradients(places, gain, grad, weights):
    widths = tuple(w.shape[1] // TEAM for w in weights)
    outs = [w.shape for w in weights] + [(1, gain.shape[0])]
    return pl.pallas_call(
        functools.partial(gradients_kernel, widths),
        grid_spec=pltpu.PrefetchScalarGridSpec(
            num_scalar_prefetch=1,
            grid=(1,),
            in_specs=[whole(t.shape) for t in (gain, grad, *weights)],
            out_specs=tuple(whole(shape) for shape in outs),
        ),
        out_shape=tuple(jax.ShapeDtypeStruct(shape, F32) for shape in outs),
        compiler_params=params(SMALL_BYTES),
        cost_estimate=cost(4 * grad.size, 8 * grad.size),
        name="gradients",
    )(places, gain, grad, *weights)


def ring_trade(blocks):
    n, here = lax.axis_size("ctx"), lax.axis_index("ctx")
    got = [lax.dynamic_index_in_dim(blocks, here, 0, False)]
    for s in range(1, n):
        block = lax.dynamic_index_in_dim(blocks, (here + s) % n, 0, False)
        got.append(lax.ppermute(block, "ctx", [(i, (i + s) % n) for i in range(n)]))
    return got


def chip_mates(evens):
    pieces = []
    for even in evens:
        pieces += [even, swap(even, 1)]
    return pieces


def tie(*values):
    leaves, tree = jax.tree.flatten(values)
    return jax.tree.unflatten(tree, lax.optimization_barrier(leaves))


def mates_trade(parts):
    evens, odds = (parts[0], parts[2]), (swap(parts[1], 1), swap(parts[3], 1))
    return (evens[0], odds[0]), mates_sum(evens, odds)


def chip_sums(blocks):
    n = lax.axis_size("dp")
    groups = [list(range(f + c, f + TEAM, 2)) for f in range(0, n, TEAM) for c in range(2)]
    return lax.all_to_all(blocks, "dp", 0, 0, axis_index_groups=groups, tiled=True)


def hop(sums):
    return [swap(r, bit) for r, bit in zip(sums, (2, 4, 6))]


def total_of(own, got):
    total = own[0][0].astype(F32) + own[1][0].astype(F32)
    for part in got:
        total = total + part.astype(F32)
    return total


def place_rows(seq_rows, order, half_rows):
    slots = seq_rows // half_rows
    hit = slots[:, None] == jnp.arange(order.shape[0], dtype=jnp.int32)[None, :]
    return jnp.sum(jnp.where(hit, order[None, :], 0), axis=1) * half_rows + seq_rows % half_rows


def angles(places):
    freqs = THETA ** (-(jnp.arange(HALF).astype(F32) * 2.0 / HEAD_DIM))
    return places.astype(F32)[:, None] * freqs[None, :]


def member_columns(own):
    return lax.all_to_all(own, "dp", 0, 0, tiled=True)


def any_columns(own, index):
    n_dp, n_ctx = lax.axis_size("dp"), lax.axis_size("ctx")
    gathered = lax.all_gather(own, ("dp", "ctx"), axis=0)
    mine = lax.dynamic_index_in_dim(gathered, index, 1, False)
    per = n_dp // TEAM
    mine = mine.reshape(TEAM, n_ctx, per * own.shape[1], own.shape[2])
    return jnp.transpose(mine, (1, 0, 2, 3))


def by_rows(columns):
    return jnp.transpose(columns, (1, 0, 2, 3)).reshape(-1, columns.shape[-1])


def any_rows(own):
    gathered = lax.all_gather(own, ("dp", "ctx"), axis=0, tiled=True)
    count = gathered.shape[0] // TEAM
    return lax.dynamic_slice_in_dim(gathered, (lax.axis_index("dp") % TEAM) * count, count, 0)


def column_blocks(grad):
    n_dp, n_ctx = lax.axis_size("dp"), lax.axis_size("ctx")
    rows_all, width = grad.shape
    blocks = grad.astype(BF16).reshape(TEAM, n_ctx, rows_all // (n_dp * n_ctx), width)
    return jnp.transpose(blocks, (1, 0, 2, 3))


def columns_home(part):
    return lax.all_to_all(part.astype(BF16), "dp", 0, 0, tiled=True)


def columns_out(grad, index):
    hit = (jnp.arange(TEAM) == index)[None, :, None]
    spread = jnp.where(hit, grad.astype(BF16)[:, None, :], jnp.zeros((), BF16))
    out = lax.psum_scatter(spread, ("dp", "ctx"), scatter_dimension=0, tiled=True)
    return jnp.transpose(out, (1, 0, 2))


def rows_out(grad):
    grad = grad.astype(BF16)
    if lax.axis_size("dp") == TEAM:
        return lax.psum_scatter(grad, "ctx", scatter_dimension=0, tiled=True).astype(F32)
    member = lax.axis_index("dp") % TEAM
    hit = (jnp.arange(TEAM) == member)[:, None, None]
    spread = jnp.where(hit, grad[None], jnp.zeros((), BF16)).reshape(-1, grad.shape[1])
    return lax.psum_scatter(spread, ("dp", "ctx"), scatter_dimension=0, tiled=True).astype(F32)


def across(value):
    return lax.all_to_all(value, "ctx", 0, 0, tiled=True)


def ctx_gather(own):
    return across(jnp.broadcast_to(own, (lax.axis_size("ctx"), *own.shape)))


def flat(value):
    return value.reshape(-1, value.shape[-1])


def norm_back(e, xhat, r):
    return r * (e - xhat * jnp.mean(e * xhat, axis=-1, keepdims=True))


def local(
    tokens, cotangent, gain_attn, w_query, w_key, w_value, w_out, gain_ffn, w_gate, w_up, w_down, order
):
    _, span, width = tokens.shape
    n_ctx = lax.axis_size("ctx")
    rows = w_query.shape[0]
    length = span * n_ctx
    half_rows = span // 2
    scale = HEAD_DIM**-0.5

    gain_a = gain_attn.astype(F32)[:, None]
    gain_f = gain_ffn.astype(F32)[:, None]
    mates = TEAM // n_ctx
    here = lax.axis_index("dp") % TEAM
    mate = here % mates
    ids = jnp.arange(TEAM, dtype=jnp.int32)
    place_of = lambda head: head // mates * mates + (head % mates ^ mate)
    member, head_at = here ^ ids, place_of(ids)
    member_at = place_of(member)
    head = lax.axis_index("ctx") * mates + mate
    one_team = lax.axis_size("dp") == TEAM and mates == 2

    storage = jnp.arange(length, dtype=jnp.int32)
    turn = angles(place_rows(storage, order, half_rows))
    sine = jnp.sin(turn)
    tables = (jnp.concatenate([jnp.cos(turn)] * 2, axis=1), jnp.concatenate([-sine, sine], axis=1))
    turn_t = angles(storage).T
    turn_t = jnp.concatenate([jnp.cos(turn_t), jnp.sin(turn_t)], axis=0)
    slots = jnp.sum(jnp.where(order[None, :] == jnp.arange(order.shape[0])[:, None], jnp.arange(order.shape[0]), 0), axis=1)
    slots = slots.astype(jnp.int32)

    tok, dy_own = tokens[0], cotangent[0]
    x = tok.astype(F32)
    low_x1 = (x * lax.rsqrt(jnp.mean(x * x, axis=-1, keepdims=True) + EPS)).astype(BF16)
    folded_qkv = fold(head_at if one_team else ids, gain_a, (w_query, w_key, w_value))
    folded_gu = fold(ids, gain_f, (w_gate, w_up))
    if one_team:
        x1 = [lax.all_gather(first_of(tok, w_out), "ctx", axis=0)]
        blocks = folded_qkv.reshape(n_ctx, mates, rows, QKV)
        blocks = jnp.stack([blocks[:, 0], swap(blocks[:, 1], 1)], axis=1)
        piece = across(blocks)
        piece, folded_gu = tie(piece, folded_gu)
        mine_gu = lax.all_to_all(folded_gu, "dp", 0, 0, tiled=True)
        pieces = [piece, swap(piece, 2), swap(piece, 4), swap(piece, 6)]
        wqkv = rows_of(member, pieces)
        packed = lax.all_gather(pack(mine_gu, w_down), "ctx", axis=0)
    else:
        wqkv = by_rows(any_columns(folded_qkv, head))
        wgu = by_rows(any_columns(folded_gu, here)).reshape(TEAM, width // TEAM, -1)
        x1 = [lax.all_gather(low_x1, "ctx", axis=0)]
        wo, wd = any_rows(w_out), any_rows(w_down)
        packed = pack(wgu, wd)[None]

    dy_even = [dy_own, swap(dy_own, 2), swap(dy_own, 4)]
    x1[0], wqkv, tables, dy_even, turn_t = tie(x1[0], wqkv, tables, dy_even, turn_t)
    if one_team:
        wo = x1[0][:, span:].reshape(QW, width)
    qkv = [qkv_of(x1[0], span, wqkv, tables)]
    if mates == 2:
        theirs, qkv = tie(swap(x1[0], 1), qkv)
        x1.append(theirs)
        qkv.append(qkv_of(theirs, span, wqkv, tables))
    other, lse_other = attend(slots, order, qkv[-1], [])
    heads, lse = (other, lse_other) if mates == 1 else attend(slots, order, qkv[0], [swap(other, 1)])
    dy_even.append(swap(dy_even[0], 6))
    heads, wo = tie(heads, wo)
    wo_all = chip_mates([wo, swap(wo, 2), swap(wo, 4), swap(wo, 6)])
    dy_all = stack(ids, chip_mates(dy_even))
    traded = across(heads)
    traded, wo_all, dy_all = tie(traded, wo_all, dy_all)

    traded = traded.reshape(TEAM, *traded.shape[2:])
    middle, top, low = middle_of(member_at, tok, traded, wo_all)
    even_a = [top, swap(top, 2), swap(top, 4)]
    even_a.append(swap(top, 6))
    x2_a = chip_mates(even_a)
    x2_a, low = tie(x2_a, low)
    even_b = [low, swap(low, 2), swap(low, 4), swap(low, 6)]
    *parts_a, hidden, dgu, x2_all = feed(0, x2_a, dy_all, packed, None)
    even_b, parts_a, hidden, dgu, x2_all = tie(even_b, parts_a, hidden, dgu, x2_all)
    odds_a = [swap(parts_a[1], 1), swap(parts_a[3], 1)]
    x2_b = chip_mates(even_b)
    *parts_b, hidden, dgu, x2_all = feed(1, x2_b, dy_all, packed, (hidden, dgu, x2_all))
    dgu = flat(dgu)
    odds_b = [swap(parts_b[1], 1), swap(parts_b[3], 1)]
    g_gate = mm_tn(flat(x2_all), dgu[:, : dgu.shape[1] // 2]).astype(BF16)
    odds_a, odds_b, g_gate = tie(odds_a, odds_b, g_gate)
    got_b = mates_all(member, [parts_a[0], parts_a[2], *odds_a, parts_b[0], parts_b[2], *odds_b])
    got_b, x2_all, dy_all, hidden = tie(got_b, x2_all, dy_all, hidden)
    got_b = chip_sums(got_b)
    g_up = mm_tn(flat(x2_all), dgu[:, dgu.shape[1] // 2 :]).astype(BF16)
    g_down = mm_tn(flat(hidden), flat(dy_all)).astype(BF16)
    if one_team:
        g_ff = pack_back(g_gate, g_up, g_down)
        g_ff = lax.psum_scatter(g_ff.reshape(-1, g_ff.shape[-1]), "ctx", scatter_dimension=0, tiled=True)
    mixed_parts = parts_of(hidden, packed, width)
    got_b, mixed_parts = tie(got_b, mixed_parts)
    sums = (got_b,)
    d_low, d_heads = d_middle_of(member_at, sums, middle, dy_own, wo_all)

    hidden, d_low, d_heads = tie(hidden, d_low, d_heads)
    d_heads = across(d_heads.reshape(n_ctx, mates, *d_heads.shape[1:]))
    mixed_own, mixed_sums = mates_trade(mixed_parts)
    mixed_got = hop(mixed_sums)
    out_parts = grad_out_parts(member_at, traded, d_low)
    d_heads, mixed_got, out_parts = tie(d_heads, mixed_got, out_parts)

    d_other = d_heads if mates == 1 else swap(d_heads[:, 1:], 1)
    d_qkv, more = [attend_back(slots, qkv[-1], d_other, lse_other, turn_t)], []
    if mates == 2:
        more = [swap(input_all(d_qkv[0], wqkv), 1)]
        d_qkv = [attend_back(slots, qkv[0], d_heads, lse, turn_t), *d_qkv]
    d_qkv, more = tie(d_qkv, more)
    e1 = input_own(d_qkv[0], wqkv, more)
    e1, d_qkv, mixed_got, out_parts = tie(e1, d_qkv, mixed_got, out_parts)
    e1 = lax.psum_scatter(e1, "ctx", scatter_dimension=0)

    g_qkv = mm_tn(flat(x1[0][:, :span]), flat(d_qkv[0]))
    for a, b in zip(x1[1:], d_qkv[1:]):
        g_qkv = g_qkv + mm_tn(flat(a[:, :span]), flat(b))
    if one_team:
        ff = g_ff.shape[1]
        cut = TEAM * rows
        ways, g_ff, out_parts = tie(pieces_of(member, g_qkv), g_ff, out_parts)
        g_gu = jnp.concatenate([g_ff[:cut].reshape(TEAM, rows, ff), g_ff[cut : 2 * cut].reshape(TEAM, rows, ff)], axis=2)
        g_gu = lax.all_to_all(g_gu, "dp", 0, 0, tiled=True)
        out_own, out_sums = mates_trade(out_parts)
        ways, out_sums = tie([ways[0], *hop(ways[1:])], out_sums)
        home = ways[0].astype(F32)
        for way in ways[1:]:
            home = home + way.astype(F32)
        home = home.astype(BF16).reshape(mates, n_ctx, rows, QKV)
        home, g_gu = tie(jnp.stack([home[0], swap(home[1], 1)], axis=1), g_gu)
        home = across(home).reshape(TEAM, rows, QKV)
        g_gu, mixed_got = tie(g_gu, mixed_got)
        g_out = total_of(out_own, hop(out_sums)).astype(BF16)
        out_ring = ring_trade(g_out.reshape(n_ctx, -1, width))
        down = g_ff[2 * cut :].reshape(width // ff, -1, ff)
        grad_down = jnp.concatenate([down[i] for i in range(width // ff)], axis=1).astype(F32)
    else:
        home = columns_out(g_qkv, head)
        g_gu = columns_out(jnp.concatenate([g_gate, g_up], axis=1), here)
        out_own, out_sums = mates_trade(out_parts)
        grad_down, grad_out = rows_out(g_down), rows_out(total_of(out_own, hop(out_sums)))
    mixed = (middle + total_of(mixed_own, mixed_got)).astype(BF16)[None]
    token_grad = token_gradient(e1, tok, d_low)
    *grads_gu, gain_f_grad = gradients(ids, gain_f, g_gu, (w_gate, w_up))
    if one_team:
        home, token_grad, mixed, gain_f_grad = tie(home, token_grad, mixed, gain_f_grad)
    *grads_qkv, gain_a_grad = gradients(head_at if one_team else ids, gain_a, home, (w_query, w_key, w_value))
    if one_team:
        out_ring, gain_a_grad = tie(out_ring, gain_a_grad)
        grad_out = sum(t.astype(F32) for t in out_ring[1:]) + out_ring[0].astype(F32)
    return (
        mixed,
        token_grad[None],
        gain_a_grad[0],
        *grads_qkv,
        grad_out,
        gain_f_grad[0],
        *grads_gu,
        grad_down,
    )


def solution(mesh):
    act = P("dp", "ctx", None)
    vec = P(("dp", "ctx"))
    mat = P(("dp", "ctx"), None)
    return jax.shard_map(
        local,
        mesh=mesh,
        in_specs=(act, act, vec, mat, mat, mat, mat, vec, mat, mat, mat, P()),
        out_specs=(act, act, vec, mat, mat, mat, mat, vec, mat, mat, mat),
        check_vma=False,
    )
```
